32 devices in a mesh: dp: 4 (over y, core), expert: 8 (over z, x).
Axes of the slice: x: 2, y: 2, z: 4, core: 2. Of those that a mesh axis runs over, the one named last changes fastest.
Arguments:
- tokens: bfloat16 [4096, 2048], P(('dp', 'expert')), may hold values from -6 to 6
- routes: int32 [4096, 4], P(('dp', 'expert')), may hold values from 0 to 7, all different within a row; in each aligned block of 128 rows (0 to 127, 128 to 255, ...) at most 96 rows name the same one
- combine: float32 [4096, 4], P(('dp', 'expert')), may hold values from 0.2 to 1
- cotangent: bfloat16 [4096, 2048], P(('dp', 'expert')), may hold values from -1.5 to 1.5
- w_gate: bfloat16 [8, 2048, 768], P('expert'), may hold values from -0.125 to 0.125
- w_up: bfloat16 [8, 2048, 768], P('expert'), may hold values from -0.125 to 0.125
- w_down: bfloat16 [8, 768, 2048], P('expert'), may hold values from -0.21875 to 0.21875
Outputs:
- output: bfloat16 [4096, 2048], P(('dp', 'expert'))
- d_tokens: bfloat16 [4096, 2048], P(('dp', 'expert'))
- d_combine: float32 [4096, 4], P(('dp', 'expert'))
- d_w_gate: bfloat16 [8, 2048, 768], P('expert', 'dp')
- d_w_up: bfloat16 [8, 2048, 768], P('expert', 'dp')
- d_w_down: bfloat16 [8, 768, 2048], P('expert', None, 'dp')
The draws below stay inside these ranges and needn't reach their ends.
Inputs may be any that keep to these rules, and one draw needn't show every extreme that they name: `routes`: each row names 4 different experts. In the rows of one device (aligned blocks of 128 rows) no expert is named by more than 96 rows, a bound that some block reaches.
All inputs are finite; a program needn't handle non-finite values.
Results may differ from the reference program's by a relative error of at most 0.014.
Values may be sent and summed in bfloat16 or wider, within the bound.
No kernel may reach another device: no remote copies, remote signals or barrier semaphores. Data moves between devices by JAX's collectives and lax.ppermute only.
A program may use at most 128 MiB of HBM per device.

```python
import math
import jax
import jax.numpy as jnp
import numpy as np
from jax import lax

D = 2048
FF = 768
TOP = 4
TOK_DEV = 128
EXPERTS = 8
CAP = 96
TOKENS = 4096
N_DP = 4
N_EXPERT = 8


def level_of(own_key, extent, shards, least, top_value):
    def one(dim, blocks):
        draws = jax.random.uniform(jax.random.fold_in(jax.random.fold_in(own_key, 6), dim), (blocks,), jnp.float32, least / len(shards), top_value / len(shards))
        return jnp.repeat(jnp.exp(draws), extent[dim] // blocks).reshape((-1,) + (1,) * (len(extent) - dim - 1))

    loudness = one(*shards[0])
    for cut in shards[1:]:
        loudness = loudness * one(*cut)
    return loudness


def routed_block(key, own, number, rows, count, top, bound, slope):
    order = jax.random.permutation(key, count)
    heavy_load, ordinary = portions_of(count, rows * top, bound, slope, True), portions_of(count, rows * top, bound, slope, False)
    places = jnp.arange(count)

    def named(lengths, rotation):
        used = int((lengths > 0).sum())
        fixed = max(1, used // 4)
        moved = fixed + (places - fixed + rotation * (used - fixed)) % max(1, count - fixed)
        return jnp.zeros((count,), jnp.int32).at[order[jnp.where(places < fixed, places, moved)]].set(jnp.asarray(lengths, jnp.int32))

    lengths = jnp.where(number % 4 == 0, named(heavy_load, number // 4), named(ordinary, number - number // 4 - 1))
    mixed = jax.random.permutation(jax.random.fold_in(own, 3), count)
    donor, receiver = mixed[0:count // 2 * 2:2], mixed[1:count // 2 * 2:2]
    margin = jnp.minimum(lengths[donor] - 1, bound - lengths[receiver]) // 2
    margin = jnp.where((donor == order[0]) | (receiver == order[0]) | (lengths[receiver] == 0), 0, jnp.maximum(margin, 0))
    moved = jax.random.randint(jax.random.fold_in(own, 4), (count // 2,), 0, 1 << 20) % (margin + 1)
    lengths = lengths.at[donor].add(-moved).at[receiver].add(moved)
    members = jnp.searchsorted(jnp.cumsum(lengths), jnp.arange(rows * top), side="right").astype(jnp.int32)
    table = members.reshape(top, rows).T
    table = table[jax.random.permutation(jax.random.fold_in(own, 1), rows)]
    rotation = jax.random.randint(jax.random.fold_in(own, 2), (rows, 1), 0, top)
    return jnp.take_along_axis(table, (jnp.arange(top)[None, :] + rotation) % top, axis=1)


def portions_of(number_of, total, bound, slope, full):
    weights = [(1 << 20) // math.isqrt(standing ** slope) + 1 for standing in range(1, number_of + 1)]
    largest = bound if full else min(bound, max(-(-total // number_of), total * weights[0] // sum(weights)))
    least = 1 if total - largest >= number_of - 1 else 0
    given, surplus = [largest] + [least] * (number_of - 1), total - largest - least * (number_of - 1)
    while surplus > 0:
        candidates = [i for i in range(1, number_of) if given[i] < largest] or [i for i in range(1, number_of) if given[i] < bound]
        pool, left = sum([weights[i] for i in candidates]), surplus
        for i in candidates:
            extra = min(bound - given[i], max(1, left * weights[i] // pool), surplus)
            given[i] = given[i] + extra
            surplus = surplus - extra
    return np.array(given)


def normal_values(rng, extent, deviation, most, shards=(), held_as=jnp.bfloat16):
    drawn = jax.random.normal(rng, extent, jnp.float32) * deviation
    if len(shards) > 0:
        drawn = level_of(rng, extent, shards, -0.22, 0.18) * drawn
    return jnp.clip(drawn, min=-most, max=most).astype(held_as)


def setup_inputs(seed: int = 0) -> dict:
    arg_keys = jax.random.split(jax.random.key(seed), 8)
    tokens = normal_values(arg_keys[0], (TOKENS, D), 1.0, 6.0, ((0, 32),))
    routes_keys = jax.random.split(jax.random.fold_in(arg_keys[1], 1), TOKENS // TOK_DEV)
    routes_turns = jax.random.permutation(jax.random.fold_in(arg_keys[1], 3), TOKENS // TOK_DEV)
    routes = jax.vmap(lambda own, number: routed_block(jax.random.fold_in(arg_keys[1], 2), own, number, TOK_DEV, EXPERTS, TOP, CAP, 2))(routes_keys, routes_turns).reshape((TOKENS, TOP))
    combine = jnp.clip(0.2 + 0.8 * jax.random.uniform(arg_keys[2], (TOKENS, TOP), jnp.float32) ** level_of(arg_keys[2], (TOKENS, TOP), ((0, 32),), -0.2, 0.2), 0.2, 1.0)
    cotangent = normal_values(arg_keys[3], (TOKENS, D), 0.25, 1.5, ((0, 32),))
    w_gate = normal_values(arg_keys[4], (EXPERTS, D, FF), D ** -0.5, 0.125, ((0, 8),))
    w_up = normal_values(arg_keys[5], (EXPERTS, D, FF), D ** -0.5, 0.125, ((0, 8),))
    w_down = normal_values(arg_keys[6], (EXPERTS, FF, D), FF ** -0.5, 0.21875, ((0, 8),))
    return {"tokens": tokens, "routes": routes, "combine": combine, "cotangent": cotangent, "w_gate": w_gate, "w_up": w_up, "w_down": w_down}


def slot_table(routes_dev, experts):
    flat_ids = routes_dev.reshape(-1)
    onehot = (flat_ids[:, None] == jnp.arange(experts, dtype=jnp.int32)[None, :]).astype(jnp.int32)
    before = jnp.cumsum(onehot, axis=0) - onehot
    return jnp.sum(before * onehot, axis=1).astype(jnp.int32)


def expert_step(pieces):
    rows_in, d_in, gate_w, up_w, down_w = pieces
    gate_pre = jnp.dot(rows_in, gate_w, preferred_element_type=jnp.float32)
    up_pre = jnp.dot(rows_in, up_w, preferred_element_type=jnp.float32)
    activated = jax.nn.silu(gate_pre)
    hidden = (activated * up_pre).astype(jnp.bfloat16)
    produced = jnp.dot(hidden, down_w, preferred_element_type=jnp.float32).astype(jnp.bfloat16)
    d_hidden = jnp.dot(d_in, down_w.T, preferred_element_type=jnp.float32)
    sigmoid_g = jax.nn.sigmoid(gate_pre)
    d_gate = (d_hidden * up_pre * sigmoid_g * (1.0 + gate_pre * (1.0 - sigmoid_g))).astype(jnp.bfloat16)
    d_up = (d_hidden * activated).astype(jnp.bfloat16)
    part_gate = jnp.dot(rows_in.T, d_gate, preferred_element_type=jnp.float32).astype(jnp.bfloat16)
    part_up = jnp.dot(rows_in.T, d_up, preferred_element_type=jnp.float32).astype(jnp.bfloat16)
    part_down = jnp.dot(hidden.T, d_in, preferred_element_type=jnp.float32).astype(jnp.bfloat16)
    d_rows = (jnp.dot(d_gate, gate_w.T, preferred_element_type=jnp.float32)
              + jnp.dot(d_up, up_w.T, preferred_element_type=jnp.float32)).astype(jnp.bfloat16)
    return produced, d_rows, part_gate, part_up, part_down


def reference(tokens, routes, combine, cotangent, w_gate, w_up, w_down):
    group_rows = TOK_DEV * N_EXPERT
    outputs = []
    d_tokens_all = []
    d_combine_all = []
    sum_gate = jnp.zeros((EXPERTS, D, FF), jnp.float32)
    sum_up = jnp.zeros((EXPERTS, D, FF), jnp.float32)
    sum_down = jnp.zeros((EXPERTS, FF, D), jnp.float32)
    for group in range(N_DP):
        tokens_g = tokens[group * group_rows:(group + 1) * group_rows]
        routes_g = routes[group * group_rows:(group + 1) * group_rows].reshape(N_EXPERT, TOK_DEV, TOP)
        combine_g = combine[group * group_rows:(group + 1) * group_rows]
        cot_g = cotangent[group * group_rows:(group + 1) * group_rows]
        slots = jax.vmap(slot_table, (0, None))(routes_g, EXPERTS)
        flat_ids = routes_g.reshape(N_EXPERT, TOK_DEV * TOP)
        source_dev = jnp.arange(N_EXPERT, dtype=jnp.int32)[:, None]
        target = (flat_ids * (N_EXPERT * CAP) + source_dev * CAP + slots).reshape(-1).astype(jnp.int32)
        pair_row = (source_dev * TOK_DEV + jnp.arange(TOK_DEV * TOP, dtype=jnp.int32)[None, :] // TOP).reshape(-1).astype(jnp.int32)
        rows_in = jnp.zeros((EXPERTS * N_EXPERT * CAP, D), jnp.bfloat16).at[target].set(tokens_g[pair_row])
        rows_in = rows_in.reshape(EXPERTS, N_EXPERT * CAP, D)
        scaled = (combine_g.reshape(-1)[:, None] * cot_g[pair_row].astype(jnp.float32)).astype(jnp.bfloat16)
        d_in = jnp.zeros((EXPERTS * N_EXPERT * CAP, D), jnp.bfloat16).at[target].set(scaled)
        d_in = d_in.reshape(EXPERTS, N_EXPERT * CAP, D)
        produced, d_rows, part_gate, part_up, part_down = lax.map(expert_step, (rows_in, d_in, w_gate, w_up, w_down))
        out_pair = produced.reshape(-1, D)[target].reshape(group_rows, TOP, D).astype(jnp.float32)
        outputs.append(jnp.sum(combine_g[:, :, None] * out_pair, axis=1).astype(jnp.bfloat16))
        d_combine_all.append(jnp.sum(out_pair * cot_g.astype(jnp.float32)[:, None, :], axis=2))
        back_pair = d_rows.reshape(-1, D)[target].reshape(group_rows, TOP, D).astype(jnp.float32)
        d_tokens_all.append(jnp.sum(back_pair, axis=1).astype(jnp.bfloat16))
        sum_gate = sum_gate + part_gate.astype(jnp.float32)
        sum_up = sum_up + part_up.astype(jnp.float32)
        sum_down = sum_down + part_down.astype(jnp.float32)
    return (jnp.concatenate(outputs, axis=0), jnp.concatenate(d_tokens_all, axis=0),
            jnp.concatenate(d_combine_all, axis=0), sum_gate.astype(jnp.bfloat16),
            sum_up.astype(jnp.bfloat16), sum_down.astype(jnp.bfloat16))
```

```python
import jax
import jax.numpy as jnp
from jax import lax
from jax.sharding import PartitionSpec as P


def per_device(tokens, routes, combine, cotangent, w_gate, w_up, w_down):
    tok_rows, features = tokens.shape
    groups = lax.axis_size("expert")
    experts = w_gate.shape[0] * groups
    mine = lax.axis_index("expert")
    bf16 = jnp.bfloat16
    f32 = jnp.float32
    chosen = routes[:, :, None] == jnp.arange(experts, dtype=jnp.int32)[None, None, :]
    weights = jnp.sum(jnp.where(chosen, combine[:, :, None], 0.0), axis=1)
    all_weights = lax.all_gather(weights, "expert", axis=0, tiled=True)
    weight = lax.dynamic_slice_in_dim(all_weights, mine, 1, axis=1)
    all_tokens = lax.all_gather(tokens, "expert", axis=0, tiled=True)
    all_cot = lax.all_gather(cotangent, "expert", axis=0, tiled=True)
    wg, wu, wd = w_gate[0], w_up[0], w_down[0]
    gate_pre = jnp.dot(all_tokens, wg, preferred_element_type=f32)
    up_pre = jnp.dot(all_tokens, wu, preferred_element_type=f32)
    sig = jax.nn.sigmoid(gate_pre)
    act = gate_pre * sig
    hidden = act * up_pre
    scaled = (hidden * weight).astype(bf16)
    out_part = jnp.dot(scaled, wd, preferred_element_type=f32).astype(bf16)
    output = lax.psum_scatter(out_part, "expert", scatter_dimension=0, tiled=True)
    d_raw = jnp.einsum("td,fd->tf", all_cot, wd, preferred_element_type=f32)
    d_comb = jnp.sum(hidden * d_raw, axis=1)
    d_hidden = d_raw * weight
    d_gate = (d_hidden * up_pre * sig * (1.0 + gate_pre * (1.0 - sig))).astype(bf16)
    d_up = (d_hidden * act).astype(bf16)
    d_rows = (
        jnp.einsum("tf,df->td", d_gate, wg, preferred_element_type=f32)
        + jnp.einsum("tf,df->td", d_up, wu, preferred_element_type=f32)
    ).astype(bf16)
    d_tokens = lax.psum_scatter(d_rows, "expert", scatter_dimension=0, tiled=True)
    part_down = jnp.einsum("tf,td->fd", scaled, all_cot, preferred_element_type=f32).astype(bf16)
    part_gate = jnp.einsum("td,tf->df", all_tokens, d_gate, preferred_element_type=f32).astype(bf16)
    part_up = jnp.einsum("td,tf->df", all_tokens, d_up, preferred_element_type=f32).astype(bf16)
    d_w_down = lax.psum_scatter(part_down, "dp", scatter_dimension=1, tiled=True)[None]
    d_w_gate = lax.psum_scatter(part_gate, "dp", scatter_dimension=0, tiled=True)[None]
    d_w_up = lax.psum_scatter(part_up, "dp", scatter_dimension=0, tiled=True)[None]
    back = lax.all_to_all(
        d_comb.reshape(groups, tok_rows), "expert", split_axis=0, concat_axis=0, tiled=True
    )
    d_combine = jnp.sum(jnp.where(chosen, back.T[:, None, :], 0.0), axis=2)
    return output, d_tokens, d_combine, d_w_gate, d_w_up, d_w_down


def solution(mesh):
    rows = P(("dp", "expert"), None)
    return jax.shard_map(
        per_device,
        mesh=mesh,
        in_specs=(rows, rows, rows, rows) + (P("expert", None, None),) * 3,
        out_specs=(
            rows,
            rows,
            rows,
            P("expert", "dp", None),
            P("expert", "dp", None),
            P("expert", None, "dp"),
        ),
        check_vma=False,
    )
```

```python
import jax
import jax.numpy as jnp
from jax import lax
from jax.sharding import PartitionSpec as P


def slot_map(routes, experts, capacity):
    flat_ids = routes.reshape(-1)
    onehot = (flat_ids[:, None] == jnp.arange(experts, dtype=jnp.int32)[None, :]).astype(jnp.int32)
    before = jnp.cumsum(onehot, axis=0) - onehot
    slots = jnp.sum(before * onehot, axis=1)
    target = flat_ids * capacity + slots
    source = (
        jnp.full((experts * capacity,), -1, jnp.int32)
        .at[target]
        .set(jnp.arange(flat_ids.shape[0], dtype=jnp.int32))
    )
    return (target, source)


def routed_plan(tokens, routes, combine, cotangent, w_gate, w_up, w_down):
    tok_rows, features = tokens.shape
    per_token = routes.shape[1]
    groups = lax.axis_size("expert")
    local_exp = w_gate.shape[0]
    experts = local_exp * groups
    capacity = 3 * tok_rows * per_token // (2 * experts)
    target, source = slot_map(routes, experts, capacity)
    filled = (source >= 0)[:, None]
    pair_index = jnp.maximum(source, 0)
    owner_row = pair_index // per_token
    outgoing = jnp.where(filled, tokens[owner_row], jnp.zeros((), jnp.bfloat16))
    outgoing = outgoing.reshape(groups, local_exp, capacity, features)
    cot_float = cotangent.astype(jnp.float32)
    scaled = (combine[:, :, None] * cot_float[:, None, :]).reshape(tok_rows * per_token, features)
    outgoing_grad = jnp.where(filled, scaled[pair_index], 0.0).astype(jnp.bfloat16)
    outgoing_grad = outgoing_grad.reshape(groups, local_exp, capacity, features)
    arrived = lax.all_to_all(outgoing, "expert", split_axis=0, concat_axis=0, tiled=True)
    gate_pre = jnp.einsum("secd,edf->secf", arrived, w_gate, preferred_element_type=jnp.float32)
    up_pre = jnp.einsum("secd,edf->secf", arrived, w_up, preferred_element_type=jnp.float32)
    activated = jax.nn.silu(gate_pre)
    hidden = (activated * up_pre).astype(jnp.bfloat16)
    produced = jnp.einsum(
        "secf,efd->secd", hidden, w_down, preferred_element_type=jnp.float32
    ).astype(jnp.bfloat16)
    returned = lax.all_to_all(produced, "expert", split_axis=0, concat_axis=0, tiled=True)
    d_in = lax.all_to_all(outgoing_grad, "expert", split_axis=0, concat_axis=0, tiled=True)
    d_hidden = jnp.einsum("secd,efd->secf", d_in, w_down, preferred_element_type=jnp.float32)
    part_down = jnp.einsum("secf,secd->efd", hidden, d_in, preferred_element_type=jnp.float32)
    sigmoid_g = jax.nn.sigmoid(gate_pre)
    d_gate = (d_hidden * up_pre * sigmoid_g * (1.0 + gate_pre * (1.0 - sigmoid_g))).astype(
        jnp.bfloat16
    )
    d_up = (d_hidden * activated).astype(jnp.bfloat16)
    part_gate = jnp.einsum("secd,secf->edf", arrived, d_gate, preferred_element_type=jnp.float32)
    part_up = jnp.einsum("secd,secf->edf", arrived, d_up, preferred_element_type=jnp.float32)
    d_rows = (
        jnp.einsum("secf,edf->secd", d_gate, w_gate, preferred_element_type=jnp.float32)
        + jnp.einsum("secf,edf->secd", d_up, w_up, preferred_element_type=jnp.float32)
    ).astype(jnp.bfloat16)
    back = lax.all_to_all(d_rows, "expert", split_axis=0, concat_axis=0, tiled=True)
    per_slot = returned.reshape(experts * capacity, features)[target]
    per_slot = per_slot.reshape(tok_rows, per_token, features).astype(jnp.float32)
    output = jnp.sum(combine[:, :, None] * per_slot, axis=1).astype(jnp.bfloat16)
    d_combine = jnp.sum(per_slot * cot_float[:, None, :], axis=2)
    back_slot = back.reshape(experts * capacity, features)[target]
    back_slot = back_slot.reshape(tok_rows, per_token, features).astype(jnp.float32)
    d_tokens = jnp.sum(back_slot, axis=1).astype(jnp.bfloat16)
    sum_gate, sum_up, sum_down = (
        lax.psum_scatter(
            part_gate.astype(jnp.bfloat16), "dp", scatter_dimension=1, tiled=True
        ).astype(jnp.float32),
        lax.psum_scatter(
            part_up.astype(jnp.bfloat16), "dp", scatter_dimension=1, tiled=True
        ).astype(jnp.float32),
        lax.psum_scatter(
            part_down.astype(jnp.bfloat16), "dp", scatter_dimension=2, tiled=True
        ).astype(jnp.float32),
    )
    d_w_down = sum_down.astype(jnp.bfloat16)
    return (
        output,
        d_tokens,
        d_combine,
        sum_gate.astype(jnp.bfloat16),
        sum_up.astype(jnp.bfloat16),
        d_w_down,
    )


RING = (0, 1, 3, 5, 7, 6, 4, 2)


def ring_perms():
    n = len(RING)
    fwd = [(RING[i], RING[(i + 1) % n]) for i in range(n)]
    bwd = [(RING[(i + 1) % n], RING[i]) for i in range(n)]
    return fwd, bwd


def ring_sources():
    n = len(RING)
    place = {e: i for i, e in enumerate(RING)}
    steps = (0, -1, 1, -2, 2, -3, 3, 4)
    return [[RING[(place[e] + r) % n] for r in steps] for e in range(n)]


def forward(value):
    return lax.ppermute(value, "expert", ring_perms()[0])


def backward(value):
    return lax.ppermute(value, "expert", ring_perms()[1])


def ring_gather(block):
    half = block.shape[0] // 2
    f1, b1 = forward(block), backward(block)
    f2, b2 = forward(f1), backward(b1)
    f3, b3 = forward(f2), backward(b2)
    f4, b4 = forward(f3[:half]), backward(b3[half:])
    return [block, f1, b1, f2, b2, f3, b3, jnp.concatenate([f4, b4], axis=0)]


def add_rounded(a, b):
    return (a.astype(jnp.float32) + b.astype(jnp.float32)).astype(jnp.bfloat16)


def ring_scatter(parts):
    own, m1, p1, m2, p2, m3, p3, far = parts
    half = own.shape[0] // 2
    f = forward(far[:half])
    b = backward(far[half:])
    f = forward(jnp.concatenate([add_rounded(p3[:half], f), p3[half:]], axis=0))
    b = backward(jnp.concatenate([m3[:half], add_rounded(m3[half:], b)], axis=0))
    f = forward(add_rounded(p2, f))
    b = backward(add_rounded(m2, b))
    f = forward(add_rounded(p1, f))
    b = backward(add_rounded(m1, b))
    total = own.astype(jnp.float32) + f.astype(jnp.float32) + b.astype(jnp.float32)
    return total.astype(jnp.bfloat16)


def dp_scatter(quarters):
    n = lax.axis_size("dp")
    y, c = lax.axis_index("dp") // 2, lax.axis_index("dp") % 2
    paired = quarters.reshape((n // 2, 2) + quarters.shape[1:])
    away = lax.dynamic_index_in_dim(paired, 1 - c, 1, keepdims=False)
    kept = lax.dynamic_index_in_dim(paired, c, 1, keepdims=False)
    got = lax.ppermute(away, "dp", [(j, j ^ 1) for j in range(n)])
    summed = kept.astype(jnp.float32) + got.astype(jnp.float32)
    other = lax.dynamic_index_in_dim(summed.astype(jnp.bfloat16), 1 - y, 0, keepdims=False)
    last = lax.ppermute(other, "dp", [(j, j ^ 2) for j in range(n)])
    mine = lax.dynamic_index_in_dim(summed, y, 0, keepdims=False)
    return (mine + last.astype(jnp.float32)).astype(jnp.bfloat16)[None]


def gathered_plan(tokens, routes, combine, cotangent, w_gate, w_up, w_down):
    tok_rows, features = tokens.shape
    groups = lax.axis_size("expert")
    me = lax.axis_index("expert")
    bf16 = jnp.bfloat16
    f32 = jnp.float32
    chosen = routes[:, :, None] == jnp.arange(groups, dtype=jnp.int32)[None, None, :]
    weights = jnp.sum(jnp.where(chosen, combine[:, :, None], 0.0), axis=1)
    sources = jnp.asarray(ring_sources(), jnp.int32)[me]
    arrived = lax.all_to_all(weights.T, "expert", split_axis=0, concat_axis=0, tiled=True)
    weight = arrived[sources].reshape(-1, 1)
    wg, wu, wd = w_gate[0], w_up[0], w_down[0]
    ff = wg.shape[1]
    all_tokens = jnp.concatenate(ring_gather(tokens), axis=0)
    all_cot = jnp.concatenate(ring_gather(cotangent), axis=0)
    gate_pre = jnp.dot(all_tokens, wg, preferred_element_type=f32)
    up_pre = jnp.dot(all_tokens, wu, preferred_element_type=f32)
    sig = jax.nn.sigmoid(gate_pre)
    act = gate_pre * sig
    hidden = act * up_pre
    scaled = (hidden * weight).astype(bf16)
    out_part = jnp.dot(scaled, wd, preferred_element_type=f32).astype(bf16)
    output = ring_scatter(jnp.split(out_part, groups, axis=0))
    d_raw = jnp.einsum("td,fd->tf", all_cot, wd, preferred_element_type=f32)
    d_comb = jnp.sum(hidden * d_raw, axis=1)
    d_hidden = d_raw * weight
    d_gate = (d_hidden * up_pre * sig * (1.0 + gate_pre * (1.0 - sig))).astype(bf16)
    d_up = (d_hidden * act).astype(bf16)
    d_rows = (
        jnp.einsum("tf,df->td", d_gate, wg, preferred_element_type=f32)
        + jnp.einsum("tf,df->td", d_up, wu, preferred_element_type=f32)
    ).astype(bf16)
    d_tokens = ring_scatter(jnp.split(d_rows, groups, axis=0))
    n_dp = lax.axis_size("dp")
    part_down = jnp.einsum("tf,td->fd", scaled, all_cot, preferred_element_type=f32).astype(bf16)
    part_gate = jnp.einsum("td,tf->df", all_tokens, d_gate, preferred_element_type=f32).astype(bf16)
    part_up = jnp.einsum("td,tf->df", all_tokens, d_up, preferred_element_type=f32).astype(bf16)
    d_w_down = dp_scatter(
        jnp.transpose(part_down.reshape(ff, n_dp, features // n_dp), (1, 0, 2))
    )
    d_w_gate = dp_scatter(part_gate.reshape(n_dp, features // n_dp, ff))
    d_w_up = dp_scatter(part_up.reshape(n_dp, features // n_dp, ff))
    by_source = jnp.zeros((groups, tok_rows), f32).at[sources].set(
        d_comb.reshape(groups, tok_rows), unique_indices=True
    )
    back = lax.all_to_all(by_source, "expert", split_axis=0, concat_axis=0, tiled=True)
    d_combine = jnp.sum(jnp.where(chosen, back.T[:, None, :], 0.0), axis=2)
    return output, d_tokens, d_combine, d_w_gate, d_w_up, d_w_down


def solution(mesh):
    rows = P(("dp", "expert"), None)
    small = mesh.shape["expert"] == len(RING) and mesh.shape["dp"] == 4
    return jax.shard_map(
        gathered_plan if small else routed_plan,
        mesh=mesh,
        in_specs=(rows, rows, rows, rows) + (P("expert", None, None),) * 3,
        out_specs=(
            rows,
            rows,
            rows,
            P("expert", "dp", None),
            P("expert", "dp", None),
            P("expert", None, "dp"),
        ),
        check_vma=False,
    )
```

```python
import jax
import jax.numpy as jnp
from jax import lax
from jax.sharding import PartitionSpec as P


def slot_map(routes, experts, capacity):
    flat_ids = routes.reshape(-1)
    onehot = (flat_ids[:, None] == jnp.arange(experts, dtype=jnp.int32)[None, :]).astype(jnp.int32)
    before = jnp.cumsum(onehot, axis=0) - onehot
    slots = jnp.sum(before * onehot, axis=1)
    target = flat_ids * capacity + slots
    source = (
        jnp.full((experts * capacity,), -1, jnp.int32)
        .at[target]
        .set(jnp.arange(flat_ids.shape[0], dtype=jnp.int32))
    )
    return (target, source)


def routed_plan(tokens, routes, combine, cotangent, w_gate, w_up, w_down):
    tok_rows, features = tokens.shape
    per_token = routes.shape[1]
    groups = lax.axis_size("expert")
    local_exp = w_gate.shape[0]
    experts = local_exp * groups
    capacity = 3 * tok_rows * per_token // (2 * experts)
    target, source = slot_map(routes, experts, capacity)
    filled = (source >= 0)[:, None]
    pair_index = jnp.maximum(source, 0)
    owner_row = pair_index // per_token
    outgoing = jnp.where(filled, tokens[owner_row], jnp.zeros((), jnp.bfloat16))
    outgoing = outgoing.reshape(groups, local_exp, capacity, features)
    cot_float = cotangent.astype(jnp.float32)
    scaled = (combine[:, :, None] * cot_float[:, None, :]).reshape(tok_rows * per_token, features)
    outgoing_grad = jnp.where(filled, scaled[pair_index], 0.0).astype(jnp.bfloat16)
    outgoing_grad = outgoing_grad.reshape(groups, local_exp, capacity, features)
    arrived = lax.all_to_all(outgoing, "expert", split_axis=0, concat_axis=0, tiled=True)
    gate_pre = jnp.einsum("secd,edf->secf", arrived, w_gate, preferred_element_type=jnp.float32)
    up_pre = jnp.einsum("secd,edf->secf", arrived, w_up, preferred_element_type=jnp.float32)
    activated = jax.nn.silu(gate_pre)
    hidden = (activated * up_pre).astype(jnp.bfloat16)
    produced = jnp.einsum(
        "secf,efd->secd", hidden, w_down, preferred_element_type=jnp.float32
    ).astype(jnp.bfloat16)
    returned = lax.all_to_all(produced, "expert", split_axis=0, concat_axis=0, tiled=True)
    d_in = lax.all_to_all(outgoing_grad, "expert", split_axis=0, concat_axis=0, tiled=True)
    d_hidden = jnp.einsum("secd,efd->secf", d_in, w_down, preferred_element_type=jnp.float32)
    part_down = jnp.einsum("secf,secd->efd", hidden, d_in, preferred_element_type=jnp.float32)
    sigmoid_g = jax.nn.sigmoid(gate_pre)
    d_gate = (d_hidden * up_pre * sigmoid_g * (1.0 + gate_pre * (1.0 - sigmoid_g))).astype(
        jnp.bfloat16
    )
    d_up = (d_hidden * activated).astype(jnp.bfloat16)
    part_gate = jnp.einsum("secd,secf->edf", arrived, d_gate, preferred_element_type=jnp.float32)
    part_up = jnp.einsum("secd,secf->edf", arrived, d_up, preferred_element_type=jnp.float32)
    d_rows = (
        jnp.einsum("secf,edf->secd", d_gate, w_gate, preferred_element_type=jnp.float32)
        + jnp.einsum("secf,edf->secd", d_up, w_up, preferred_element_type=jnp.float32)
    ).astype(jnp.bfloat16)
    back = lax.all_to_all(d_rows, "expert", split_axis=0, concat_axis=0, tiled=True)
    per_slot = returned.reshape(experts * capacity, features)[target]
    per_slot = per_slot.reshape(tok_rows, per_token, features).astype(jnp.float32)
    output = jnp.sum(combine[:, :, None] * per_slot, axis=1).astype(jnp.bfloat16)
    d_combine = jnp.sum(per_slot * cot_float[:, None, :], axis=2)
    back_slot = back.reshape(experts * capacity, features)[target]
    back_slot = back_slot.reshape(tok_rows, per_token, features).astype(jnp.float32)
    d_tokens = jnp.sum(back_slot, axis=1).astype(jnp.bfloat16)
    sum_gate, sum_up, sum_down = (
        lax.psum_scatter(
            part_gate.astype(jnp.bfloat16), "dp", scatter_dimension=1, tiled=True
        ).astype(jnp.float32),
        lax.psum_scatter(
            part_up.astype(jnp.bfloat16), "dp", scatter_dimension=1, tiled=True
        ).astype(jnp.float32),
        lax.psum_scatter(
            part_down.astype(jnp.bfloat16), "dp", scatter_dimension=2, tiled=True
        ).astype(jnp.float32),
    )
    d_w_down = sum_down.astype(jnp.bfloat16)
    return (
        output,
        d_tokens,
        d_combine,
        sum_gate.astype(jnp.bfloat16),
        sum_up.astype(jnp.bfloat16),
        d_w_down,
    )


RING = (0, 1, 3, 5, 7, 6, 4, 2)


def ring_perms():
    n = len(RING)
    fwd = [(RING[i], RING[(i + 1) % n]) for i in range(n)]
    bwd = [(RING[(i + 1) % n], RING[i]) for i in range(n)]
    return fwd, bwd


def ring_sources():
    n = len(RING)
    place = {e: i for i, e in enumerate(RING)}
    steps = (0, -1, 1, -2, 2, -3, 3, 4)
    return [[RING[(place[e] + r) % n] for r in steps] for e in range(n)]


def forward(value):
    return lax.ppermute(value, "expert", ring_perms()[0])


def backward(value):
    return lax.ppermute(value, "expert", ring_perms()[1])


def tie(*values):
    return lax.optimization_barrier(values)


def add_rounded(a, b):
    return (a.astype(jnp.float32) + b.astype(jnp.float32)).astype(jnp.bfloat16)


def core_swap(quarters):
    n = lax.axis_size("dp")
    c = lax.axis_index("dp") % 2
    paired = quarters.reshape(n // 2, 2, quarters.shape[0] // n, quarters.shape[1])
    away = lax.dynamic_index_in_dim(paired, 1 - c, 1, keepdims=False)
    kept = lax.dynamic_index_in_dim(paired, c, 1, keepdims=False)
    return kept, lax.ppermute(away, "dp", [(j, j ^ 1) for j in range(n)])


def y_swap(kept, got):
    n = lax.axis_size("dp")
    y = lax.axis_index("dp") // 2
    summed = kept.astype(jnp.float32) + got.astype(jnp.float32)
    other = lax.dynamic_index_in_dim(summed.astype(jnp.bfloat16), 1 - y, 0, keepdims=False)
    mine = lax.dynamic_index_in_dim(summed, y, 0, keepdims=False)
    return mine, lax.ppermute(other, "dp", [(j, j ^ 2) for j in range(n)])


def gathered_plan(tokens, routes, combine, cotangent, w_gate, w_up, w_down):
    tok_rows, features = tokens.shape
    groups = lax.axis_size("expert")
    me = lax.axis_index("expert")
    half = tok_rows // 2
    bf16 = jnp.bfloat16
    f32 = jnp.float32
    chosen = routes[:, :, None] == jnp.arange(groups, dtype=jnp.int32)[None, None, :]
    weights = jnp.sum(jnp.where(chosen, combine[:, :, None], 0.0), axis=1)
    sources = jnp.asarray(ring_sources(), jnp.int32)[me]
    wg, wu, wd = w_gate[0], w_up[0], w_down[0]

    def first_half(x, weight):
        gate_pre = jnp.dot(x, wg, preferred_element_type=f32)
        up_pre = jnp.dot(x, wu, preferred_element_type=f32)
        hidden = gate_pre * jax.nn.sigmoid(gate_pre) * up_pre
        scaled = (hidden * weight).astype(bf16)
        out_part = jnp.dot(scaled, wd, preferred_element_type=f32).astype(bf16)
        return gate_pre, up_pre, scaled, out_part

    def second_half(g, gate_pre, up_pre, weight):
        d_raw = jnp.einsum("td,fd->tf", g, wd, preferred_element_type=f32)
        sig = jax.nn.sigmoid(gate_pre)
        act = gate_pre * sig
        d_comb = jnp.sum(act * up_pre * d_raw, axis=1)
        d_hidden = d_raw * weight
        d_gate = (d_hidden * up_pre * sig * (1.0 + gate_pre * (1.0 - sig))).astype(bf16)
        d_up = (d_hidden * act).astype(bf16)
        d_rows = (
            jnp.einsum("tf,df->td", d_gate, wg, preferred_element_type=f32)
            + jnp.einsum("tf,df->td", d_up, wu, preferred_element_type=f32)
        ).astype(bf16)
        return d_gate, d_up, d_rows, d_comb

    xf, xb = forward(tokens), backward(tokens)
    gf, gb = forward(cotangent), backward(cotangent)
    arrived = lax.all_to_all(weights.T, "expert", split_axis=0, concat_axis=0, tiled=True)
    weight = arrived[sources]
    xs, gs = [tokens], [cotangent]
    x, g = tokens, cotangent
    firsts, seconds = [], []
    at = 0
    for step in range(5):
        rows = x.shape[0]
        w = lax.dynamic_slice_in_dim(weight.reshape(-1), at, rows, 0)[:, None]
        at += rows
        one = first_half(x, w)
        gf, gb, *one = tie(gf, gb, *one)
        if step > 0:
            g = jnp.concatenate([hold_gf, hold_gb], axis=0)
            gs.append(g)
        two = second_half(g, one[0], one[1], w)
        firsts.append(one)
        seconds.append(two)
        if step == 4:
            break
        hold_gf, hold_gb = gf, gb
        if step < 2:
            gf, gb = forward(gf), backward(gb)
        elif step == 2:
            gf, gb = forward(gf[:half]), backward(gb[half:])
        xf, xb, *two = tie(xf, xb, *two)
        seconds[-1] = two
        x = jnp.concatenate([xf, xb], axis=0)
        xs.append(x)
        if step < 2:
            xf, xb = forward(xf), backward(xb)
        elif step == 2:
            xf, xb = forward(xf[:half]), backward(xb[half:])

    scaled = jnp.concatenate([f[2] for f in firsts], axis=0)
    d_gate = jnp.concatenate([s[0] for s in seconds], axis=0)
    d_up = jnp.concatenate([s[1] for s in seconds], axis=0)
    all_x = jnp.concatenate(xs, axis=0)
    all_g = jnp.concatenate(gs, axis=0)
    d_comb = jnp.concatenate([s[3] for s in seconds], axis=0).reshape(groups, tok_rows)

    def grad(rows, cols):
        return jnp.einsum("td,tf->df", rows, cols, preferred_element_type=f32).astype(bf16)

    def send(chain, step, parts, got):
        own, one, two, three, far = parts
        f, b = got
        if step == 0:
            return forward(far[:half]), backward(far[half:])
        if step == 1:
            f = jnp.concatenate([add_rounded(three[:half], f), three[half:tok_rows]], axis=0)
            b = jnp.concatenate(
                [three[tok_rows:tok_rows + half], add_rounded(three[tok_rows + half:], b)], axis=0
            )
            return forward(f), backward(b)
        part = two if step == 2 else one
        return (
            forward(add_rounded(part[:tok_rows], f)),
            backward(add_rounded(part[tok_rows:], b)),
        )

    def finish(parts, got):
        total = parts[0].astype(f32) + got[0].astype(f32) + got[1].astype(f32)
        return total.astype(bf16)

    def swapped(parts):
        own, one, two, three, far = parts
        turn = lambda c: jnp.concatenate([c[tok_rows:], c[:tok_rows]], axis=0)
        return own, turn(one), turn(two), turn(three), far

    outs = swapped([f[3] for f in firsts])
    backs = swapped([s[2] for s in seconds])
    o = send("o", 0, outs, (None, None))
    t = send("t", 0, backs, (None, None))
    g_down = grad(all_g, scaled)
    *o, g_down = tie(*o, g_down)
    o = send("o", 1, outs, o)
    kept_d, got_d = core_swap(g_down)
    g_gate = grad(all_x, d_gate)
    *t, g_gate = tie(*t, g_gate)
    t = send("t", 1, backs, t)
    kept_g, got_g = core_swap(g_gate)
    g_up = grad(all_x, d_up)
    *o, g_up, got_d = tie(*o, g_up, got_d)
    o = send("o", 2, outs, o)
    mine_d, last_d = y_swap(kept_d, got_d)
    kept_u, got_u = core_swap(g_up)
    *t, got_g = tie(*t, got_g)
    t = send("t", 2, backs, t)
    mine_g, last_g = y_swap(kept_g, got_g)
    *o, got_u = tie(*o, got_u)
    o = send("o", 3, outs, o)
    mine_u, last_u = y_swap(kept_u, got_u)
    *t, last_d = tie(*t, last_d)
    t = send("t", 3, backs, t)
    d_w_down = (mine_d + last_d.astype(f32)).astype(bf16).T[None]
    d_w_gate = (mine_g + last_g.astype(f32)).astype(bf16)[None]
    output = finish(outs, o)
    d_w_up = (mine_u + last_u.astype(f32)).astype(bf16)[None]
    d_tokens = finish(backs, t)
    table = ring_sources()
    inverse = jnp.asarray([[row.index(e) for e in range(groups)] for row in table], jnp.int32)[me]
    back = lax.all_to_all(d_comb[inverse], "expert", split_axis=0, concat_axis=0, tiled=True)
    d_combine = jnp.sum(jnp.where(chosen, back.T[:, None, :], 0.0), axis=2)
    return output, d_tokens, d_combine, d_w_gate, d_w_up, d_w_down


def solution(mesh):
    rows = P(("dp", "expert"), None)
    small = mesh.shape["expert"] == len(RING) and mesh.shape["dp"] == 4
    return jax.shard_map(
        gathered_plan if small else routed_plan,
        mesh=mesh,
        in_specs=(rows, rows, rows, rows) + (P("expert", None, None),) * 3,
        out_specs=(
            rows,
            rows,
            rows,
            P("expert", "dp", None),
            P("expert", "dp", None),
            P("expert", None, "dp"),
        ),
        check_vma=False,
    )
```

```python
import functools
import jax
import jax.numpy as jnp
from jax import lax
from jax.experimental import pallas as pl
from jax.experimental.pallas import tpu as pltpu
from jax.sharding import PartitionSpec as P


def slot_map(routes, experts, capacity):
    flat_ids = routes.reshape(-1)
    onehot = (flat_ids[:, None] == jnp.arange(experts, dtype=jnp.int32)[None, :]).astype(jnp.int32)
    before = jnp.cumsum(onehot, axis=0) - onehot
    slots = jnp.sum(before * onehot, axis=1)
    target = flat_ids * capacity + slots
    source = (
        jnp.full((experts * capacity,), -1, jnp.int32)
        .at[target]
        .set(jnp.arange(flat_ids.shape[0], dtype=jnp.int32))
    )
    return (target, source)


def routed_plan(tokens, routes, combine, cotangent, w_gate, w_up, w_down):
    tok_rows, features = tokens.shape
    per_token = routes.shape[1]
    groups = lax.axis_size("expert")
    local_exp = w_gate.shape[0]
    experts = local_exp * groups
    capacity = 3 * tok_rows * per_token // (2 * experts)
    target, source = slot_map(routes, experts, capacity)
    filled = (source >= 0)[:, None]
    pair_index = jnp.maximum(source, 0)
    owner_row = pair_index // per_token
    outgoing = jnp.where(filled, tokens[owner_row], jnp.zeros((), jnp.bfloat16))
    outgoing = outgoing.reshape(groups, local_exp, capacity, features)
    cot_float = cotangent.astype(jnp.float32)
    scaled = (combine[:, :, None] * cot_float[:, None, :]).reshape(tok_rows * per_token, features)
    outgoing_grad = jnp.where(filled, scaled[pair_index], 0.0).astype(jnp.bfloat16)
    outgoing_grad = outgoing_grad.reshape(groups, local_exp, capacity, features)
    arrived = lax.all_to_all(outgoing, "expert", split_axis=0, concat_axis=0, tiled=True)
    gate_pre = jnp.einsum("secd,edf->secf", arrived, w_gate, preferred_element_type=jnp.float32)
    up_pre = jnp.einsum("secd,edf->secf", arrived, w_up, preferred_element_type=jnp.float32)
    activated = jax.nn.silu(gate_pre)
    hidden = (activated * up_pre).astype(jnp.bfloat16)
    produced = jnp.einsum(
        "secf,efd->secd", hidden, w_down, preferred_element_type=jnp.float32
    ).astype(jnp.bfloat16)
    returned = lax.all_to_all(produced, "expert", split_axis=0, concat_axis=0, tiled=True)
    d_in = lax.all_to_all(outgoing_grad, "expert", split_axis=0, concat_axis=0, tiled=True)
    d_hidden = jnp.einsum("secd,efd->secf", d_in, w_down, preferred_element_type=jnp.float32)
    part_down = jnp.einsum("secf,secd->efd", hidden, d_in, preferred_element_type=jnp.float32)
    sigmoid_g = jax.nn.sigmoid(gate_pre)
    d_gate = (d_hidden * up_pre * sigmoid_g * (1.0 + gate_pre * (1.0 - sigmoid_g))).astype(
        jnp.bfloat16
    )
    d_up = (d_hidden * activated).astype(jnp.bfloat16)
    part_gate = jnp.einsum("secd,secf->edf", arrived, d_gate, preferred_element_type=jnp.float32)
    part_up = jnp.einsum("secd,secf->edf", arrived, d_up, preferred_element_type=jnp.float32)
    d_rows = (
        jnp.einsum("secf,edf->secd", d_gate, w_gate, preferred_element_type=jnp.float32)
        + jnp.einsum("secf,edf->secd", d_up, w_up, preferred_element_type=jnp.float32)
    ).astype(jnp.bfloat16)
    back = lax.all_to_all(d_rows, "expert", split_axis=0, concat_axis=0, tiled=True)
    per_slot = returned.reshape(experts * capacity, features)[target]
    per_slot = per_slot.reshape(tok_rows, per_token, features).astype(jnp.float32)
    output = jnp.sum(combine[:, :, None] * per_slot, axis=1).astype(jnp.bfloat16)
    d_combine = jnp.sum(per_slot * cot_float[:, None, :], axis=2)
    back_slot = back.reshape(experts * capacity, features)[target]
    back_slot = back_slot.reshape(tok_rows, per_token, features).astype(jnp.float32)
    d_tokens = jnp.sum(back_slot, axis=1).astype(jnp.bfloat16)
    sum_gate, sum_up, sum_down = (
        lax.psum_scatter(
            part_gate.astype(jnp.bfloat16), "dp", scatter_dimension=1, tiled=True
        ).astype(jnp.float32),
        lax.psum_scatter(
            part_up.astype(jnp.bfloat16), "dp", scatter_dimension=1, tiled=True
        ).astype(jnp.float32),
        lax.psum_scatter(
            part_down.astype(jnp.bfloat16), "dp", scatter_dimension=2, tiled=True
        ).astype(jnp.float32),
    )
    d_w_down = sum_down.astype(jnp.bfloat16)
    return (
        output,
        d_tokens,
        d_combine,
        sum_gate.astype(jnp.bfloat16),
        sum_up.astype(jnp.bfloat16),
        d_w_down,
    )


RING = (0, 1, 3, 5, 7, 6, 4, 2)


def ring_perms():
    n = len(RING)
    fwd = [(RING[i], RING[(i + 1) % n]) for i in range(n)]
    bwd = [(RING[(i + 1) % n], RING[i]) for i in range(n)]
    return fwd, bwd


def ring_sources():
    n = len(RING)
    place = {e: i for i, e in enumerate(RING)}
    steps = (0, -1, 1, -2, 2, -3, 3, 4)
    return [[RING[(place[e] + r) % n] for r in steps] for e in range(n)]


def forward(value):
    return lax.ppermute(value, "expert", ring_perms()[0])


def backward(value):
    return lax.ppermute(value, "expert", ring_perms()[1])


def tie(*values):
    return lax.optimization_barrier(values)


def add_rounded(a, b):
    return (a.astype(jnp.float32) + b.astype(jnp.float32)).astype(jnp.bfloat16)


def core_swap(quarters):
    n = lax.axis_size("dp")
    c = lax.axis_index("dp") % 2
    paired = quarters.reshape(n // 2, 2, quarters.shape[0] // n, quarters.shape[1])
    away = lax.dynamic_index_in_dim(paired, 1 - c, 1, keepdims=False)
    kept = lax.dynamic_index_in_dim(paired, c, 1, keepdims=False)
    return kept, lax.ppermute(away, "dp", [(j, j ^ 1) for j in range(n)])


def y_swap(kept, got):
    n = lax.axis_size("dp")
    y = lax.axis_index("dp") // 2
    summed = kept.astype(jnp.float32) + got.astype(jnp.float32)
    other = lax.dynamic_index_in_dim(summed.astype(jnp.bfloat16), 1 - y, 0, keepdims=False)
    mine = lax.dynamic_index_in_dim(summed, y, 0, keepdims=False)
    return mine, lax.ppermute(other, "dp", [(j, j ^ 2) for j in range(n)])


ANY = pl.BlockSpec(memory_space=pl.ANY)
NT = (((1,), (1,)), ((), ()))
TILE = 256
WIDE = 512


def dot_nt(a, b):
    return lax.dot_general(a, b, NT, preferred_element_type=jnp.float32)


class Mover:
    def __init__(self, sems):
        self.sems = sems
        self.used = 0

    def go(self, src, dst):
        copy = pltpu.make_async_copy(src, dst, self.sems.at[self.used])
        self.used += 1
        copy.start()
        return copy


def first_kernel(at, n, seeded, *refs):
    blocks, refs = refs[:n], refs[n:]
    w, wg, wu, wd = refs[:4]
    refs = refs[4 + (2 if seeded else 0):]
    outs, refs = refs[:n], refs[n:]
    gate_o, up_o, xall, sall, x2, wv, wgv, wuv, wdv, gv, uv, sv, ov, sems = refs
    part = blocks[0].shape[0]
    rows, features = x2.shape
    ff = gv.shape[1]
    move = Mover(sems)
    loads = [move.go(w.at[pl.ds(at, rows)], wv)]
    loads += [move.go(b, x2.at[pl.ds(i * part, part)]) for i, b in enumerate(blocks)]
    loads.append(move.go(wg, wgv))
    load_u = move.go(wu, wuv)
    load_d = move.go(wd, wdv)
    stores = [move.go(b, xall.at[pl.ds(at + i * part, part)]) for i, b in enumerate(blocks)]
    for c in loads:
        c.wait()
    for f in range(0, ff, TILE):
        gv[:, f:f + TILE] = jnp.dot(
            x2[...], wgv[:, f:f + TILE], preferred_element_type=jnp.float32
        )
    stores.append(move.go(gv, gate_o))
    load_u.wait()
    for f in range(0, ff, TILE):
        up = jnp.dot(x2[...], wuv[:, f:f + TILE], preferred_element_type=jnp.float32)
        uv[:, f:f + TILE] = up
        gate = gv[:, f:f + TILE]
        sv[:, f:f + TILE] = (gate * jax.nn.sigmoid(gate) * up * wv[...]).astype(jnp.bfloat16)
    stores.append(move.go(uv, up_o))
    stores.append(move.go(sv, sall.at[pl.ds(at, rows)]))
    load_d.wait()
    for d in range(0, features, WIDE):
        ov[:, d:d + WIDE] = jnp.dot(
            sv[...], wdv[:, d:d + WIDE], preferred_element_type=jnp.float32
        ).astype(jnp.bfloat16)
    stores += [move.go(ov.at[pl.ds(i * part, part)], o) for i, o in enumerate(outs)]
    for c in stores:
        c.wait()


def second_kernel(at, n, seeded, *refs):
    blocks, refs = refs[:n], refs[n:]
    gate_i, up_i, w, wg, wu, wd = refs[:6]
    refs = refs[6 + (3 if seeded else 0):]
    outs, refs = refs[:n], refs[n:]
    comb_o, gall, dgall, duall, g2, wv, wgv, wuv, wdv, gv, uv, dgv, duv, cv, ov, sems = refs
    part = blocks[0].shape[0]
    rows, features = g2.shape
    ff = gv.shape[1]
    move = Mover(sems)
    loads = [move.go(w.at[pl.ds(at, rows)], wv)]
    loads += [move.go(b, g2.at[pl.ds(i * part, part)]) for i, b in enumerate(blocks)]
    loads += [move.go(wd, wdv), move.go(gate_i, gv), move.go(up_i, uv)]
    late = [move.go(wg, wgv), move.go(wu, wuv)]
    stores = [move.go(b, gall.at[pl.ds(at + i * part, part)]) for i, b in enumerate(blocks)]
    for c in loads:
        c.wait()
    comb = jnp.zeros((rows, 1), jnp.float32)
    for f in range(0, ff, TILE):
        d_raw = dot_nt(g2[...], wdv[f:f + TILE, :])
        gate, up = gv[:, f:f + TILE], uv[:, f:f + TILE]
        sig = jax.nn.sigmoid(gate)
        act = gate * sig
        comb += jnp.sum(act * up * d_raw, axis=1, keepdims=True)
        d_hidden = d_raw * wv[...]
        dgv[:, f:f + TILE] = (d_hidden * up * sig * (1.0 + gate * (1.0 - sig))).astype(jnp.bfloat16)
        duv[:, f:f + TILE] = (d_hidden * act).astype(jnp.bfloat16)
    cv[...] = comb
    stores.append(move.go(cv, comb_o))
    stores.append(move.go(dgv, dgall.at[pl.ds(at, rows)]))
    stores.append(move.go(duv, duall.at[pl.ds(at, rows)]))
    for c in late:
        c.wait()
    for d in range(0, features, WIDE):
        ov[:, d:d + WIDE] = (
            dot_nt(dgv[...], wgv[d:d + WIDE, :]) + dot_nt(duv[...], wuv[d:d + WIDE, :])
        ).astype(jnp.bfloat16)
    stores += [move.go(ov.at[pl.ds(i * part, part)], o) for i, o in enumerate(outs)]
    for c in stores:
        c.wait()


def chunk_call(kernel, name, at, blocks, extra, weight, w_at, ws, wholes, out_shapes, total, scratch, flops):
    n = len(blocks)
    seeded = wholes[0] is not None
    whole_shapes = [jax.ShapeDtypeStruct((total, c), jnp.bfloat16) for c in scratch["wholes"]]
    operands = list(blocks) + list(extra) + [weight] + list(ws) + (list(wholes) if seeded else [])
    first_whole_in = n + len(extra) + 1 + len(ws)
    first_whole_out = len(out_shapes)
    aliases = (
        {first_whole_in + i: first_whole_out + i for i in range(len(whole_shapes))} if seeded else {}
    )
    return pl.pallas_call(
        kernel,
        out_shape=list(out_shapes) + whole_shapes,
        in_specs=[ANY] * len(operands),
        out_specs=[ANY] * (len(out_shapes) + len(whole_shapes)),
        scratch_shapes=scratch["vmem"] + [pltpu.SemaphoreType.DMA((20,))],
        input_output_aliases=aliases,
        compiler_params=pltpu.CompilerParams(vmem_limit_bytes=36 * 1024 * 1024),
        cost_estimate=pl.CostEstimate(flops=flops, bytes_accessed=12_000_000, transcendentals=0),
        name=name,
    )(*operands)


def first_half(at, blocks, weight, w_at, ws, wholes, total):
    n, (part, features) = len(blocks), blocks[0].shape
    ff = ws[0].shape[1]
    rows = n * part
    bf16, f32 = jnp.bfloat16, jnp.float32
    out_shapes = [jax.ShapeDtypeStruct((part, features), bf16)] * n
    out_shapes += [jax.ShapeDtypeStruct((rows, ff), f32)] * 2
    scratch = {
        "wholes": (features, ff),
        "vmem": [
            pltpu.VMEM((rows, features), bf16),
            pltpu.VMEM((rows, 1), f32),
            pltpu.VMEM((features, ff), bf16),
            pltpu.VMEM((features, ff), bf16),
            pltpu.VMEM((ff, features), bf16),
            pltpu.VMEM((rows, ff), f32),
            pltpu.VMEM((rows, ff), f32),
            pltpu.VMEM((rows, ff), bf16),
            pltpu.VMEM((rows, features), bf16),
        ],
    }
    res = chunk_call(
        functools.partial(first_kernel, at, n, wholes[0] is not None), f"first_{at}",
        at, blocks, [], weight, w_at, ws, wholes, out_shapes, total, scratch,
        6 * rows * features * ff,
    )
    return res[:n], res[n], res[n + 1], res[n + 2:]


def second_half(at, blocks, gate, up, weight, w_at, ws, wholes, total):
    n, (part, features) = len(blocks), blocks[0].shape
    ff = ws[0].shape[1]
    rows = n * part
    bf16, f32 = jnp.bfloat16, jnp.float32
    out_shapes = [jax.ShapeDtypeStruct((part, features), bf16)] * n
    out_shapes += [jax.ShapeDtypeStruct((rows, 1), f32)]
    scratch = {
        "wholes": (features, ff, ff),
        "vmem": [
            pltpu.VMEM((rows, features), bf16),
            pltpu.VMEM((rows, 1), f32),
            pltpu.VMEM((features, ff), bf16),
            pltpu.VMEM((features, ff), bf16),
            pltpu.VMEM((ff, features), bf16),
            pltpu.VMEM((rows, ff), f32),
            pltpu.VMEM((rows, ff), f32),
            pltpu.VMEM((rows, ff), bf16),
            pltpu.VMEM((rows, ff), bf16),
            pltpu.VMEM((rows, 1), f32),
            pltpu.VMEM((rows, features), bf16),
        ],
    }
    res = chunk_call(
        functools.partial(second_kernel, at, n, wholes[0] is not None), f"second_{at}",
        at, blocks, [gate, up], weight, w_at, ws, wholes, out_shapes, total, scratch,
        6 * rows * features * ff,
    )
    return res[:n], res[n], res[n + 1:]


def gathered_plan(tokens, routes, combine, cotangent, w_gate, w_up, w_down):
    tok_rows, features = tokens.shape
    groups = lax.axis_size("expert")
    me = lax.axis_index("expert")
    half = tok_rows // 2
    total = groups * tok_rows
    bf16 = jnp.bfloat16
    f32 = jnp.float32
    chosen = routes[:, :, None] == jnp.arange(groups, dtype=jnp.int32)[None, None, :]
    weights = jnp.sum(jnp.where(chosen, combine[:, :, None], 0.0), axis=1)
    sources = jnp.asarray(ring_sources(), jnp.int32)[me]
    ws = (w_gate[0], w_up[0], w_down[0])

    xf, xb = forward(tokens), backward(tokens)
    gf, gb = forward(cotangent), backward(cotangent)
    mine = jnp.arange(groups, dtype=jnp.int32)[None, :] == me
    own_weight = jnp.sum(jnp.where(mine, weights, 0.0), axis=1, keepdims=True)
    arrived = lax.all_to_all(weights.T, "expert", split_axis=0, concat_axis=0, tiled=True)
    weight = arrived[sources].reshape(total, 1)

    outs, backs, combs = [], [], []
    firsts, seconds = (None, None), (None, None, None)
    at = 0
    xs, gs = [tokens], [cotangent]
    for step in range(5):
        w = own_weight if step == 0 else weight
        out, gate, up, firsts = first_half(at, xs, w, at, ws, firsts, total)
        outs.append(out)
        if step == 4:
            o = (forward(out[0]), backward(out[1]))
        gf, gb, gate, *firsts = tie(gf, gb, gate, *firsts)
        if step > 0:
            gs = [hold_gf, hold_gb]
        if step < 4:
            hold_gf, hold_gb = gf, gb
        if step < 2:
            gf, gb = forward(gf), backward(gb)
        elif step == 2:
            gf, gb = forward(gf[:half]), backward(gb[half:])
        back, comb, seconds = second_half(at, gs, gate, up, w, at, ws, seconds, total)
        backs.append(back)
        combs.append(comb)
        at += len(xs) * xs[0].shape[0]
        if step == 4:
            break
        xf, xb, *seconds = tie(xf, xb, *seconds)
        xs = [xf, xb]
        if step < 2:
            xf, xb = forward(xf), backward(xb)
        elif step == 2:
            xf, xb = forward(xf[:half]), backward(xb[half:])

    all_x, scaled = firsts
    all_g, d_gate, d_up = seconds

    def grad(rows, cols):
        return jnp.einsum("td,tf->df", rows, cols, preferred_element_type=f32).astype(bf16)

    def advance(step, parts, got):
        behind, ahead = parts[4 - step]
        f, b = got
        if step == 1:
            f = lax.dynamic_update_slice(ahead, add_rounded(ahead[:half], f), (0, 0))
            b = lax.dynamic_update_slice(behind, add_rounded(behind[half:], b), (half, 0))
            return forward(f), backward(b)
        return forward(add_rounded(ahead, f)), backward(add_rounded(behind, b))

    def finish(parts, got):
        (own,) = parts[0]
        return (own.astype(f32) + got[0].astype(f32) + got[1].astype(f32)).astype(bf16)

    t = (forward(backs[4][0]), backward(backs[4][1]))
    g_down = grad(all_g, scaled)
    kept_d, got_d = core_swap(g_down)
    *o, g_down = tie(*o, g_down)
    o = advance(1, outs, o)
    *t, d_gate, comb_last = tie(*t, d_gate, combs[-1])
    t = advance(1, backs, t)
    g_gate = grad(all_x, d_gate)
    kept_g, got_g = core_swap(g_gate)
    got_d, g_gate, comb_last = tie(got_d, g_gate, comb_last)
    mine_d, last_d = y_swap(kept_d, got_d)
    d_comb = jnp.concatenate(combs[:-1] + [comb_last], axis=0).reshape(groups, tok_rows)
    table = ring_sources()
    inverse = jnp.asarray([[row.index(e) for e in range(groups)] for row in table], jnp.int32)[me]
    back = lax.all_to_all(d_comb[inverse], "expert", split_axis=0, concat_axis=0, tiled=True)
    *o, d_up = tie(*o, d_up)
    o = advance(2, outs, o)
    g_up = grad(all_x, d_up)
    kept_u, got_u = core_swap(g_up)
    *t, g_up, got_g = tie(*t, g_up, got_g)
    t = advance(2, backs, t)
    mine_g, last_g = y_swap(kept_g, got_g)
    *o, got_u = tie(*o, got_u)
    o = advance(3, outs, o)
    mine_u, last_u = y_swap(kept_u, got_u)
    *t, last_d = tie(*t, last_d)
    t = advance(3, backs, t)
    d_w_down = (mine_d + last_d.astype(f32)).astype(bf16).T[None]
    output = finish(outs, o)
    d_w_gate = (mine_g + last_g.astype(f32)).astype(bf16)[None]
    d_w_up = (mine_u + last_u.astype(f32)).astype(bf16)[None]
    d_tokens = finish(backs, t)
    d_combine = jnp.sum(jnp.where(chosen, back.T[:, None, :], 0.0), axis=2)
    return output, d_tokens, d_combine, d_w_gate, d_w_up, d_w_down


def solution(mesh):
    rows = P(("dp", "expert"), None)
    small = mesh.shape["expert"] == len(RING) and mesh.shape["dp"] == 4
    return jax.shard_map(
        gathered_plan if small else routed_plan,
        mesh=mesh,
        in_specs=(rows, rows, rows, rows) + (P("expert", None, None),) * 3,
        out_specs=(
            rows,
            rows,
            rows,
            P("expert", "dp", None),
            P("expert", "dp", None),
            P("expert", None, "dp"),
        ),
        check_vma=False,
    )
```

```python
import functools
import jax
import jax.numpy as jnp
from jax import lax
from jax.experimental import pallas as pl
from jax.experimental.pallas import tpu as pltpu
from jax.sharding import PartitionSpec as P


def slot_map(routes, experts, capacity):
    flat_ids = routes.reshape(-1)
    onehot = (flat_ids[:, None] == jnp.arange(experts, dtype=jnp.int32)[None, :]).astype(jnp.int32)
    before = jnp.cumsum(onehot, axis=0) - onehot
    slots = jnp.sum(before * onehot, axis=1)
    target = flat_ids * capacity + slots
    source = (
        jnp.full((experts * capacity,), -1, jnp.int32)
        .at[target]
        .set(jnp.arange(flat_ids.shape[0], dtype=jnp.int32))
    )
    return (target, source)


def routed_plan(tokens, routes, combine, cotangent, w_gate, w_up, w_down):
    tok_rows, features = tokens.shape
    per_token = routes.shape[1]
    groups = lax.axis_size("expert")
    local_exp = w_gate.shape[0]
    experts = local_exp * groups
    capacity = 3 * tok_rows * per_token // (2 * experts)
    target, source = slot_map(routes, experts, capacity)
    filled = (source >= 0)[:, None]
    pair_index = jnp.maximum(source, 0)
    owner_row = pair_index // per_token
    outgoing = jnp.where(filled, tokens[owner_row], jnp.zeros((), jnp.bfloat16))
    outgoing = outgoing.reshape(groups, local_exp, capacity, features)
    cot_float = cotangent.astype(jnp.float32)
    scaled = (combine[:, :, None] * cot_float[:, None, :]).reshape(tok_rows * per_token, features)
    outgoing_grad = jnp.where(filled, scaled[pair_index], 0.0).astype(jnp.bfloat16)
    outgoing_grad = outgoing_grad.reshape(groups, local_exp, capacity, features)
    arrived = lax.all_to_all(outgoing, "expert", split_axis=0, concat_axis=0, tiled=True)
    gate_pre = jnp.einsum("secd,edf->secf", arrived, w_gate, preferred_element_type=jnp.float32)
    up_pre = jnp.einsum("secd,edf->secf", arrived, w_up, preferred_element_type=jnp.float32)
    activated = jax.nn.silu(gate_pre)
    hidden = (activated * up_pre).astype(jnp.bfloat16)
    produced = jnp.einsum(
        "secf,efd->secd", hidden, w_down, preferred_element_type=jnp.float32
    ).astype(jnp.bfloat16)
    returned = lax.all_to_all(produced, "expert", split_axis=0, concat_axis=0, tiled=True)
    d_in = lax.all_to_all(outgoing_grad, "expert", split_axis=0, concat_axis=0, tiled=True)
    d_hidden = jnp.einsum("secd,efd->secf", d_in, w_down, preferred_element_type=jnp.float32)
    part_down = jnp.einsum("secf,secd->efd", hidden, d_in, preferred_element_type=jnp.float32)
    sigmoid_g = jax.nn.sigmoid(gate_pre)
    d_gate = (d_hidden * up_pre * sigmoid_g * (1.0 + gate_pre * (1.0 - sigmoid_g))).astype(
        jnp.bfloat16
    )
    d_up = (d_hidden * activated).astype(jnp.bfloat16)
    part_gate = jnp.einsum("secd,secf->edf", arrived, d_gate, preferred_element_type=jnp.float32)
    part_up = jnp.einsum("secd,secf->edf", arrived, d_up, preferred_element_type=jnp.float32)
    d_rows = (
        jnp.einsum("secf,edf->secd", d_gate, w_gate, preferred_element_type=jnp.float32)
        + jnp.einsum("secf,edf->secd", d_up, w_up, preferred_element_type=jnp.float32)
    ).astype(jnp.bfloat16)
    back = lax.all_to_all(d_rows, "expert", split_axis=0, concat_axis=0, tiled=True)
    per_slot = returned.reshape(experts * capacity, features)[target]
    per_slot = per_slot.reshape(tok_rows, per_token, features).astype(jnp.float32)
    output = jnp.sum(combine[:, :, None] * per_slot, axis=1).astype(jnp.bfloat16)
    d_combine = jnp.sum(per_slot * cot_float[:, None, :], axis=2)
    back_slot = back.reshape(experts * capacity, features)[target]
    back_slot = back_slot.reshape(tok_rows, per_token, features).astype(jnp.float32)
    d_tokens = jnp.sum(back_slot, axis=1).astype(jnp.bfloat16)
    sum_gate, sum_up, sum_down = (
        lax.psum_scatter(
            part_gate.astype(jnp.bfloat16), "dp", scatter_dimension=1, tiled=True
        ).astype(jnp.float32),
        lax.psum_scatter(
            part_up.astype(jnp.bfloat16), "dp", scatter_dimension=1, tiled=True
        ).astype(jnp.float32),
        lax.psum_scatter(
            part_down.astype(jnp.bfloat16), "dp", scatter_dimension=2, tiled=True
        ).astype(jnp.float32),
    )
    d_w_down = sum_down.astype(jnp.bfloat16)
    return (
        output,
        d_tokens,
        d_combine,
        sum_gate.astype(jnp.bfloat16),
        sum_up.astype(jnp.bfloat16),
        d_w_down,
    )


RING = (0, 1, 3, 5, 7, 6, 4, 2)


def ring_perms():
    n = len(RING)
    fwd = [(RING[i], RING[(i + 1) % n]) for i in range(n)]
    bwd = [(RING[(i + 1) % n], RING[i]) for i in range(n)]
    return fwd, bwd


def ring_sources():
    n = len(RING)
    place = {e: i for i, e in enumerate(RING)}
    steps = (0, -1, 1, -2, 2, -3, 3, 4)
    return [[RING[(place[e] + r) % n] for r in steps] for e in range(n)]


def forward(value):
    return lax.ppermute(value, "expert", ring_perms()[0])


def backward(value):
    return lax.ppermute(value, "expert", ring_perms()[1])


def tie(*values):
    return lax.optimization_barrier(values)


def add_rounded(a, b):
    return (a.astype(jnp.float32) + b.astype(jnp.float32)).astype(jnp.bfloat16)


def core_swap(away):
    n = lax.axis_size("dp")
    return lax.ppermute(away, "dp", [(j, j ^ 1) for j in range(n)])


def pick(halves, y):
    return lax.dynamic_index_in_dim(halves, y, 0, keepdims=False)


def y_swap(kept, got):
    n = lax.axis_size("dp")
    y = lax.axis_index("dp") // 2
    other = add_rounded(pick(kept, 1 - y), pick(got, 1 - y))
    return lax.ppermute(other, "dp", [(j, j ^ 2) for j in range(n)])


def dp_total(kept, got, last):
    y = lax.axis_index("dp") // 2
    total = pick(kept, y).astype(jnp.float32) + pick(got, y).astype(jnp.float32)
    return (total + last.astype(jnp.float32)).astype(jnp.bfloat16)[None]


HBM = pl.BlockSpec(memory_space=pltpu.HBM)
NT = (((1,), (1,)), ((), ()))
TILE = 256
KERNEL_VMEM = 61 * 1024 * 1024
WIDE = 512


def dot_nt(a, b):
    return lax.dot_general(a, b, NT, preferred_element_type=jnp.float32)


class Mover:
    def __init__(self, sems):
        self.sems = sems
        self.used = 0

    def go(self, src, dst):
        copy = pltpu.make_async_copy(src, dst, self.sems.at[self.used])
        self.used += 1
        copy.start()
        return copy


def first_kernel(at, n, seeded, *refs):
    blocks, refs = refs[:n], refs[n:]
    w, wg, wu, wd = refs[:4]
    refs = refs[4 + (2 if seeded else 0):]
    outs, refs = refs[:n], refs[n:]
    gate_o, up_o, xall, sall, x2, wv, wgv, wuv, wdv, gv, uv, sv, ov, sems = refs
    part = blocks[0].shape[0]
    rows, features = x2.shape
    ff = gv.shape[1]
    move = Mover(sems)
    cols = [pl.ds(f, TILE) for f in range(0, ff, TILE)]
    wide = [pl.ds(d, WIDE) for d in range(0, features, WIDE)]
    load_x = [move.go(b, x2.at[pl.ds(i * part, part)]) for i, b in enumerate(blocks)]
    load_g = [move.go(wg.at[:, c], wgv.at[:, c]) for c in cols]
    load_w = move.go(w.at[pl.ds(at, rows)], wv)
    load_u = [move.go(wu.at[:, c], wuv.at[:, c]) for c in cols]
    load_d = [move.go(wd.at[:, c], wdv.at[:, c]) for c in wide]
    for c in load_x:
        c.wait()
    stores = [move.go(x2, xall.at[pl.ds(at, rows)])]
    for c, load in zip(cols, load_g):
        load.wait()
        gv[:, c] = jnp.dot(x2[...], wgv[:, c], preferred_element_type=jnp.float32)
    stores.append(move.go(gv, gate_o))
    load_w.wait()
    for c, load in zip(cols, load_u):
        load.wait()
        up = jnp.dot(x2[...], wuv[:, c], preferred_element_type=jnp.float32)
        uv[:, c] = up
        gate = gv[:, c]
        sv[:, c] = (gate * jax.nn.sigmoid(gate) * up * wv[...]).astype(jnp.bfloat16)
    stores.append(move.go(uv, up_o))
    stores.append(move.go(sv, sall.at[pl.ds(at, rows)]))
    for c, load in zip(wide, load_d):
        load.wait()
        ov[:, c] = jnp.dot(sv[...], wdv[:, c], preferred_element_type=jnp.float32).astype(
            jnp.bfloat16
        )
    stores += [move.go(ov.at[pl.ds(i * part, part)], o) for i, o in enumerate(outs)]
    for c in stores:
        c.wait()


def second_kernel(at, n, seeded, *refs):
    blocks, refs = refs[:n], refs[n:]
    gate_i, up_i, w, wg, wu, wd = refs[:6]
    refs = refs[6 + (3 if seeded else 0):]
    outs, refs = refs[:n], refs[n:]
    comb_o, gall, dgall, duall, g2, wv, wgv, wuv, wdv, gv, uv, dgv, duv, cv, ov, sems = refs
    part = blocks[0].shape[0]
    rows, features = g2.shape
    ff = gv.shape[1]
    move = Mover(sems)
    cols = [pl.ds(f, TILE) for f in range(0, ff, TILE)]
    wide = [pl.ds(d, WIDE) for d in range(0, features, WIDE)]
    load_x = [move.go(b, g2.at[pl.ds(i * part, part)]) for i, b in enumerate(blocks)]
    load_d = [move.go(wd.at[c], wdv.at[c]) for c in cols]
    load_p = [move.go(w.at[pl.ds(at, rows)], wv), move.go(gate_i, gv), move.go(up_i, uv)]
    load_g = [move.go(wg.at[c], wgv.at[c]) for c in wide]
    load_u = [move.go(wu.at[c], wuv.at[c]) for c in wide]
    for c in load_x:
        c.wait()
    stores = [move.go(g2, gall.at[pl.ds(at, rows)])]
    comb = jnp.zeros((rows, 1), jnp.float32)
    for i, c in enumerate(cols):
        load_d[i].wait()
        d_raw = dot_nt(g2[...], wdv[c, :])
        if i == 0:
            for load in load_p:
                load.wait()
        gate, up = gv[:, c], uv[:, c]
        sig = jax.nn.sigmoid(gate)
        act = gate * sig
        comb += jnp.sum(act * up * d_raw, axis=1, keepdims=True)
        d_hidden = d_raw * wv[...]
        dgv[:, c] = (d_hidden * up * sig * (1.0 + gate * (1.0 - sig))).astype(jnp.bfloat16)
        duv[:, c] = (d_hidden * act).astype(jnp.bfloat16)
    cv[...] = comb
    stores.append(move.go(cv, comb_o))
    stores.append(move.go(dgv, dgall.at[pl.ds(at, rows)]))
    stores.append(move.go(duv, duall.at[pl.ds(at, rows)]))
    for i, c in enumerate(wide):
        load_g[i].wait()
        load_u[i].wait()
        ov[:, c] = (dot_nt(dgv[...], wgv[c, :]) + dot_nt(duv[...], wuv[c, :])).astype(jnp.bfloat16)
    stores += [move.go(ov.at[pl.ds(i * part, part)], o) for i, o in enumerate(outs)]
    for c in stores:
        c.wait()


def cut_kernel(core, cut, whole, away, kept):
    product = lax.dot_general(
        cut[...], whole[...], (((0,), (0,)), ((), ())), preferred_element_type=jnp.float32
    ).astype(jnp.bfloat16)[None]
    held = pl.program_id(0) // 2

    @pl.when(held == 0)
    def _():
        away[...] = product

    @pl.when(held == 1)
    def _():
        kept[...] = product


def cut_kernel_right(core, cut, whole, away, kept):
    product = lax.dot_general(
        whole[...], cut[...], (((0,), (0,)), ((), ())), preferred_element_type=jnp.float32
    ).astype(jnp.bfloat16)[None]
    held = pl.program_id(0) // 2

    @pl.when(held == 0)
    def _():
        away[...] = product

    @pl.when(held == 1)
    def _():
        kept[...] = product


def gradient(cut, whole, name, cut_left):
    rows, features = cut.shape
    ff = whole.shape[1]
    n = lax.axis_size("dp")
    size = features // n
    core = (lax.axis_index("dp") % 2).reshape(1)
    shape = (1, size, ff) if cut_left else (1, ff, size)
    half = jax.ShapeDtypeStruct((n // 2,) + shape[1:], jnp.bfloat16)

    def quarter(i, core):
        held = i // 2
        return 0, (i % 2) * 2 + jnp.where(held == 0, 1 - core[0], core[0])

    return pl.pallas_call(
        cut_kernel if cut_left else cut_kernel_right,
        out_shape=[half, half],
        grid_spec=pltpu.PrefetchScalarGridSpec(
            num_scalar_prefetch=1,
            grid=(n,),
            in_specs=[
                pl.BlockSpec((rows, size), quarter),
                pl.BlockSpec((rows, ff), lambda i, core: (0, 0)),
            ],
            out_specs=[
                pl.BlockSpec(shape, lambda i, core: (jnp.minimum(i, 1), 0, 0)),
                pl.BlockSpec(shape, lambda i, core: (jnp.maximum(i - 2, 0), 0, 0)),
            ],
        ),
        compiler_params=pltpu.CompilerParams(vmem_limit_bytes=KERNEL_VMEM),
        cost_estimate=pl.CostEstimate(
            flops=2 * rows * features * ff, bytes_accessed=9_000_000, transcendentals=0
        ),
        name=name,
    )(core, cut, whole)


def chunk_call(kernel, name, at, blocks, extra, weight, w_at, ws, wholes, out_shapes, total, scratch, flops):
    n = len(blocks)
    seeded = wholes[0] is not None
    whole_shapes = [jax.ShapeDtypeStruct((total, c), jnp.bfloat16) for c in scratch["wholes"]]
    operands = list(blocks) + list(extra) + [weight] + list(ws) + (list(wholes) if seeded else [])
    first_whole_in = n + len(extra) + 1 + len(ws)
    first_whole_out = len(out_shapes)
    aliases = (
        {first_whole_in + i: first_whole_out + i for i in range(len(whole_shapes))} if seeded else {}
    )
    return pl.pallas_call(
        kernel,
        out_shape=list(out_shapes) + whole_shapes,
        in_specs=[HBM] * len(operands),
        out_specs=[HBM] * (len(out_shapes) + len(whole_shapes)),
        scratch_shapes=scratch["vmem"] + [pltpu.SemaphoreType.DMA((24,))],
        input_output_aliases=aliases,
        compiler_params=pltpu.CompilerParams(vmem_limit_bytes=KERNEL_VMEM),
        cost_estimate=pl.CostEstimate(flops=flops, bytes_accessed=12_000_000, transcendentals=0),
        name=name,
    )(*operands)


def first_half(at, blocks, weight, w_at, ws, wholes, total):
    n, (part, features) = len(blocks), blocks[0].shape
    ff = ws[0].shape[1]
    rows = n * part
    bf16, f32 = jnp.bfloat16, jnp.float32
    out_shapes = [jax.ShapeDtypeStruct((part, features), bf16)] * n
    out_shapes += [jax.ShapeDtypeStruct((rows, ff), f32)] * 2
    scratch = {
        "wholes": (features, ff),
        "vmem": [
            pltpu.VMEM((rows, features), bf16),
            pltpu.VMEM((rows, 1), f32),
            pltpu.VMEM((features, ff), bf16),
            pltpu.VMEM((features, ff), bf16),
            pltpu.VMEM((ff, features), bf16),
            pltpu.VMEM((rows, ff), f32),
            pltpu.VMEM((rows, ff), f32),
            pltpu.VMEM((rows, ff), bf16),
            pltpu.VMEM((rows, features), bf16),
        ],
    }
    res = chunk_call(
        functools.partial(first_kernel, at, n, wholes[0] is not None), f"first_{at}",
        at, blocks, [], weight, w_at, ws, wholes, out_shapes, total, scratch,
        6 * rows * features * ff,
    )
    return res[:n], res[n], res[n + 1], res[n + 2:]


def second_half(at, blocks, gate, up, weight, w_at, ws, wholes, total):
    n, (part, features) = len(blocks), blocks[0].shape
    ff = ws[0].shape[1]
    rows = n * part
    bf16, f32 = jnp.bfloat16, jnp.float32
    out_shapes = [jax.ShapeDtypeStruct((part, features), bf16)] * n
    out_shapes += [jax.ShapeDtypeStruct((rows, 1), f32)]
    scratch = {
        "wholes": (features, ff, ff),
        "vmem": [
            pltpu.VMEM((rows, features), bf16),
            pltpu.VMEM((rows, 1), f32),
            pltpu.VMEM((features, ff), bf16),
            pltpu.VMEM((features, ff), bf16),
            pltpu.VMEM((ff, features), bf16),
            pltpu.VMEM((rows, ff), f32),
            pltpu.VMEM((rows, ff), f32),
            pltpu.VMEM((rows, ff), bf16),
            pltpu.VMEM((rows, ff), bf16),
            pltpu.VMEM((rows, 1), f32),
            pltpu.VMEM((rows, features), bf16),
        ],
    }
    res = chunk_call(
        functools.partial(second_kernel, at, n, wholes[0] is not None), f"second_{at}",
        at, blocks, [gate, up], weight, w_at, ws, wholes, out_shapes, total, scratch,
        6 * rows * features * ff,
    )
    return res[:n], res[n], res[n + 1:]


def gathered_plan(tokens, routes, combine, cotangent, w_gate, w_up, w_down):
    tok_rows, features = tokens.shape
    groups = lax.axis_size("expert")
    me = lax.axis_index("expert")
    half = tok_rows // 2
    total = groups * tok_rows
    bf16 = jnp.bfloat16
    f32 = jnp.float32
    chosen = routes[:, :, None] == jnp.arange(groups, dtype=jnp.int32)[None, None, :]
    weights = jnp.sum(jnp.where(chosen, combine[:, :, None], 0.0), axis=1)
    sources = jnp.asarray(ring_sources(), jnp.int32)[me]
    ws = (w_gate[0], w_up[0], w_down[0])

    xf, xb = forward(tokens), backward(tokens)
    gf, gb = forward(cotangent), backward(cotangent)
    mine = jnp.arange(groups, dtype=jnp.int32)[None, :] == me
    own_weight = jnp.sum(jnp.where(mine, weights, 0.0), axis=1, keepdims=True)
    arrived = lax.all_to_all(weights.T, "expert", split_axis=0, concat_axis=0, tiled=True)
    weight = arrived[sources].reshape(total, 1)

    outs, backs, combs = [], [], []
    firsts, seconds = (None, None), (None, None, None)
    at = 0
    xs, gs = [tokens], [cotangent]
    for step in range(5):
        w = own_weight if step == 0 else weight
        out, gate, up, firsts = first_half(at, xs, w, at, ws, firsts, total)
        outs.append(out)
        if step == 4:
            o = (forward(out[0]), backward(out[1]))
        gf, gb, gate, *firsts = tie(gf, gb, gate, *firsts)
        if step > 0:
            gs = [hold_gf, hold_gb]
        if step < 4:
            hold_gf, hold_gb = gf, gb
        if step < 2:
            gf, gb = forward(gf), backward(gb)
        elif step == 2:
            gf, gb = forward(gf[:half]), backward(gb[half:])
        back, comb, seconds = second_half(at, gs, gate, up, w, at, ws, seconds, total)
        backs.append(back)
        combs.append(comb)
        at += len(xs) * xs[0].shape[0]
        if step == 4:
            break
        xf, xb, *seconds = tie(xf, xb, *seconds)
        xs = [xf, xb]
        if step < 2:
            xf, xb = forward(xf), backward(xb)
        elif step == 2:
            xf, xb = forward(xf[:half]), backward(xb[half:])

    all_x, scaled = firsts
    all_g, d_gate, d_up = seconds

    def advance(step, parts, got):
        behind, ahead = parts[4 - step]
        f, b = got
        if step == 1:
            f = lax.dynamic_update_slice(ahead, add_rounded(ahead[:half], f), (0, 0))
            b = lax.dynamic_update_slice(behind, add_rounded(behind[half:], b), (half, 0))
            return forward(f), backward(b)
        return forward(add_rounded(ahead, f)), backward(add_rounded(behind, b))

    def finish(parts, got):
        (own,) = parts[0]
        return (own.astype(f32) + got[0].astype(f32) + got[1].astype(f32)).astype(bf16)

    t = (forward(backs[4][0]), backward(backs[4][1]))
    away_d, kept_d = gradient(all_g, scaled, "grad_down", False)
    got_d = core_swap(away_d)
    *o, kept_d = tie(*o, kept_d)
    o = advance(1, outs, o)
    *t, d_gate, comb_last = tie(*t, d_gate, combs[-1])
    t = advance(1, backs, t)
    away_g, kept_g = gradient(all_x, d_gate, "grad_gate", True)
    got_g = core_swap(away_g)
    got_d, kept_g, comb_last = tie(got_d, kept_g, comb_last)
    last_d = y_swap(kept_d, got_d)
    d_comb = jnp.concatenate(combs[:-1] + [comb_last], axis=0).reshape(groups, tok_rows)
    table = ring_sources()
    inverse = jnp.asarray([[row.index(e) for e in range(groups)] for row in table], jnp.int32)[me]
    *o, d_up = tie(*o, d_up)
    o = advance(2, outs, o)
    away_u, kept_u = gradient(all_x, d_up, "grad_up", True)
    got_u = core_swap(away_u)
    *t, kept_u, got_g, d_comb = tie(*t, kept_u, got_g, d_comb)
    t = advance(2, backs, t)
    last_g = y_swap(kept_g, got_g)
    back = lax.all_to_all(d_comb[inverse], "expert", split_axis=0, concat_axis=0, tiled=True)
    *o, got_u = tie(*o, got_u)
    o = advance(3, outs, o)
    last_u = y_swap(kept_u, got_u)
    *t, last_d = tie(*t, last_d)
    t = advance(3, backs, t)
    d_w_down = dp_total(kept_d, got_d, last_d)
    output = finish(outs, o)
    d_w_gate = dp_total(kept_g, got_g, last_g)
    d_tokens = finish(backs, t)
    d_w_up = dp_total(kept_u, got_u, last_u)
    d_combine = jnp.sum(jnp.where(chosen, back.T[:, None, :], 0.0), axis=2)
    return output, d_tokens, d_combine, d_w_gate, d_w_up, d_w_down


def solution(mesh):
    rows = P(("dp", "expert"), None)
    small = mesh.shape["expert"] == len(RING) and mesh.shape["dp"] == 4
    return jax.shard_map(
        gathered_plan if small else routed_plan,
        mesh=mesh,
        in_specs=(rows, rows, rows, rows) + (P("expert", None, None),) * 3,
        out_specs=(
            rows,
            rows,
            rows,
            P("expert", "dp", None),
            P("expert", "dp", None),
            P("expert", None, "dp"),
        ),
        check_vma=False,
    )
```

```python
import functools
import jax
import jax.numpy as jnp
from jax import lax
from jax.experimental import pallas as pl
from jax.experimental.pallas import tpu as pltpu
from jax.sharding import PartitionSpec as P


def slot_map(routes, experts, capacity):
    flat_ids = routes.reshape(-1)
    onehot = (flat_ids[:, None] == jnp.arange(experts, dtype=jnp.int32)[None, :]).astype(jnp.int32)
    before = jnp.cumsum(onehot, axis=0) - onehot
    slots = jnp.sum(before * onehot, axis=1)
    target = flat_ids * capacity + slots
    source = (
        jnp.full((experts * capacity,), -1, jnp.int32)
        .at[target]
        .set(jnp.arange(flat_ids.shape[0], dtype=jnp.int32))
    )
    return (target, source)


def routed_plan(tokens, routes, combine, cotangent, w_gate, w_up, w_down):
    tok_rows, features = tokens.shape
    per_token = routes.shape[1]
    groups = lax.axis_size("expert")
    local_exp = w_gate.shape[0]
    experts = local_exp * groups
    capacity = 3 * tok_rows * per_token // (2 * experts)
    target, source = slot_map(routes, experts, capacity)
    filled = (source >= 0)[:, None]
    pair_index = jnp.maximum(source, 0)
    owner_row = pair_index // per_token
    outgoing = jnp.where(filled, tokens[owner_row], jnp.zeros((), jnp.bfloat16))
    outgoing = outgoing.reshape(groups, local_exp, capacity, features)
    cot_float = cotangent.astype(jnp.float32)
    scaled = (combine[:, :, None] * cot_float[:, None, :]).reshape(tok_rows * per_token, features)
    outgoing_grad = jnp.where(filled, scaled[pair_index], 0.0).astype(jnp.bfloat16)
    outgoing_grad = outgoing_grad.reshape(groups, local_exp, capacity, features)
    arrived = lax.all_to_all(outgoing, "expert", split_axis=0, concat_axis=0, tiled=True)
    gate_pre = jnp.einsum("secd,edf->secf", arrived, w_gate, preferred_element_type=jnp.float32)
    up_pre = jnp.einsum("secd,edf->secf", arrived, w_up, preferred_element_type=jnp.float32)
    activated = jax.nn.silu(gate_pre)
    hidden = (activated * up_pre).astype(jnp.bfloat16)
    produced = jnp.einsum(
        "secf,efd->secd", hidden, w_down, preferred_element_type=jnp.float32
    ).astype(jnp.bfloat16)
    returned = lax.all_to_all(produced, "expert", split_axis=0, concat_axis=0, tiled=True)
    d_in = lax.all_to_all(outgoing_grad, "expert", split_axis=0, concat_axis=0, tiled=True)
    d_hidden = jnp.einsum("secd,efd->secf", d_in, w_down, preferred_element_type=jnp.float32)
    part_down = jnp.einsum("secf,secd->efd", hidden, d_in, preferred_element_type=jnp.float32)
    sigmoid_g = jax.nn.sigmoid(gate_pre)
    d_gate = (d_hidden * up_pre * sigmoid_g * (1.0 + gate_pre * (1.0 - sigmoid_g))).astype(
        jnp.bfloat16
    )
    d_up = (d_hidden * activated).astype(jnp.bfloat16)
    part_gate = jnp.einsum("secd,secf->edf", arrived, d_gate, preferred_element_type=jnp.float32)
    part_up = jnp.einsum("secd,secf->edf", arrived, d_up, preferred_element_type=jnp.float32)
    d_rows = (
        jnp.einsum("secf,edf->secd", d_gate, w_gate, preferred_element_type=jnp.float32)
        + jnp.einsum("secf,edf->secd", d_up, w_up, preferred_element_type=jnp.float32)
    ).astype(jnp.bfloat16)
    back = lax.all_to_all(d_rows, "expert", split_axis=0, concat_axis=0, tiled=True)
    per_slot = returned.reshape(experts * capacity, features)[target]
    per_slot = per_slot.reshape(tok_rows, per_token, features).astype(jnp.float32)
    output = jnp.sum(combine[:, :, None] * per_slot, axis=1).astype(jnp.bfloat16)
    d_combine = jnp.sum(per_slot * cot_float[:, None, :], axis=2)
    back_slot = back.reshape(experts * capacity, features)[target]
    back_slot = back_slot.reshape(tok_rows, per_token, features).astype(jnp.float32)
    d_tokens = jnp.sum(back_slot, axis=1).astype(jnp.bfloat16)
    sum_gate, sum_up, sum_down = (
        lax.psum_scatter(
            part_gate.astype(jnp.bfloat16), "dp", scatter_dimension=1, tiled=True
        ).astype(jnp.float32),
        lax.psum_scatter(
            part_up.astype(jnp.bfloat16), "dp", scatter_dimension=1, tiled=True
        ).astype(jnp.float32),
        lax.psum_scatter(
            part_down.astype(jnp.bfloat16), "dp", scatter_dimension=2, tiled=True
        ).astype(jnp.float32),
    )
    d_w_down = sum_down.astype(jnp.bfloat16)
    return (
        output,
        d_tokens,
        d_combine,
        sum_gate.astype(jnp.bfloat16),
        sum_up.astype(jnp.bfloat16),
        d_w_down,
    )


RING = (0, 1, 3, 5, 7, 6, 4, 2)


def ring_perms():
    n = len(RING)
    fwd = [(RING[i], RING[(i + 1) % n]) for i in range(n)]
    bwd = [(RING[(i + 1) % n], RING[i]) for i in range(n)]
    return fwd, bwd


def ring_sources():
    n = len(RING)
    place = {e: i for i, e in enumerate(RING)}
    steps = (0, -1, 1, -2, 2, -3, 3, 4)
    return [[RING[(place[e] + r) % n] for r in steps] for e in range(n)]


def forward(value):
    return lax.ppermute(value, "expert", ring_perms()[0])


def backward(value):
    return lax.ppermute(value, "expert", ring_perms()[1])


def tie(*values):
    return lax.optimization_barrier(values)


def add_rounded(a, b):
    return (a.astype(jnp.float32) + b.astype(jnp.float32)).astype(jnp.bfloat16)


def core_swap(away):
    n = lax.axis_size("dp")
    return lax.ppermute(away, "dp", [(j, j ^ 1) for j in range(n)])


def pick(halves, y):
    return lax.dynamic_index_in_dim(halves, y, 0, keepdims=False)


def y_swap(kept, got):
    n = lax.axis_size("dp")
    y = lax.axis_index("dp") // 2
    other = add_rounded(pick(kept, 1 - y), pick(got, 1 - y))
    return lax.ppermute(other, "dp", [(j, j ^ 2) for j in range(n)])


ANY = pl.BlockSpec(memory_space=pl.ANY)


class Mover:
    def __init__(self, sems):
        self.sems = sems
        self.used = 0

    def go(self, src, dst):
        copy = pltpu.make_async_copy(src, dst, self.sems.at[self.used])
        self.used += 1
        copy.start()
        return copy


def gradient_kernel(spots, n_narrow, core, *refs):
    n = len(spots)
    wide, refs = refs[:n], refs[n:]
    narrow, refs = [refs[i * n:(i + 1) * n] for i in range(n_narrow)], refs[n_narrow * n:]
    away, kept, xs, sv, st, ov, sems = refs
    quarters, _, size = xs.shape
    ff = sv.shape[2]
    move = Mover(sems)
    load_s = [
        [move.go(r, sv.at[k, pl.ds(at, r.shape[0])]) for r, at in zip(narrow[k], spots)]
        for k in range(n_narrow)
    ]
    load_x = []
    for i in range(quarters):
        c = core[0] if i >= quarters // 2 else 1 - core[0]
        first = pl.multiple_of(((i % (quarters // 2)) * 2 + c) * size, size)
        load_x.append([
            move.go(r.at[:, pl.ds(first, size)], xs.at[i, pl.ds(at, r.shape[0])])
            for r, at in zip(wide, spots)
        ])
    for k in range(n_narrow):
        for c in load_s[k]:
            c.wait()
        for f in range(0, ff, 256):
            st[k * ff + f:k * ff + f + 256, :] = sv[k, :, f:f + 256].T
    stores = []
    for i in range(quarters):
        for c in load_x[i]:
            c.wait()
        for f in range(0, n_narrow * ff, 256):
            ov[i, f:f + 256, :] = jnp.dot(
                st[f:f + 256, :], xs[i], preferred_element_type=jnp.float32
            ).astype(jnp.bfloat16)
        half = quarters // 2
        stores.append(move.go(ov.at[i], away.at[i] if i < half else kept.at[i - half]))
    for c in stores:
        c.wait()


def gradient(wide, narrows, name):
    n_dp = lax.axis_size("dp")
    spots, at = [], 0
    for x in wide:
        spots.append(at)
        at += x.shape[0]
    features, ff = wide[0].shape[1], narrows[0][0].shape[1]
    size, tall = features // n_dp, len(narrows) * ff
    half = jax.ShapeDtypeStruct((n_dp // 2, tall, size), jnp.bfloat16)
    core = (lax.axis_index("dp") % 2).reshape(1)
    flat = [r for rows in narrows for r in rows]
    return pl.pallas_call(
        functools.partial(gradient_kernel, tuple(spots), len(narrows)),
        out_shape=[half, half],
        in_specs=[pl.BlockSpec(memory_space=pltpu.SMEM)] + [ANY] * (len(wide) + len(flat)),
        out_specs=[ANY, ANY],
        scratch_shapes=[
            pltpu.VMEM((n_dp, at, size), jnp.bfloat16),
            pltpu.VMEM((len(narrows), at, ff), jnp.bfloat16),
            pltpu.VMEM((tall, at), jnp.bfloat16),
            pltpu.VMEM((n_dp, tall, size), jnp.bfloat16),
            pltpu.SemaphoreType.DMA(((len(narrows) + n_dp) * len(wide) + n_dp,)),
        ],
        compiler_params=pltpu.CompilerParams(vmem_limit_bytes=30 * 1024 * 1024),
        cost_estimate=pl.CostEstimate(
            flops=2 * at * features * tall, bytes_accessed=6_000_000, transcendentals=0
        ),
        name=name,
    )(core, *wide, *flat)


def last_add_kernel(turned, y, kept, got, last, out):
    total = kept[0].astype(jnp.float32) + got[0].astype(jnp.float32) + last[...].astype(jnp.float32)
    out[...] = (total.T if turned else total).astype(jnp.bfloat16)[None]


def last_add(kept, got, last, row, ff, turned, name):
    size = kept.shape[2]
    y = (lax.axis_index("dp") // 2).reshape(1)
    shape = (1, size, ff) if turned else (1, ff, size)
    half = pl.BlockSpec((1, ff, size), lambda i, y: (y[0], row, 0))
    return pl.pallas_call(
        functools.partial(last_add_kernel, turned),
        out_shape=jax.ShapeDtypeStruct(shape, jnp.bfloat16),
        grid_spec=pltpu.PrefetchScalarGridSpec(
            num_scalar_prefetch=1,
            grid=(1,),
            in_specs=[half, half, pl.BlockSpec((ff, size), lambda i, y: (row, 0))],
            out_specs=pl.BlockSpec(shape, lambda i, y: (0, 0, 0)),
        ),
        compiler_params=pltpu.CompilerParams(vmem_limit_bytes=24 * 1024 * 1024),
        cost_estimate=pl.CostEstimate(flops=0, bytes_accessed=3_000_000, transcendentals=0),
        name=name,
    )(y, kept, got, last)


def gathered_plan(tokens, routes, combine, cotangent, w_gate, w_up, w_down):
    tok_rows, features = tokens.shape
    groups = lax.axis_size("expert")
    me = lax.axis_index("expert")
    half = tok_rows // 2
    bf16 = jnp.bfloat16
    f32 = jnp.float32
    chosen = routes[:, :, None] == jnp.arange(groups, dtype=jnp.int32)[None, None, :]
    weights = jnp.sum(jnp.where(chosen, combine[:, :, None], 0.0), axis=1)
    sources = jnp.asarray(ring_sources(), jnp.int32)[me]
    wg, wu, wd = w_gate[0], w_up[0], w_down[0]
    ff = wg.shape[1]

    def first_half(x, weight):
        gate = jnp.dot(x, wg, preferred_element_type=f32)
        up = jnp.dot(x, wu, preferred_element_type=f32)
        scaled = (gate * jax.nn.sigmoid(gate) * up * weight).astype(bf16)
        out = jnp.dot(scaled, wd, preferred_element_type=f32).astype(bf16)
        return gate, up, scaled, out

    def second_half(g, gate, up, weight):
        d_raw = jnp.einsum("td,fd->tf", g, wd, preferred_element_type=f32)
        sig = jax.nn.sigmoid(gate)
        act = gate * sig
        d_comb = jnp.sum(act * up * d_raw, axis=1)
        d_hidden = d_raw * weight
        d_gate = (d_hidden * up * sig * (1.0 + gate * (1.0 - sig))).astype(bf16)
        d_up = (d_hidden * act).astype(bf16)
        d_rows = (
            jnp.einsum("tf,df->td", d_gate, wg, preferred_element_type=f32)
            + jnp.einsum("tf,df->td", d_up, wu, preferred_element_type=f32)
        ).astype(bf16)
        return d_gate, d_up, d_rows, d_comb

    xf, xb = forward(tokens), backward(tokens)
    gf, gb = forward(cotangent), backward(cotangent)
    mine = jnp.arange(groups, dtype=jnp.int32)[None, :] == me
    own_weight = jnp.sum(jnp.where(mine, weights, 0.0), axis=1, keepdims=True)
    arrived = lax.all_to_all(weights.T, "expert", split_axis=0, concat_axis=0, tiled=True)
    weight = arrived[sources]

    all_x, all_g, firsts, seconds = [], [], [], []
    xs, gs = [tokens], [cotangent]
    for step in range(5):
        if step == 0:
            ws = [own_weight]
        elif step < 4:
            ws = [weight[2 * step - 1][:, None], weight[2 * step][:, None]]
        else:
            xs = [jnp.concatenate(xs, axis=0)]
            ws = [weight[7][:, None]]
        ones = [first_half(x, w) for x, w in zip(xs, ws)]
        if step == 4:
            far = ones[0][3]
            o = (forward(far[:half]), backward(far[half:]))
        gf, gb, *flat = tie(gf, gb, *[v for one in ones for v in one])
        ones = [tuple(flat[4 * i:4 * i + 4]) for i in range(len(ones))]
        if step > 0:
            gs = [hold_gf, hold_gb]
            if step == 4:
                gs = [jnp.concatenate(gs, axis=0)]
        if step < 4:
            hold_gf, hold_gb = gf, gb
        if step < 2:
            gf, gb = forward(gf), backward(gb)
        elif step == 2:
            gf, gb = forward(gf[:half]), backward(gb[half:])
        twos = [second_half(g, one[0], one[1], w) for g, one, w in zip(gs, ones, ws)]
        all_x += xs
        all_g += gs
        firsts += ones
        if step == 4:
            seconds += twos
            break
        xf, xb, *flat = tie(xf, xb, *[v for two in twos for v in two])
        seconds += [tuple(flat[4 * i:4 * i + 4]) for i in range(len(twos))]
        xs = [xf, xb]
        if step < 2:
            xf, xb = forward(xf), backward(xb)
        elif step == 2:
            xf, xb = forward(xf[:half]), backward(xb[half:])

    outs = [one[3] for one in firsts]
    backs = [two[2] for two in seconds]
    scaled = [one[2] for one in firsts]
    d_gate = [two[0] for two in seconds]
    d_up = [two[1] for two in seconds]

    def advance(step, parts, got):
        behind, ahead = parts[7 - 2 * step], parts[8 - 2 * step]
        f, b = got
        if step == 1:
            f = lax.dynamic_update_slice(ahead, add_rounded(ahead[:half], f), (0, 0))
            b = lax.dynamic_update_slice(behind, add_rounded(behind[half:], b), (half, 0))
            return forward(f), backward(b)
        return forward(add_rounded(ahead, f)), backward(add_rounded(behind, b))

    def finish(parts, got):
        return (parts[0].astype(f32) + got[0].astype(f32) + got[1].astype(f32)).astype(bf16)

    t = (forward(backs[7][:half]), backward(backs[7][half:]))
    away_d, kept_d = gradient(all_g, [scaled], "grad_down")
    got_d = core_swap(away_d)
    *o, kept_d = tie(*o, kept_d)
    o = advance(1, outs, o)
    *t, last_gate = tie(*t, d_gate[-1])
    t = advance(1, backs, t)
    away_u, kept_u = gradient(all_x, [d_gate[:-1] + [last_gate], d_up], "grad_gate_up")
    got_u = core_swap(away_u)
    *o, got_d = tie(*o, got_d)
    o = advance(2, outs, o)
    last_d = y_swap(kept_d, got_d)
    *t, kept_u = tie(*t, kept_u)
    t = advance(2, backs, t)
    *o, got_u = tie(*o, got_u)
    o = advance(3, outs, o)
    last_u = y_swap(kept_u, got_u)
    *t, last_comb = tie(*t, seconds[-1][3])
    t = advance(3, backs, t)
    d_comb = jnp.stack([two[3] for two in seconds[:-1]] + [last_comb])
    table = ring_sources()
    inverse = jnp.asarray([[row.index(e) for e in range(groups)] for row in table], jnp.int32)[me]
    back = lax.all_to_all(d_comb[inverse], "expert", split_axis=0, concat_axis=0, tiled=True)
    d_w_down = last_add(kept_d, got_d, last_d, 0, ff, False, "sum_down")
    output = finish(outs, o)
    d_tokens = finish(backs, t)
    d_w_gate = last_add(kept_u, got_u, last_u, 0, ff, True, "sum_gate")
    d_w_up = last_add(kept_u, got_u, last_u, 1, ff, True, "sum_up")
    d_combine = jnp.sum(jnp.where(chosen, back.T[:, None, :], 0.0), axis=2)
    return output, d_tokens, d_combine, d_w_gate, d_w_up, d_w_down


def solution(mesh):
    rows = P(("dp", "expert"), None)
    small = mesh.shape["expert"] == len(RING) and mesh.shape["dp"] == 4
    return jax.shard_map(
        gathered_plan if small else routed_plan,
        mesh=mesh,
        in_specs=(rows, rows, rows, rows) + (P("expert", None, None),) * 3,
        out_specs=(
            rows,
            rows,
            rows,
            P("expert", "dp", None),
            P("expert", "dp", None),
            P("expert", None, "dp"),
        ),
        check_vma=False,
    )
```

```python
import functools
import jax
import jax.numpy as jnp
from jax import lax
from jax.experimental import pallas as pl
from jax.experimental.pallas import tpu as pltpu
from jax.sharding import PartitionSpec as P


def slot_map(routes, experts, capacity):
    flat_ids = routes.reshape(-1)
    onehot = (flat_ids[:, None] == jnp.arange(experts, dtype=jnp.int32)[None, :]).astype(jnp.int32)
    before = jnp.cumsum(onehot, axis=0) - onehot
    slots = jnp.sum(before * onehot, axis=1)
    target = flat_ids * capacity + slots
    source = (
        jnp.full((experts * capacity,), -1, jnp.int32)
        .at[target]
        .set(jnp.arange(flat_ids.shape[0], dtype=jnp.int32))
    )
    return (target, source)


def routed_plan(tokens, routes, combine, cotangent, w_gate, w_up, w_down):
    tok_rows, features = tokens.shape
    per_token = routes.shape[1]
    groups = lax.axis_size("expert")
    local_exp = w_gate.shape[0]
    experts = local_exp * groups
    capacity = 3 * tok_rows * per_token // (2 * experts)
    target, source = slot_map(routes, experts, capacity)
    filled = (source >= 0)[:, None]
    pair_index = jnp.maximum(source, 0)
    owner_row = pair_index // per_token
    outgoing = jnp.where(filled, tokens[owner_row], jnp.zeros((), jnp.bfloat16))
    outgoing = outgoing.reshape(groups, local_exp, capacity, features)
    cot_float = cotangent.astype(jnp.float32)
    scaled = (combine[:, :, None] * cot_float[:, None, :]).reshape(tok_rows * per_token, features)
    outgoing_grad = jnp.where(filled, scaled[pair_index], 0.0).astype(jnp.bfloat16)
    outgoing_grad = outgoing_grad.reshape(groups, local_exp, capacity, features)
    arrived = lax.all_to_all(outgoing, "expert", split_axis=0, concat_axis=0, tiled=True)
    gate_pre = jnp.einsum("secd,edf->secf", arrived, w_gate, preferred_element_type=jnp.float32)
    up_pre = jnp.einsum("secd,edf->secf", arrived, w_up, preferred_element_type=jnp.float32)
    activated = jax.nn.silu(gate_pre)
    hidden = (activated * up_pre).astype(jnp.bfloat16)
    produced = jnp.einsum(
        "secf,efd->secd", hidden, w_down, preferred_element_type=jnp.float32
    ).astype(jnp.bfloat16)
    returned = lax.all_to_all(produced, "expert", split_axis=0, concat_axis=0, tiled=True)
    d_in = lax.all_to_all(outgoing_grad, "expert", split_axis=0, concat_axis=0, tiled=True)
    d_hidden = jnp.einsum("secd,efd->secf", d_in, w_down, preferred_element_type=jnp.float32)
    part_down = jnp.einsum("secf,secd->efd", hidden, d_in, preferred_element_type=jnp.float32)
    sigmoid_g = jax.nn.sigmoid(gate_pre)
    d_gate = (d_hidden * up_pre * sigmoid_g * (1.0 + gate_pre * (1.0 - sigmoid_g))).astype(
        jnp.bfloat16
    )
    d_up = (d_hidden * activated).astype(jnp.bfloat16)
    part_gate = jnp.einsum("secd,secf->edf", arrived, d_gate, preferred_element_type=jnp.float32)
    part_up = jnp.einsum("secd,secf->edf", arrived, d_up, preferred_element_type=jnp.float32)
    d_rows = (
        jnp.einsum("secf,edf->secd", d_gate, w_gate, preferred_element_type=jnp.float32)
        + jnp.einsum("secf,edf->secd", d_up, w_up, preferred_element_type=jnp.float32)
    ).astype(jnp.bfloat16)
    back = lax.all_to_all(d_rows, "expert", split_axis=0, concat_axis=0, tiled=True)
    per_slot = returned.reshape(experts * capacity, features)[target]
    per_slot = per_slot.reshape(tok_rows, per_token, features).astype(jnp.float32)
    output = jnp.sum(combine[:, :, None] * per_slot, axis=1).astype(jnp.bfloat16)
    d_combine = jnp.sum(per_slot * cot_float[:, None, :], axis=2)
    back_slot = back.reshape(experts * capacity, features)[target]
    back_slot = back_slot.reshape(tok_rows, per_token, features).astype(jnp.float32)
    d_tokens = jnp.sum(back_slot, axis=1).astype(jnp.bfloat16)
    sum_gate, sum_up, sum_down = (
        lax.psum_scatter(
            part_gate.astype(jnp.bfloat16), "dp", scatter_dimension=1, tiled=True
        ).astype(jnp.float32),
        lax.psum_scatter(
            part_up.astype(jnp.bfloat16), "dp", scatter_dimension=1, tiled=True
        ).astype(jnp.float32),
        lax.psum_scatter(
            part_down.astype(jnp.bfloat16), "dp", scatter_dimension=2, tiled=True
        ).astype(jnp.float32),
    )
    d_w_down = sum_down.astype(jnp.bfloat16)
    return (
        output,
        d_tokens,
        d_combine,
        sum_gate.astype(jnp.bfloat16),
        sum_up.astype(jnp.bfloat16),
        d_w_down,
    )


RING = (0, 1, 3, 5, 7, 6, 4, 2)


def ring_perms():
    n = len(RING)
    fwd = [(RING[i], RING[(i + 1) % n]) for i in range(n)]
    bwd = [(RING[(i + 1) % n], RING[i]) for i in range(n)]
    return fwd, bwd


def ring_sources():
    n = len(RING)
    place = {e: i for i, e in enumerate(RING)}
    steps = (0, -1, 1, -2, 2, -3, 3, 4)
    return [[RING[(place[e] + r) % n] for r in steps] for e in range(n)]


def forward(value):
    return lax.ppermute(value, "expert", ring_perms()[0])


def backward(value):
    return lax.ppermute(value, "expert", ring_perms()[1])


def tie(*values):
    return lax.optimization_barrier(values)


def add_rounded(a, b):
    return (a.astype(jnp.float32) + b.astype(jnp.float32)).astype(jnp.bfloat16)


def core_swap(away):
    n = lax.axis_size("dp")
    return lax.ppermute(away, "dp", [(j, j ^ 1) for j in range(n)])


def pick(halves, y):
    return lax.dynamic_index_in_dim(halves, y, 0, keepdims=False)


def y_part(kept, got):
    y = lax.axis_index("dp") // 2
    return add_rounded(pick(kept, 1 - y), pick(got, 1 - y))


def y_swap(other):
    n = lax.axis_size("dp")
    return lax.ppermute(other, "dp", [(j, j ^ 2) for j in range(n)])


ANY = pl.BlockSpec(memory_space=pl.ANY)


class Mover:
    def __init__(self, sems):
        self.sems = sems
        self.used = 0

    def go(self, src, dst):
        copy = pltpu.make_async_copy(src, dst, self.sems.at[self.used])
        self.used += 1
        copy.start()
        return copy


def gradient_kernel(which, spots, core, *refs):
    n = len(spots)
    wide, refs = refs[:n], refs[n:]
    m = len(refs) - 7
    narrow, refs = refs[:m], refs[m:]
    away, kept, xs, sv, st, ov, sems = refs
    quarters, _, size = xs.shape
    ff = sv.shape[1]
    move = Mover(sems)
    load_s, load_x, at = [], [], 0
    for r in narrow:
        load_s.append(move.go(r, sv.at[pl.ds(at, r.shape[0])]))
        at += r.shape[0]
    for i in range(quarters):
        c = core[0] if i >= quarters // 2 else 1 - core[0]
        first = pl.multiple_of(((i % (quarters // 2)) * 2 + c) * size, size)
        load_x.append([
            move.go(r.at[which, :, pl.ds(first, size)], xs.at[i, pl.ds(at, r.shape[1])])
            for r, at in zip(wide, spots)
        ])
    for c in load_s:
        c.wait()
    for f in range(0, ff, 256):
        st[f:f + 256, :] = sv[:, f:f + 256].T
    stores = []
    for i in range(quarters):
        for c in load_x[i]:
            c.wait()
        for f in range(0, ff, 256):
            ov[i, f:f + 256, :] = jnp.dot(
                st[f:f + 256, :], xs[i], preferred_element_type=jnp.float32
            ).astype(jnp.bfloat16)
        half = quarters // 2
        stores.append(move.go(ov.at[i], away.at[i] if i < half else kept.at[i - half]))
    for c in stores:
        c.wait()


FREE = pl.CostEstimate(flops=0, bytes_accessed=0, transcendentals=0)


def gradient(wide, which, narrow, name):
    n_dp = lax.axis_size("dp")
    spots, at = [], 0
    for x in wide:
        spots.append(at)
        at += x.shape[1]
    features, ff = wide[0].shape[2], narrow[0].shape[1]
    size = features // n_dp
    half = jax.ShapeDtypeStruct((n_dp // 2, ff, size), jnp.bfloat16)
    core = (lax.axis_index("dp") % 2).reshape(1)
    return pl.pallas_call(
        functools.partial(gradient_kernel, which, tuple(spots)),
        out_shape=[half, half],
        in_specs=[pl.BlockSpec(memory_space=pltpu.SMEM)] + [ANY] * (len(wide) + len(narrow)),
        out_specs=[ANY, ANY],
        scratch_shapes=[
            pltpu.VMEM((n_dp, at, size), jnp.bfloat16),
            pltpu.VMEM((at, ff), jnp.bfloat16),
            pltpu.VMEM((ff, at), jnp.bfloat16),
            pltpu.VMEM((n_dp, ff, size), jnp.bfloat16),
            pltpu.SemaphoreType.DMA((len(narrow) + n_dp * len(wide) + n_dp,)),
        ],
        compiler_params=pltpu.CompilerParams(vmem_limit_bytes=24 * 1024 * 1024),
        cost_estimate=FREE,
        name=name,
    )(core, *wide, *narrow)


def total_of(*values):
    total = values[0].astype(jnp.float32)
    for v in values[1:]:
        total = total + v.astype(jnp.float32)
    return total.astype(jnp.bfloat16)


def pack_kernel(far_o, far_t, f, b):
    half = f.shape[1]
    for i, far in enumerate((far_o, far_t)):
        f[i] = far[:half]
        b[i] = far[half:]


def step_kernel(behind_o, behind_t, ahead_o, ahead_t, got_f, got_b, f, b):
    rows, some = f.shape[1], got_f.shape[1]
    for i, (behind, ahead) in enumerate(((behind_o, ahead_o), (behind_t, ahead_t))):
        f[i, :some] = total_of(ahead[:some], got_f[i])
        b[i, rows - some:] = total_of(behind[rows - some:], got_b[i])
        if some < rows:
            f[i, some:] = ahead[some:]
            b[i, :rows - some] = behind[:rows - some]


def end_kernel(own_o, own_t, got_f, got_b, o, t):
    o[...] = total_of(own_o[...], got_f[0], got_b[0])
    t[...] = total_of(own_t[...], got_f[1], got_b[1])


def by_columns(kernel, operands, out_shapes, name):
    features = out_shapes[0][-1]

    def spec(shape):
        block = tuple(shape[:-1]) + (features // 4,)
        return pl.BlockSpec(block, lambda i, n=len(shape): (0,) * (n - 1) + (i,))

    return pl.pallas_call(
        kernel,
        out_shape=[jax.ShapeDtypeStruct(s, jnp.bfloat16) for s in out_shapes],
        grid=(4,),
        in_specs=[spec(v.shape) for v in operands],
        out_specs=[spec(s) for s in out_shapes],
        compiler_params=pltpu.CompilerParams(vmem_limit_bytes=16 * 1024 * 1024),
        cost_estimate=FREE,
        name=name,
    )(*operands)


def last_add_kernel(turned, y, kept, got, last, out):
    total = kept[0].astype(jnp.float32) + got[0].astype(jnp.float32) + last[...].astype(jnp.float32)
    out[...] = (total.T if turned else total).astype(jnp.bfloat16)[None]


def last_add(kept, got, last, row, ff, turned, name):
    size = kept.shape[2]
    y = (lax.axis_index("dp") // 2).reshape(1)
    shape = (1, size, ff) if turned else (1, ff, size)
    half = pl.BlockSpec((1, ff, size), lambda i, y: (y[0], row, 0))
    return pl.pallas_call(
        functools.partial(last_add_kernel, turned),
        out_shape=jax.ShapeDtypeStruct(shape, jnp.bfloat16),
        grid_spec=pltpu.PrefetchScalarGridSpec(
            num_scalar_prefetch=1,
            grid=(1,),
            in_specs=[half, half, pl.BlockSpec((ff, size), lambda i, y: (row, 0))],
            out_specs=pl.BlockSpec(shape, lambda i, y: (0, 0, 0)),
        ),
        compiler_params=pltpu.CompilerParams(vmem_limit_bytes=24 * 1024 * 1024),
        cost_estimate=FREE,
        name=name,
    )(y, kept, got, last)


def gathered_plan(tokens, routes, combine, cotangent, w_gate, w_up, w_down):
    tok_rows, features = tokens.shape
    groups = lax.axis_size("expert")
    me = lax.axis_index("expert")
    half = tok_rows // 2
    bf16 = jnp.bfloat16
    f32 = jnp.float32
    chosen = routes[:, :, None] == jnp.arange(groups, dtype=jnp.int32)[None, None, :]
    weights = jnp.sum(jnp.where(chosen, combine[:, :, None], 0.0), axis=1)
    sources = jnp.asarray(ring_sources(), jnp.int32)[me]
    wg, wu, wd = w_gate[0], w_up[0], w_down[0]
    ff = wg.shape[1]

    def first_half(x, weight):
        gate = jnp.dot(x, wg, preferred_element_type=f32)
        up = jnp.dot(x, wu, preferred_element_type=f32)
        scaled = (gate * jax.nn.sigmoid(gate) * up * weight).astype(bf16)
        out = jnp.dot(scaled, wd, preferred_element_type=f32).astype(bf16)
        return gate, up, scaled, out

    def second_half(g, gate, up, weight):
        d_raw = jnp.einsum("td,fd->tf", g, wd, preferred_element_type=f32)
        sig = jax.nn.sigmoid(gate)
        act = gate * sig
        d_comb = jnp.sum(act * up * d_raw, axis=1)
        d_hidden = d_raw * weight
        d_gate = (d_hidden * up * sig * (1.0 + gate * (1.0 - sig))).astype(bf16)
        d_up = (d_hidden * act).astype(bf16)
        d_rows = (
            jnp.einsum("tf,df->td", d_gate, wg, preferred_element_type=f32)
            + jnp.einsum("tf,df->td", d_up, wu, preferred_element_type=f32)
        ).astype(bf16)
        return d_gate, d_up, d_rows, d_comb

    mine = jnp.arange(groups, dtype=jnp.int32)[None, :] == me
    own_weight = jnp.sum(jnp.where(mine, weights, 0.0), axis=1, keepdims=True)

    wide, firsts, seconds = [], [], []
    both = jnp.stack([tokens, cotangent])
    f, b = both, both
    held = [both]
    for step in range(5):
        wide += held
        if step < 3:
            f, b = forward(f), backward(b)
        elif step == 3:
            f, b = forward(f[:, :half]), backward(b[:, half:])
        if step == 0:
            xs, gs, ws = [tokens], [cotangent], [own_weight]
            arrived = lax.all_to_all(weights.T, "expert", split_axis=0, concat_axis=0, tiled=True)
            weight = arrived[sources]
        elif step < 4:
            xs, gs = [v[0] for v in held], [v[1] for v in held]
            ws = [weight[2 * step - 1][:, None], weight[2 * step][:, None]]
        else:
            far = jnp.concatenate(held, axis=1)
            xs, gs, ws = [far[0]], [far[1]], [weight[7][:, None]]
        ones = [first_half(x, w) for x, w in zip(xs, ws)]
        twos = [second_half(g, one[0], one[1], w) for g, one, w in zip(gs, ones, ws)]
        n = len(ones)
        kept = [v for one in ones for v in one[2:]] + [v for two in twos for v in two]
        if step < 4:
            f, b, *kept = tie(f, b, *kept)
            held = [f, b]
        firsts += [kept[2 * i:2 * i + 2] for i in range(n)]
        seconds += [kept[2 * n + 4 * i:2 * n + 4 * i + 4] for i in range(n)]

    scaled, outs = [one[0] for one in firsts], [one[1] for one in firsts]
    d_gate, d_up = [two[0] for two in seconds], [two[1] for two in seconds]
    backs = [two[2] for two in seconds]
    combs = jnp.stack([two[3] for two in seconds])
    full, halves = (2, tok_rows, features), (2, half, features)

    def summed(step, got):
        behind, ahead = 7 - 2 * step, 8 - 2 * step
        operands = [outs[behind], backs[behind], outs[ahead], backs[ahead], *got]
        return by_columns(step_kernel, operands, [full, full], f"sum_step_{step}")

    f, b = by_columns(pack_kernel, [outs[7], backs[7]], [halves, halves], "sum_step_0")
    f, b, last_scaled = tie(f, b, scaled[-1])
    f, b = forward(f), backward(b)
    away_d, kept_d = gradient(wide, 1, scaled[:-1] + [last_scaled], "grad_down")
    f, b, away_d, d_gate[-1], d_up[-1] = tie(f, b, away_d, d_gate[-1], d_up[-1])

    got_d = core_swap(away_d)
    f, b = summed(1, (f, b))
    f, b = forward(f), backward(b)
    other_d = y_part(kept_d, got_d)
    other_d, d_gate[-1], d_up[-1] = tie(other_d, d_gate[-1], d_up[-1])
    last_d = y_swap(other_d)
    away_g, kept_g = gradient(wide, 0, d_gate, "grad_gate")
    away_u, kept_u = gradient(wide, 0, d_up, "grad_up")
    f, b, last_d, away_g, away_u, combs = tie(f, b, last_d, away_g, away_u, combs)

    got_g, got_u = core_swap(away_g), core_swap(away_u)
    f, b = summed(2, (f, b))
    f, b = forward(f), backward(b)
    last_g = y_swap(y_part(kept_g, got_g))
    table = ring_sources()
    inverse = jnp.asarray([[row.index(e) for e in range(groups)] for row in table], jnp.int32)[me]
    back = lax.all_to_all(combs[inverse], "expert", split_axis=0, concat_axis=0, tiled=True)
    f, b, last_g, got_u, last_d = tie(f, b, last_g, got_u, last_d)

    f, b = summed(3, (f, b))
    f, b, last_u = forward(f), backward(b), y_swap(y_part(kept_u, got_u))
    d_w_down = last_add(kept_d, got_d, last_d, 0, ff, False, "sum_down")
    d_w_gate = last_add(kept_g, got_g, last_g, 0, ff, True, "sum_gate")
    d_combine = jnp.sum(jnp.where(chosen, back.T[:, None, :], 0.0), axis=2)
    d_w_up = last_add(kept_u, got_u, last_u, 0, ff, True, "sum_up")
    output, d_tokens = by_columns(
        end_kernel, [outs[0], backs[0], f, b], [tokens.shape, tokens.shape], "sum_end"
    )
    return output, d_tokens, d_combine, d_w_gate, d_w_up, d_w_down


def solution(mesh):
    rows = P(("dp", "expert"), None)
    small = mesh.shape["expert"] == len(RING) and mesh.shape["dp"] == 4
    return jax.shard_map(
        gathered_plan if small else routed_plan,
        mesh=mesh,
        in_specs=(rows, rows, rows, rows) + (P("expert", None, None),) * 3,
        out_specs=(
            rows,
            rows,
            rows,
            P("expert", "dp", None),
            P("expert", "dp", None),
            P("expert", None, "dp"),
        ),
        check_vma=False,
    )
```

```python
import functools
import jax
import jax.numpy as jnp
from jax import lax
from jax.experimental import pallas as pl
from jax.experimental.pallas import tpu as pltpu
from jax.sharding import PartitionSpec as P


def slot_map(routes, experts, capacity):
    flat_ids = routes.reshape(-1)
    onehot = (flat_ids[:, None] == jnp.arange(experts, dtype=jnp.int32)[None, :]).astype(jnp.int32)
    before = jnp.cumsum(onehot, axis=0) - onehot
    slots = jnp.sum(before * onehot, axis=1)
    target = flat_ids * capacity + slots
    source = (
        jnp.full((experts * capacity,), -1, jnp.int32)
        .at[target]
        .set(jnp.arange(flat_ids.shape[0], dtype=jnp.int32))
    )
    return (target, source)


def routed_plan(tokens, routes, combine, cotangent, w_gate, w_up, w_down):
    tok_rows, features = tokens.shape
    per_token = routes.shape[1]
    groups = lax.axis_size("expert")
    local_exp = w_gate.shape[0]
    experts = local_exp * groups
    capacity = 3 * tok_rows * per_token // (2 * experts)
    target, source = slot_map(routes, experts, capacity)
    filled = (source >= 0)[:, None]
    pair_index = jnp.maximum(source, 0)
    owner_row = pair_index // per_token
    outgoing = jnp.where(filled, tokens[owner_row], jnp.zeros((), jnp.bfloat16))
    outgoing = outgoing.reshape(groups, local_exp, capacity, features)
    cot_float = cotangent.astype(jnp.float32)
    scaled = (combine[:, :, None] * cot_float[:, None, :]).reshape(tok_rows * per_token, features)
    outgoing_grad = jnp.where(filled, scaled[pair_index], 0.0).astype(jnp.bfloat16)
    outgoing_grad = outgoing_grad.reshape(groups, local_exp, capacity, features)
    arrived = lax.all_to_all(outgoing, "expert", split_axis=0, concat_axis=0, tiled=True)
    gate_pre = jnp.einsum("secd,edf->secf", arrived, w_gate, preferred_element_type=jnp.float32)
    up_pre = jnp.einsum("secd,edf->secf", arrived, w_up, preferred_element_type=jnp.float32)
    activated = jax.nn.silu(gate_pre)
    hidden = (activated * up_pre).astype(jnp.bfloat16)
    produced = jnp.einsum(
        "secf,efd->secd", hidden, w_down, preferred_element_type=jnp.float32
    ).astype(jnp.bfloat16)
    returned = lax.all_to_all(produced, "expert", split_axis=0, concat_axis=0, tiled=True)
    d_in = lax.all_to_all(outgoing_grad, "expert", split_axis=0, concat_axis=0, tiled=True)
    d_hidden = jnp.einsum("secd,efd->secf", d_in, w_down, preferred_element_type=jnp.float32)
    part_down = jnp.einsum("secf,secd->efd", hidden, d_in, preferred_element_type=jnp.float32)
    sigmoid_g = jax.nn.sigmoid(gate_pre)
    d_gate = (d_hidden * up_pre * sigmoid_g * (1.0 + gate_pre * (1.0 - sigmoid_g))).astype(
        jnp.bfloat16
    )
    d_up = (d_hidden * activated).astype(jnp.bfloat16)
    part_gate = jnp.einsum("secd,secf->edf", arrived, d_gate, preferred_element_type=jnp.float32)
    part_up = jnp.einsum("secd,secf->edf", arrived, d_up, preferred_element_type=jnp.float32)
    d_rows = (
        jnp.einsum("secf,edf->secd", d_gate, w_gate, preferred_element_type=jnp.float32)
        + jnp.einsum("secf,edf->secd", d_up, w_up, preferred_element_type=jnp.float32)
    ).astype(jnp.bfloat16)
    back = lax.all_to_all(d_rows, "expert", split_axis=0, concat_axis=0, tiled=True)
    per_slot = returned.reshape(experts * capacity, features)[target]
    per_slot = per_slot.reshape(tok_rows, per_token, features).astype(jnp.float32)
    output = jnp.sum(combine[:, :, None] * per_slot, axis=1).astype(jnp.bfloat16)
    d_combine = jnp.sum(per_slot * cot_float[:, None, :], axis=2)
    back_slot = back.reshape(experts * capacity, features)[target]
    back_slot = back_slot.reshape(tok_rows, per_token, features).astype(jnp.float32)
    d_tokens = jnp.sum(back_slot, axis=1).astype(jnp.bfloat16)
    sum_gate, sum_up, sum_down = (
        lax.psum_scatter(
            part_gate.astype(jnp.bfloat16), "dp", scatter_dimension=1, tiled=True
        ).astype(jnp.float32),
        lax.psum_scatter(
            part_up.astype(jnp.bfloat16), "dp", scatter_dimension=1, tiled=True
        ).astype(jnp.float32),
        lax.psum_scatter(
            part_down.astype(jnp.bfloat16), "dp", scatter_dimension=2, tiled=True
        ).astype(jnp.float32),
    )
    d_w_down = sum_down.astype(jnp.bfloat16)
    return (
        output,
        d_tokens,
        d_combine,
        sum_gate.astype(jnp.bfloat16),
        sum_up.astype(jnp.bfloat16),
        d_w_down,
    )


RING = (0, 1, 3, 5, 7, 6, 4, 2)


def ring_perms():
    n = len(RING)
    fwd = [(RING[i], RING[(i + 1) % n]) for i in range(n)]
    bwd = [(RING[(i + 1) % n], RING[i]) for i in range(n)]
    return fwd, bwd


def ring_sources():
    n = len(RING)
    place = {e: i for i, e in enumerate(RING)}
    steps = (0, -1, 1, -2, 2, -3, 3, 4)
    return [[RING[(place[e] + r) % n] for r in steps] for e in range(n)]


def forward(value):
    return lax.ppermute(value, "expert", ring_perms()[0])


def backward(value):
    return lax.ppermute(value, "expert", ring_perms()[1])


def tie(*values):
    return lax.optimization_barrier(values)


def add_rounded(a, b):
    return (a.astype(jnp.float32) + b.astype(jnp.float32)).astype(jnp.bfloat16)


def core_swap(away):
    n = lax.axis_size("dp")
    return lax.ppermute(away, "dp", [(j, j ^ 1) for j in range(n)])


def pick(halves, y):
    return lax.dynamic_index_in_dim(halves, y, 0, keepdims=False)


def y_part(kept, got):
    y = lax.axis_index("dp") // 2
    return add_rounded(pick(kept, 1 - y), pick(got, 1 - y))


def y_swap(other):
    n = lax.axis_size("dp")
    return lax.ppermute(other, "dp", [(j, j ^ 2) for j in range(n)])


ANY = pl.BlockSpec(memory_space=pl.ANY)
KERNEL_VMEM = 60 * 1024 * 1024


class Mover:
    def __init__(self, sems):
        self.sems = sems
        self.used = 0

    def go(self, src, dst):
        copy = pltpu.make_async_copy(src, dst, self.sems.at[self.used])
        self.used += 1
        copy.start()
        return copy


def gradient_kernel(spots, core, *refs):
    n = len(spots)
    wide, refs = refs[:n], refs[n:]
    m = len(refs) - 7
    narrow, refs = refs[:m], refs[m:]
    away, kept, xs, sv, st, ov, sems = refs
    quarters, _, size = xs.shape
    ff = sv.shape[1]
    move = Mover(sems)
    load_s, load_x, at = [], [], 0
    for r in narrow:
        load_s.append(move.go(r, sv.at[pl.ds(at, r.shape[0])]))
        at += r.shape[0]
    for i in range(quarters):
        c = core[0] if i >= quarters // 2 else 1 - core[0]
        first = pl.multiple_of(((i % (quarters // 2)) * 2 + c) * size, size)
        load_x.append([
            move.go(r.at[:, pl.ds(first, size)], xs.at[i, pl.ds(at, r.shape[0])])
            for r, at in zip(wide, spots)
        ])
    for c in load_s:
        c.wait()
    for f in range(0, ff, 256):
        st[f:f + 256, :] = sv[:, f:f + 256].T
    stores = []
    for i in range(quarters):
        for c in load_x[i]:
            c.wait()
        for f in range(0, ff, 256):
            ov[i, f:f + 256, :] = jnp.dot(
                st[f:f + 256, :], xs[i], preferred_element_type=jnp.float32
            ).astype(jnp.bfloat16)
        half = quarters // 2
        stores.append(move.go(ov.at[i], away.at[i] if i < half else kept.at[i - half]))
    for c in stores:
        c.wait()


FREE = pl.CostEstimate(flops=0, bytes_accessed=0, transcendentals=0)


def gradient(wide, narrow, name):
    n_dp = lax.axis_size("dp")
    spots, at = [], 0
    for x in wide:
        spots.append(at)
        at += x.shape[0]
    features, ff = wide[0].shape[1], narrow[0].shape[1]
    size = features // n_dp
    half = jax.ShapeDtypeStruct((n_dp // 2, ff, size), jnp.bfloat16)
    core = (lax.axis_index("dp") % 2).reshape(1)
    return pl.pallas_call(
        functools.partial(gradient_kernel, tuple(spots)),
        out_shape=[half, half],
        in_specs=[pl.BlockSpec(memory_space=pltpu.SMEM)] + [ANY] * (len(wide) + len(narrow)),
        out_specs=[ANY, ANY],
        scratch_shapes=[
            pltpu.VMEM((n_dp, at, size), jnp.bfloat16),
            pltpu.VMEM((at, ff), jnp.bfloat16),
            pltpu.VMEM((ff, at), jnp.bfloat16),
            pltpu.VMEM((n_dp, ff, size), jnp.bfloat16),
            pltpu.SemaphoreType.DMA((len(narrow) + n_dp * len(wide) + n_dp,)),
        ],
        compiler_params=pltpu.CompilerParams(vmem_limit_bytes=KERNEL_VMEM),
        cost_estimate=FREE,
        name=name,
    )(core, *wide, *narrow)


def total_of(*values):
    total = values[0].astype(jnp.float32)
    for v in values[1:]:
        total = total + v.astype(jnp.float32)
    return total.astype(jnp.bfloat16)


def ahead_kernel(part, got, out):
    some = got.shape[1]
    out[:, :some] = total_of(part[:, :some], got[...])
    if some < part.shape[1]:
        out[:, some:] = part[:, some:]


def behind_kernel(part, got, out):
    rest = part.shape[1] - got.shape[1]
    out[:, rest:] = total_of(part[:, rest:], got[...])
    if rest:
        out[:, :rest] = part[:, :rest]


def end_kernel(own, got_f, got_b, o, t):
    o[...] = total_of(own[0], got_f[0], got_b[0])
    t[...] = total_of(own[1], got_f[1], got_b[1])


def by_columns(kernel, operands, out_shapes, name):
    features = out_shapes[0][-1]
    steps = 2

    def spec(shape):
        block = tuple(shape[:-1]) + (features // steps,)
        return pl.BlockSpec(block, lambda i, n=len(shape): (0,) * (n - 1) + (i,))

    return pl.pallas_call(
        kernel,
        out_shape=[jax.ShapeDtypeStruct(s, jnp.bfloat16) for s in out_shapes],
        grid=(steps,),
        in_specs=[spec(v.shape) for v in operands],
        out_specs=[spec(s) for s in out_shapes],
        compiler_params=pltpu.CompilerParams(vmem_limit_bytes=KERNEL_VMEM),
        cost_estimate=FREE,
        name=name,
    )(*operands)


def last_add_kernel(turned, y, kept, got, last, out):
    total = kept[0].astype(jnp.float32) + got[0].astype(jnp.float32) + last[...].astype(jnp.float32)
    out[...] = (total.T if turned else total).astype(jnp.bfloat16)[None]


def last_add(kept, got, last, turned, name):
    ff, size = kept.shape[1:]
    y = (lax.axis_index("dp") // 2).reshape(1)
    shape = (1, size, ff) if turned else (1, ff, size)
    half = pl.BlockSpec((1, ff, size), lambda i, y: (y[0], 0, 0))
    return pl.pallas_call(
        functools.partial(last_add_kernel, turned),
        out_shape=jax.ShapeDtypeStruct(shape, jnp.bfloat16),
        grid_spec=pltpu.PrefetchScalarGridSpec(
            num_scalar_prefetch=1,
            grid=(1,),
            in_specs=[half, half, pl.BlockSpec((ff, size), lambda i, y: (0, 0))],
            out_specs=pl.BlockSpec(shape, lambda i, y: (0, 0, 0)),
        ),
        compiler_params=pltpu.CompilerParams(vmem_limit_bytes=KERNEL_VMEM),
        cost_estimate=FREE,
        name=name,
    )(y, kept, got, last)


def expert_kernel(n, *refs):
    xs, gs, refs = refs[:n], refs[n:2 * n], refs[2 * n:]
    w, wg, wu, wd, wdt, wgt, wut = refs[:7]
    refs = refs[7:]
    both, refs = refs[:n], refs[n:]
    s_o, dg_o, du_o, comb_o = refs[:4]
    x2, g2, wgv, wuv, wdv, wdtv, wgtv, wutv, gv, uv, sv, dgv, duv, ov, rv, sems = refs[4:]
    part = xs[0].shape[0]
    features = x2.shape[1]
    ff = gv.shape[1]
    f32, bf16 = jnp.float32, jnp.bfloat16
    move = Mover(sems)
    cols = [pl.ds(f, 256) for f in range(0, ff, 256)]
    wide = [pl.ds(d, 512) for d in range(0, features, 512)]
    spots = [pl.ds(i * part, part) for i in range(n)]
    load_x = [move.go(r, x2.at[s]) for r, s in zip(xs, spots)]
    load_g = [move.go(wg.at[:, c], wgv.at[:, c]) for c in cols]
    load_u = move.go(wu, wuv)
    load_d = move.go(wd, wdv)
    for c in load_x:
        c.wait()
    for c, load in zip(cols, load_g):
        load.wait()
        gv[:, c] = jnp.dot(x2[...], wgv[:, c], preferred_element_type=f32)
    load_cot = [move.go(r, g2.at[s]) for r, s in zip(gs, spots)]
    load_dt = move.go(wdt, wdtv)
    load_u.wait()
    for c in cols:
        up = jnp.dot(x2[...], wuv[:, c], preferred_element_type=f32)
        uv[:, c] = up
        gate = gv[:, c]
        sv[:, c] = (gate * jax.nn.sigmoid(gate) * up * w[...]).astype(bf16)
    stores = [move.go(sv, s_o)]
    load_gt = move.go(wgt, wgtv)
    load_ut = move.go(wut, wutv)
    load_d.wait()
    for c in wide:
        ov[:, c] = jnp.dot(sv[...], wdv[:, c], preferred_element_type=f32).astype(bf16)
    stores += [move.go(ov.at[s], r.at[0]) for r, s in zip(both, spots)]
    for c in load_cot:
        c.wait()
    load_dt.wait()
    comb = jnp.zeros_like(comb_o)
    for c in cols:
        d_raw = jnp.dot(g2[...], wdtv[:, c], preferred_element_type=f32)
        gate, up = gv[:, c], uv[:, c]
        sig = jax.nn.sigmoid(gate)
        act = gate * sig
        comb += jnp.sum(act * up * d_raw, axis=1, keepdims=True)
        d_hidden = d_raw * w[...]
        dgv[:, c] = (d_hidden * up * sig * (1.0 + gate * (1.0 - sig))).astype(bf16)
        duv[:, c] = (d_hidden * act).astype(bf16)
    comb_o[...] = comb
    stores += [move.go(dgv, dg_o), move.go(duv, du_o)]
    load_gt.wait()
    load_ut.wait()
    for c in wide:
        rv[:, c] = (
            jnp.dot(dgv[...], wgtv[:, c], preferred_element_type=f32)
            + jnp.dot(duv[...], wutv[:, c], preferred_element_type=f32)
        ).astype(bf16)
    stores += [move.go(rv.at[s], r.at[1]) for r, s in zip(both, spots)]
    for c in stores:
        c.wait()


def expert(xs, gs, weight, ws, name):
    n, (part, features) = len(xs), xs[0].shape
    ff = ws[0].shape[1]
    rows = n * part
    bf16, f32 = jnp.bfloat16, jnp.float32
    vmem = pl.BlockSpec(memory_space=pltpu.VMEM)
    block = jax.ShapeDtypeStruct((2, part, features), bf16)
    narrow = jax.ShapeDtypeStruct((rows, ff), bf16)
    operands = [*xs, *gs, weight, *ws]
    res = pl.pallas_call(
        functools.partial(expert_kernel, n),
        out_shape=[block] * n + [narrow] * 3 + [jax.ShapeDtypeStruct((rows, 1), f32)],
        in_specs=[ANY] * (2 * n) + [vmem] + [ANY] * 6,
        out_specs=[ANY] * (n + 3) + [vmem],
        scratch_shapes=[
            pltpu.VMEM((rows, features), bf16),
            pltpu.VMEM((rows, features), bf16),
            pltpu.VMEM((features, ff), bf16),
            pltpu.VMEM((features, ff), bf16),
            pltpu.VMEM((ff, features), bf16),
            pltpu.VMEM((features, ff), bf16),
            pltpu.VMEM((ff, features), bf16),
            pltpu.VMEM((ff, features), bf16),
            pltpu.VMEM((rows, ff), f32),
            pltpu.VMEM((rows, ff), f32),
            pltpu.VMEM((rows, ff), bf16),
            pltpu.VMEM((rows, ff), bf16),
            pltpu.VMEM((rows, ff), bf16),
            pltpu.VMEM((rows, features), bf16),
            pltpu.VMEM((rows, features), bf16),
            pltpu.SemaphoreType.DMA((24,)),
        ],
        compiler_params=pltpu.CompilerParams(vmem_limit_bytes=KERNEL_VMEM),
        cost_estimate=FREE,
        name=name,
    )(*operands)
    return res[:n], res[n:]


def gathered_plan(tokens, routes, combine, cotangent, w_gate, w_up, w_down):
    tok_rows, features = tokens.shape
    groups = lax.axis_size("expert")
    me = lax.axis_index("expert")
    half = tok_rows // 2
    f32 = jnp.float32
    chosen = routes[:, :, None] == jnp.arange(groups, dtype=jnp.int32)[None, None, :]
    weights = jnp.sum(jnp.where(chosen, combine[:, :, None], 0.0), axis=1)
    sources = jnp.asarray(ring_sources(), jnp.int32)[me]
    wg, wu, wd = w_gate[0], w_up[0], w_down[0]
    ws = (wg, wu, wd, wd.T, wg.T, wu.T)

    arrived = lax.all_to_all(weights.T, "expert", split_axis=0, concat_axis=0, tiled=True)
    weight = arrived[sources].reshape(groups * tok_rows, 1)
    moving = [forward(tokens), backward(tokens), forward(cotangent), backward(cotangent)]
    *moving, w_down_t, w_gate_t, w_up_t = tie(*moving, *ws[3:])
    ws = (wg, wu, wd, w_down_t, w_gate_t, w_up_t)
    all_x, all_g, parts, smalls = [], [], [], []
    at = 0
    for step in range(1, 5):
        xs, gs = moving[:2], moving[2:]
        if step < 4:
            sent = moving
            if step == 3:
                sent = [moving[0][:half], moving[1][half:], moving[2][:half], moving[3][half:]]
            moving = [forward(sent[0]), backward(sent[1]), forward(sent[2]), backward(sent[3])]
        if step == 1:
            xs, gs = [tokens, *xs], [cotangent, *gs]
        rows = sum(x.shape[0] for x in xs)
        w = lax.dynamic_slice_in_dim(weight, at, rows, 0)
        at += rows
        part, small = expert(xs, gs, w, ws, f"expert_{step}")
        if step < 4:
            *moving, first_small = tie(*moving, small[0])
            small = [first_small, *small[1:]]
        all_x += xs
        all_g += gs
        parts += part
        smalls.append(small)

    scaled, d_gate, d_up, combs = (list(v) for v in zip(*smalls))
    full = [parts[0].shape]

    def summed(step, f, b):
        f, = by_columns(ahead_kernel, [parts[8 - 2 * step], f], full, f"ahead_{step}")
        b, = by_columns(behind_kernel, [parts[7 - 2 * step], b], full, f"behind_{step}")
        return f, b

    f, b = forward(parts[7]), backward(parts[8])
    away_d, kept_d = gradient(all_g, scaled, "grad_down")
    f, b, away_d, d_gate[-1], d_up[-1] = tie(f, b, away_d, d_gate[-1], d_up[-1])

    got_d = core_swap(away_d)
    f, b = summed(1, f, b)
    f, b = forward(f), backward(b)
    other_d = y_part(kept_d, got_d)
    other_d, d_gate[-1], d_up[-1] = tie(other_d, d_gate[-1], d_up[-1])
    last_d = y_swap(other_d)
    away_g, kept_g = gradient(all_x, d_gate, "grad_gate")
    away_u, kept_u = gradient(all_x, d_up, "grad_up")
    f, b, last_d, away_g, away_u, combs[-1] = tie(f, b, last_d, away_g, away_u, combs[-1])

    got_g, got_u = core_swap(away_g), core_swap(away_u)
    f, b = summed(2, f, b)
    f, b = forward(f), backward(b)
    last_g = y_swap(y_part(kept_g, got_g))
    table = ring_sources()
    inverse = jnp.asarray([[row.index(e) for e in range(groups)] for row in table], jnp.int32)[me]
    d_comb = jnp.concatenate(combs, axis=0).reshape(groups, tok_rows)[inverse]
    returned = lax.all_to_all(d_comb, "expert", split_axis=0, concat_axis=0, tiled=True)
    f, b, last_g, got_u, last_d, returned = tie(f, b, last_g, got_u, last_d, returned)

    f, b = summed(3, f, b)
    f, b, last_u = forward(f), backward(b), y_swap(y_part(kept_u, got_u))
    d_w_down = last_add(kept_d, got_d, last_d, False, "sum_down")
    d_w_gate = last_add(kept_g, got_g, last_g, True, "sum_gate")
    d_combine = jnp.sum(jnp.where(chosen, returned.T[:, None, :], 0.0), axis=2)
    output, d_tokens = by_columns(
        end_kernel, [parts[0], f, b], [tokens.shape, tokens.shape], "sum_end"
    )
    d_w_up = last_add(kept_u, got_u, last_u, True, "sum_up")
    return output, d_tokens, d_combine, d_w_gate, d_w_up, d_w_down


def solution(mesh):
    rows = P(("dp", "expert"), None)
    small = mesh.shape["expert"] == len(RING) and mesh.shape["dp"] == 4
    return jax.shard_map(
        gathered_plan if small else routed_plan,
        mesh=mesh,
        in_specs=(rows, rows, rows, rows) + (P("expert", None, None),) * 3,
        out_specs=(
            rows,
            rows,
            rows,
            P("expert", "dp", None),
            P("expert", "dp", None),
            P("expert", None, "dp"),
        ),
        check_vma=False,
    )
```

```python
import functools
import jax
import jax.numpy as jnp
from jax import lax
from jax.experimental import pallas as pl
from jax.experimental.pallas import tpu as pltpu
from jax.sharding import PartitionSpec as P


def slot_map(routes, experts, capacity):
    flat_ids = routes.reshape(-1)
    onehot = (flat_ids[:, None] == jnp.arange(experts, dtype=jnp.int32)[None, :]).astype(jnp.int32)
    before = jnp.cumsum(onehot, axis=0) - onehot
    slots = jnp.sum(before * onehot, axis=1)
    target = flat_ids * capacity + slots
    source = (
        jnp.full((experts * capacity,), -1, jnp.int32)
        .at[target]
        .set(jnp.arange(flat_ids.shape[0], dtype=jnp.int32))
    )
    return (target, source)


def routed_plan(tokens, routes, combine, cotangent, w_gate, w_up, w_down):
    tok_rows, features = tokens.shape
    per_token = routes.shape[1]
    groups = lax.axis_size("expert")
    local_exp = w_gate.shape[0]
    experts = local_exp * groups
    capacity = 3 * tok_rows * per_token // (2 * experts)
    target, source = slot_map(routes, experts, capacity)
    filled = (source >= 0)[:, None]
    pair_index = jnp.maximum(source, 0)
    owner_row = pair_index // per_token
    outgoing = jnp.where(filled, tokens[owner_row], jnp.zeros((), jnp.bfloat16))
    outgoing = outgoing.reshape(groups, local_exp, capacity, features)
    cot_float = cotangent.astype(jnp.float32)
    scaled = (combine[:, :, None] * cot_float[:, None, :]).reshape(tok_rows * per_token, features)
    outgoing_grad = jnp.where(filled, scaled[pair_index], 0.0).astype(jnp.bfloat16)
    outgoing_grad = outgoing_grad.reshape(groups, local_exp, capacity, features)
    arrived = lax.all_to_all(outgoing, "expert", split_axis=0, concat_axis=0, tiled=True)
    gate_pre = jnp.einsum("secd,edf->secf", arrived, w_gate, preferred_element_type=jnp.float32)
    up_pre = jnp.einsum("secd,edf->secf", arrived, w_up, preferred_element_type=jnp.float32)
    activated = jax.nn.silu(gate_pre)
    hidden = (activated * up_pre).astype(jnp.bfloat16)
    produced = jnp.einsum(
        "secf,efd->secd", hidden, w_down, preferred_element_type=jnp.float32
    ).astype(jnp.bfloat16)
    returned = lax.all_to_all(produced, "expert", split_axis=0, concat_axis=0, tiled=True)
    d_in = lax.all_to_all(outgoing_grad, "expert", split_axis=0, concat_axis=0, tiled=True)
    d_hidden = jnp.einsum("secd,efd->secf", d_in, w_down, preferred_element_type=jnp.float32)
    part_down = jnp.einsum("secf,secd->efd", hidden, d_in, preferred_element_type=jnp.float32)
    sigmoid_g = jax.nn.sigmoid(gate_pre)
    d_gate = (d_hidden * up_pre * sigmoid_g * (1.0 + gate_pre * (1.0 - sigmoid_g))).astype(
        jnp.bfloat16
    )
    d_up = (d_hidden * activated).astype(jnp.bfloat16)
    part_gate = jnp.einsum("secd,secf->edf", arrived, d_gate, preferred_element_type=jnp.float32)
    part_up = jnp.einsum("secd,secf->edf", arrived, d_up, preferred_element_type=jnp.float32)
    d_rows = (
        jnp.einsum("secf,edf->secd", d_gate, w_gate, preferred_element_type=jnp.float32)
        + jnp.einsum("secf,edf->secd", d_up, w_up, preferred_element_type=jnp.float32)
    ).astype(jnp.bfloat16)
    back = lax.all_to_all(d_rows, "expert", split_axis=0, concat_axis=0, tiled=True)
    per_slot = returned.reshape(experts * capacity, features)[target]
    per_slot = per_slot.reshape(tok_rows, per_token, features).astype(jnp.float32)
    output = jnp.sum(combine[:, :, None] * per_slot, axis=1).astype(jnp.bfloat16)
    d_combine = jnp.sum(per_slot * cot_float[:, None, :], axis=2)
    back_slot = back.reshape(experts * capacity, features)[target]
    back_slot = back_slot.reshape(tok_rows, per_token, features).astype(jnp.float32)
    d_tokens = jnp.sum(back_slot, axis=1).astype(jnp.bfloat16)
    sum_gate, sum_up, sum_down = (
        lax.psum_scatter(
            part_gate.astype(jnp.bfloat16), "dp", scatter_dimension=1, tiled=True
        ).astype(jnp.float32),
        lax.psum_scatter(
            part_up.astype(jnp.bfloat16), "dp", scatter_dimension=1, tiled=True
        ).astype(jnp.float32),
        lax.psum_scatter(
            part_down.astype(jnp.bfloat16), "dp", scatter_dimension=2, tiled=True
        ).astype(jnp.float32),
    )
    d_w_down = sum_down.astype(jnp.bfloat16)
    return (
        output,
        d_tokens,
        d_combine,
        sum_gate.astype(jnp.bfloat16),
        sum_up.astype(jnp.bfloat16),
        d_w_down,
    )


RING = (0, 1, 3, 5, 7, 6, 4, 2)


def ring_perms():
    n = len(RING)
    fwd = [(RING[i], RING[(i + 1) % n]) for i in range(n)]
    bwd = [(RING[(i + 1) % n], RING[i]) for i in range(n)]
    return fwd, bwd


def ring_sources():
    n = len(RING)
    place = {e: i for i, e in enumerate(RING)}
    steps = (0, -1, 1, -2, 2, -3, 3, 4)
    return [[RING[(place[e] + r) % n] for r in steps] for e in range(n)]


def forward(value):
    return lax.ppermute(value, "expert", ring_perms()[0])


def backward(value):
    return lax.ppermute(value, "expert", ring_perms()[1])


def tie(*values):
    return lax.optimization_barrier(values)


def add_rounded(a, b):
    return (a.astype(jnp.float32) + b.astype(jnp.float32)).astype(jnp.bfloat16)


def core_swap(away):
    n = lax.axis_size("dp")
    return lax.ppermute(away, "dp", [(j, j ^ 1) for j in range(n)])


def pick(halves, y):
    return lax.dynamic_index_in_dim(halves, y, 0, keepdims=False)


def y_parts(kept, got):
    y = lax.axis_index("dp") // 2
    half = kept.shape[1] // 2
    kept, got = pick(kept, 1 - y), pick(got, 1 - y)
    return add_rounded(kept[:half], got[:half]), add_rounded(kept[half:], got[half:])


def y_swap(other):
    n = lax.axis_size("dp")
    return lax.ppermute(other, "dp", [(j, j ^ 2) for j in range(n)])


ANY = pl.BlockSpec(memory_space=pl.ANY)
KERNEL_VMEM = 60 * 1024 * 1024
EXTRA = 16


class Mover:
    def __init__(self, sems):
        self.sems = sems
        self.used = 0

    def go(self, src, dst):
        copy = pltpu.make_async_copy(src, dst, self.sems.at[self.used])
        self.used += 1
        copy.start()
        return copy


def gradient_kernel(part, spots, tall_spots, core, *refs):
    n, m = len(spots), len(tall_spots)
    wide, narrow, refs = refs[:n], refs[n:n + m], refs[n + m:]
    away, kept, xs, st, ov, sems = refs
    quarters, _, size = xs.shape
    move = Mover(sems)
    load_s = [
        move.go(r, st.at[pl.ds(top, r.shape[0]), pl.ds(at, r.shape[1])])
        for r, (top, at) in zip(narrow, tall_spots)
    ]
    load_x = []
    for i in range(quarters):
        c = core[0] if i >= quarters // 2 else 1 - core[0]
        first = pl.multiple_of(((i % (quarters // 2)) * 2 + c) * size, size)
        load_x.append([
            move.go(r.at[pl.ds(0, part), pl.ds(first, size)], xs.at[i, pl.ds(at, part)])
            for r, at in zip(wide, spots)
        ])
    for c in load_s:
        c.wait()
    stores = []
    for i in range(quarters):
        for c in load_x[i]:
            c.wait()
        for f in range(0, st.shape[0], 256):
            ov[i, f:f + 256, :] = jnp.dot(
                st[f:f + 256, :], xs[i], preferred_element_type=jnp.float32
            ).astype(jnp.bfloat16)
        half = quarters // 2
        stores.append(move.go(ov.at[i], away.at[i] if i < half else kept.at[i - half]))
    for c in stores:
        c.wait()


FREE = pl.CostEstimate(flops=0, bytes_accessed=0, transcendentals=0)


def gradient(wide, part, narrows, name):
    n_dp = lax.axis_size("dp")
    spots, at = [part * i for i in range(len(wide))], part * len(wide)
    flat, tall_spots, tall = [], [], 0
    for pieces in narrows:
        col = 0
        for piece in pieces:
            flat.append(piece)
            tall_spots.append((tall, col))
            col += piece.shape[1]
        tall += pieces[0].shape[0]
    size = wide[0].shape[1] // n_dp
    half = jax.ShapeDtypeStruct((n_dp // 2, tall, size), jnp.bfloat16)
    core = (lax.axis_index("dp") % 2).reshape(1)
    return pl.pallas_call(
        functools.partial(gradient_kernel, part, tuple(spots), tuple(tall_spots)),
        out_shape=[half, half],
        in_specs=[pl.BlockSpec(memory_space=pltpu.SMEM)] + [ANY] * (len(wide) + len(flat)),
        out_specs=[ANY, ANY],
        scratch_shapes=[
            pltpu.VMEM((n_dp, at, size), jnp.bfloat16),
            pltpu.VMEM((tall, at), jnp.bfloat16),
            pltpu.VMEM((n_dp, tall, size), jnp.bfloat16),
            pltpu.SemaphoreType.DMA((len(flat) + n_dp * len(wide) + n_dp,)),
        ],
        compiler_params=pltpu.CompilerParams(vmem_limit_bytes=KERNEL_VMEM),
        cost_estimate=FREE,
        name=name,
    )(core, *wide, *flat)


def total_of(*values):
    total = values[0].astype(jnp.float32)
    for v in values[1:]:
        total = total + v.astype(jnp.float32)
    return total.astype(jnp.bfloat16)


def pair_kernel(part_f, got_f, part_b, got_b, f, b):
    f[...] = total_of(part_f[...], got_f[...])
    b[...] = total_of(part_b[...], got_b[...])


def end_kernel(own_o, of, ob, own_t, tf, tb, o, t):
    o[...] = total_of(own_o[...], of[...], ob[...])
    t[...] = total_of(own_t[...], tf[...], tb[...])


def by_columns(kernel, operands, out_shapes, name):
    features = out_shapes[0][-1]
    steps = 2

    def spec(shape):
        block = tuple(shape[:-1]) + (features // steps,)
        return pl.BlockSpec(block, lambda i, n=len(shape): (0,) * (n - 1) + (i,))

    return pl.pallas_call(
        kernel,
        out_shape=[jax.ShapeDtypeStruct(s, jnp.bfloat16) for s in out_shapes],
        grid=(steps,),
        in_specs=[spec(v.shape) for v in operands],
        out_specs=[spec(s) for s in out_shapes],
        compiler_params=pltpu.CompilerParams(vmem_limit_bytes=KERNEL_VMEM),
        cost_estimate=FREE,
        name=name,
    )(*operands)


def last_add_kernel(turned, y, kept, got, last_0, last_1, out):
    half = last_0.shape[0]
    for i, last in enumerate((last_0, last_1)):
        rows = pl.ds(i * half, half)
        total = kept[0, rows].astype(jnp.float32) + got[0, rows].astype(jnp.float32)
        total = total + last[...].astype(jnp.float32)
        if turned:
            out[0, :, rows] = total.T.astype(jnp.bfloat16)
        else:
            out[0, rows] = total.astype(jnp.bfloat16)


def last_add(kept, got, lasts, turned, name):
    _, ff, size = kept.shape
    y = (lax.axis_index("dp") // 2).reshape(1)
    shape = (1, size, ff) if turned else (1, ff, size)
    half = pl.BlockSpec((1, ff, size), lambda i, y: (y[0], 0, 0))
    piece = pl.BlockSpec((ff // 2, size), lambda i, y: (0, 0))
    return pl.pallas_call(
        functools.partial(last_add_kernel, turned),
        out_shape=jax.ShapeDtypeStruct(shape, jnp.bfloat16),
        grid_spec=pltpu.PrefetchScalarGridSpec(
            num_scalar_prefetch=1,
            grid=(1,),
            in_specs=[half, half, piece, piece],
            out_specs=pl.BlockSpec(shape, lambda i, y: (0, 0, 0)),
        ),
        compiler_params=pltpu.CompilerParams(vmem_limit_bytes=KERNEL_VMEM),
        cost_estimate=FREE,
        name=name,
    )(y, kept, got, *lasts)


def with_weights_kernel(cot, routes, combine, out):
    rows, features = cot.shape
    out[:rows] = cot[...]
    lane = lax.broadcasted_iota(jnp.int32, (rows, 128), 1)
    weights = jnp.zeros((rows, 128), jnp.float32)
    for k in range(routes.shape[1]):
        weights += jnp.where(routes[:, k:k + 1] == lane, combine[:, k:k + 1], 0.0)
    weights = weights.T[:EXTRA]
    wide = weights * 65537.0
    high = wide - (wide - weights)
    rest = weights - high
    wide = rest * 65537.0
    middle = wide - (wide - rest)
    out[rows:] = jnp.zeros((EXTRA, features), jnp.bfloat16)
    for i, term in enumerate((high, middle, rest - middle)):
        out[rows:, i * rows:(i + 1) * rows] = term.astype(jnp.bfloat16)


def with_weights(cot, routes, combine):
    return pl.pallas_call(
        with_weights_kernel,
        out_shape=jax.ShapeDtypeStruct((cot.shape[0] + EXTRA, cot.shape[1]), cot.dtype),
        cost_estimate=FREE,
        name="with_weights",
    )(cot, routes, combine)


def expert_kernel(n, me, *refs):
    xs, gs, refs = refs[:n], refs[n:2 * n], refs[2 * n:]
    wg, wu, wd, wdt, wgt, wut = refs[:6]
    outs, backs, refs = refs[6:6 + n], refs[6 + n:6 + 2 * n], refs[6 + 2 * n:]
    s_o, dg_o, du_o, comb_o = refs[:4]
    x2, g2, wgv, wuv, wdv, wdtv, wgtv, wutv, gv, uv, sv, dgv, duv, wb, wv, st, dgt, dut, ov, rv, sems = refs[4:]
    part = xs[0].shape[0]
    rows, features = x2.shape
    ff = gv.shape[1]
    f32, bf16 = jnp.float32, jnp.bfloat16
    move = Mover(sems)
    cols = [pl.ds(f, 256) for f in range(0, ff, 256)]
    wide = [pl.ds(d, 512) for d in range(0, features, 512)]
    spots = [pl.ds(i * part, part) for i in range(n)]

    def load(src, dst, pieces):
        size = src.shape[0] // pieces
        return [
            move.go(src.at[pl.ds(i * size, size)], dst.at[pl.ds(i * size, size)])
            for i in range(pieces)
        ]

    load_x = [move.go(r, x2.at[s]) for r, s in zip(xs, spots)]
    span = wb.shape[2]
    load_w = [move.go(r.at[pl.ds(part, EXTRA), pl.ds(0, span)], wb.at[i]) for i, r in enumerate(gs)]
    load_g = load(wg, wgv, 4)
    load_u = load(wu, wuv, 4)
    load_cot = [move.go(r.at[pl.ds(0, part)], g2.at[s]) for r, s in zip(gs, spots)]
    load_d = load(wd, wdv, 4)
    load_dt = load(wdt, wdtv, 4)
    load_gt = load(wgt, wgtv, 4)
    load_ut = load(wut, wutv, 4)
    for c in load_w:
        c.wait()
    for i, s in enumerate(spots):
        terms = wb[i].astype(f32)
        mine = lax.broadcasted_iota(jnp.int32, terms.shape, 0) == me[0]
        terms = jnp.sum(jnp.where(mine, terms, 0.0), axis=0, keepdims=True)
        terms = terms[:, :part] + terms[:, part:2 * part] + terms[:, 2 * part:]
        wv[s, :] = jnp.broadcast_to(terms, (128, part)).T[:, :1]
    for c in load_x + load_g:
        c.wait()
    for c in cols:
        gv[:, c] = jnp.dot(x2[...], wgv[:, c], preferred_element_type=f32)
    for c in load_u:
        c.wait()
    for c in cols:
        up = jnp.dot(x2[...], wuv[:, c], preferred_element_type=f32)
        uv[:, c] = up
        gate = gv[:, c]
        scaled = (gate * jax.nn.sigmoid(gate) * up * wv[...]).astype(bf16)
        sv[:, c] = scaled
        st[c, :] = scaled.T
    stores = [move.go(st, s_o)]
    for c in load_d:
        c.wait()
    for c in wide:
        ov[:, c] = jnp.dot(sv[...], wdv[:, c], preferred_element_type=f32).astype(bf16)
    stores += [move.go(ov.at[s], r) for r, s in zip(outs, spots)]
    for c in load_cot + load_dt:
        c.wait()
    comb = jnp.zeros((rows, 1), f32)
    for c in cols:
        d_raw = jnp.dot(g2[...], wdtv[:, c], preferred_element_type=f32)
        gate, up = gv[:, c], uv[:, c]
        sig = jax.nn.sigmoid(gate)
        act = gate * sig
        comb += jnp.sum(act * up * d_raw, axis=1, keepdims=True)
        d_hidden = d_raw * wv[...]
        d_gate = (d_hidden * up * sig * (1.0 + gate * (1.0 - sig))).astype(bf16)
        d_up = (d_hidden * act).astype(bf16)
        dgv[:, c] = d_gate
        duv[:, c] = d_up
        dgt[c, :] = d_gate.T
        dut[c, :] = d_up.T
    comb_o[...] = jnp.broadcast_to(comb, (rows, 128)).T[:1, :]
    stores += [move.go(dgt, dg_o), move.go(dut, du_o)]
    for c in load_gt + load_ut:
        c.wait()
    for c in wide:
        rv[:, c] = (
            jnp.dot(dgv[...], wgtv[:, c], preferred_element_type=f32)
            + jnp.dot(duv[...], wutv[:, c], preferred_element_type=f32)
        ).astype(bf16)
    stores += [move.go(rv.at[s], r) for r, s in zip(backs, spots)]
    for c in stores:
        c.wait()


def expert(xs, gs, matrices, name):
    n, (part, features) = len(xs), xs[0].shape
    ff = matrices[0].shape[1]
    rows = n * part
    bf16, f32 = jnp.bfloat16, jnp.float32
    vmem = pl.BlockSpec(memory_space=pltpu.VMEM)
    block = jax.ShapeDtypeStruct((part, features), bf16)
    turned = jax.ShapeDtypeStruct((ff, rows), bf16)
    me = lax.axis_index("expert").reshape(1)
    res = pl.pallas_call(
        functools.partial(expert_kernel, n),
        out_shape=[block] * (2 * n) + [turned] * 3 + [jax.ShapeDtypeStruct((1, rows), f32)],
        in_specs=[pl.BlockSpec(memory_space=pltpu.SMEM)] + [ANY] * (2 * n + 6),
        out_specs=[ANY] * (2 * n + 3) + [vmem],
        scratch_shapes=[
            pltpu.VMEM((rows, features), bf16),
            pltpu.VMEM((rows, features), bf16),
            pltpu.VMEM((features, ff), bf16),
            pltpu.VMEM((features, ff), bf16),
            pltpu.VMEM((ff, features), bf16),
            pltpu.VMEM((features, ff), bf16),
            pltpu.VMEM((ff, features), bf16),
            pltpu.VMEM((ff, features), bf16),
            pltpu.VMEM((rows, ff), f32),
            pltpu.VMEM((rows, ff), f32),
            pltpu.VMEM((rows, ff), bf16),
            pltpu.VMEM((rows, ff), bf16),
            pltpu.VMEM((rows, ff), bf16),
            pltpu.VMEM((n, EXTRA, 3 * part), bf16),
            pltpu.VMEM((rows, 1), f32),
            pltpu.VMEM((ff, rows), bf16),
            pltpu.VMEM((ff, rows), bf16),
            pltpu.VMEM((ff, rows), bf16),
            pltpu.VMEM((rows, features), bf16),
            pltpu.VMEM((rows, features), bf16),
            pltpu.SemaphoreType.DMA((5 * n + 27,)),
        ],
        compiler_params=pltpu.CompilerParams(vmem_limit_bytes=KERNEL_VMEM),
        cost_estimate=FREE,
        name=name,
    )(me, *xs, *gs, *matrices)
    return res[:n], res[n:2 * n], res[2 * n:]


def gathered_plan(tokens, routes, combine, cotangent, w_gate, w_up, w_down):
    tok_rows, features = tokens.shape
    groups = lax.axis_size("expert")
    me = lax.axis_index("expert")
    chosen = routes[:, :, None] == jnp.arange(groups, dtype=jnp.int32)[None, None, :]
    matrices = [w_gate[0], w_up[0], w_down[0], w_down[0].T, w_gate[0].T, w_up[0].T]

    xs = [forward(tokens), backward(tokens)]
    both = with_weights(cotangent, routes, combine)
    gs = [forward(both), backward(both)]
    *moving, m3, m4, m5 = tie(*xs, *gs, *matrices[3:])
    matrices = matrices[:3] + [m3, m4, m5]
    all_x, all_g, outs, backs, smalls = [], [], [], [], []
    for step in range(1, 5):
        if step < 4:
            here_x, here_g = moving[:2], moving[2:]
        else:
            here_x, here_g = moving[:1], moving[1:]
        if step < 3:
            moving = [forward(here_x[0]), backward(here_x[1]), forward(here_g[0]), backward(here_g[1])]
        elif step == 3:
            moving = [forward(here_x[0]), backward(here_g[1])]
        else:
            moving = [forward(backs[6]), backward(outs[5])]
        if step == 1:
            here_x, here_g = [tokens, *here_x], [both, *here_g]
        out, back, small = expert(here_x, here_g, matrices, f"expert_{step}")
        *moving, first = tie(*moving, small[0])
        all_x += here_x
        all_g += here_g
        outs += out
        backs += back
        smalls.append([first, *small[1:]])

    scaled, d_gate, d_up, combs = (list(v) for v in zip(*smalls))
    two = [tokens.shape] * 2

    def summed(part_f, got_f, part_b, got_b, name):
        return by_columns(pair_kernel, [part_f, got_f, part_b, got_b], two, name)

    tf, ob = moving
    of, tb = forward(outs[7]), backward(backs[7])
    tf, ob = summed(backs[4], tf, outs[3], ob, "sum_a2")
    away_d, kept_d = gradient(all_g, tok_rows, [scaled], "grad_down")
    of, tb, tf, ob, away_d, d_gate[-1] = tie(of, tb, tf, ob, away_d, d_gate[-1])

    tf, ob, got_d = forward(tf), backward(ob), core_swap(away_d)
    of, tb = summed(outs[6], of, backs[5], tb, "sum_b3")
    last_d = [y_swap(v) for v in y_parts(kept_d, got_d)]
    away_g, kept_g = gradient(all_x, tok_rows, [d_gate], "grad_gate")
    tf, ob, of, tb, away_g, d_up[-1], *last_d = tie(tf, ob, of, tb, away_g, d_up[-1], *last_d)

    of, tb, got_g = forward(of), backward(tb), core_swap(away_g)
    tf, ob = summed(backs[2], tf, outs[1], ob, "sum_a1")
    first_g, other_g = y_parts(kept_g, got_g)
    first_g = y_swap(first_g)
    away_u, kept_u = gradient(all_x, tok_rows, [d_up], "grad_up")
    of, tb, tf, ob, away_u, first_g, other_g = tie(of, tb, tf, ob, away_u, first_g, other_g)

    tf, ob, got_u, other_g = forward(tf), backward(ob), core_swap(away_u), y_swap(other_g)
    of, tb = summed(outs[4], of, backs[3], tb, "sum_b2")
    d_w_down = last_add(kept_d, got_d, last_d, False, "sum_down")
    tf, ob, of, tb, got_u, other_g = tie(tf, ob, of, tb, got_u, other_g)

    of, tb = forward(of), backward(tb)
    first_u, other_u = y_parts(kept_u, got_u)
    first_u = y_swap(first_u)
    d_w_gate = last_add(kept_g, got_g, [first_g, other_g], True, "sum_gate")
    of, tb, first_u, other_u = tie(of, tb, first_u, other_u)

    of, tb = summed(outs[2], of, backs[1], tb, "sum_b1")
    of, tb, other_u = forward(of), backward(tb), y_swap(other_u)
    combs[-1], _ = tie(combs[-1], d_w_gate)
    d_comb = jnp.concatenate(combs, axis=1).reshape(groups, tok_rows)
    table = ring_sources()
    inverse = jnp.asarray([[row.index(e) for e in range(groups)] for row in table], jnp.int32)[me]
    returned = lax.all_to_all(d_comb[inverse], "expert", split_axis=0, concat_axis=0, tiled=True)
    d_combine = jnp.sum(jnp.where(chosen, returned.T[:, None, :], 0.0), axis=2)
    output, d_tokens = by_columns(
        end_kernel, [outs[0], of, ob, backs[0], tf, tb], two, "sum_end"
    )
    d_w_up = last_add(kept_u, got_u, [first_u, other_u], True, "sum_up")
    return output, d_tokens, d_combine, d_w_gate, d_w_up, d_w_down


def solution(mesh):
    rows = P(("dp", "expert"), None)
    small = mesh.shape["expert"] == len(RING) and mesh.shape["dp"] == 4
    return jax.shard_map(
        gathered_plan if small else routed_plan,
        mesh=mesh,
        in_specs=(rows, rows, rows, rows) + (P("expert", None, None),) * 3,
        out_specs=(
            rows,
            rows,
            rows,
            P("expert", "dp", None),
            P("expert", "dp", None),
            P("expert", None, "dp"),
        ),
        check_vma=False,
    )
```

```python
import functools
import jax
import jax.numpy as jnp
from jax import lax
from jax.experimental import pallas as pl
from jax.experimental.pallas import tpu as pltpu
from jax.sharding import PartitionSpec as P


def slot_map(routes, experts, capacity):
    flat_ids = routes.reshape(-1)
    onehot = (flat_ids[:, None] == jnp.arange(experts, dtype=jnp.int32)[None, :]).astype(jnp.int32)
    before = jnp.cumsum(onehot, axis=0) - onehot
    slots = jnp.sum(before * onehot, axis=1)
    target = flat_ids * capacity + slots
    source = (
        jnp.full((experts * capacity,), -1, jnp.int32)
        .at[target]
        .set(jnp.arange(flat_ids.shape[0], dtype=jnp.int32))
    )
    return (target, source)


def routed_plan(tokens, routes, combine, cotangent, w_gate, w_up, w_down):
    tok_rows, features = tokens.shape
    per_token = routes.shape[1]
    groups = lax.axis_size("expert")
    local_exp = w_gate.shape[0]
    experts = local_exp * groups
    capacity = 3 * tok_rows * per_token // (2 * experts)
    target, source = slot_map(routes, experts, capacity)
    filled = (source >= 0)[:, None]
    pair_index = jnp.maximum(source, 0)
    owner_row = pair_index // per_token
    outgoing = jnp.where(filled, tokens[owner_row], jnp.zeros((), jnp.bfloat16))
    outgoing = outgoing.reshape(groups, local_exp, capacity, features)
    cot_float = cotangent.astype(jnp.float32)
    scaled = (combine[:, :, None] * cot_float[:, None, :]).reshape(tok_rows * per_token, features)
    outgoing_grad = jnp.where(filled, scaled[pair_index], 0.0).astype(jnp.bfloat16)
    outgoing_grad = outgoing_grad.reshape(groups, local_exp, capacity, features)
    arrived = lax.all_to_all(outgoing, "expert", split_axis=0, concat_axis=0, tiled=True)
    gate_pre = jnp.einsum("secd,edf->secf", arrived, w_gate, preferred_element_type=jnp.float32)
    up_pre = jnp.einsum("secd,edf->secf", arrived, w_up, preferred_element_type=jnp.float32)
    activated = jax.nn.silu(gate_pre)
    hidden = (activated * up_pre).astype(jnp.bfloat16)
    produced = jnp.einsum(
        "secf,efd->secd", hidden, w_down, preferred_element_type=jnp.float32
    ).astype(jnp.bfloat16)
    returned = lax.all_to_all(produced, "expert", split_axis=0, concat_axis=0, tiled=True)
    d_in = lax.all_to_all(outgoing_grad, "expert", split_axis=0, concat_axis=0, tiled=True)
    d_hidden = jnp.einsum("secd,efd->secf", d_in, w_down, preferred_element_type=jnp.float32)
    part_down = jnp.einsum("secf,secd->efd", hidden, d_in, preferred_element_type=jnp.float32)
    sigmoid_g = jax.nn.sigmoid(gate_pre)
    d_gate = (d_hidden * up_pre * sigmoid_g * (1.0 + gate_pre * (1.0 - sigmoid_g))).astype(
        jnp.bfloat16
    )
    d_up = (d_hidden * activated).astype(jnp.bfloat16)
    part_gate = jnp.einsum("secd,secf->edf", arrived, d_gate, preferred_element_type=jnp.float32)
    part_up = jnp.einsum("secd,secf->edf", arrived, d_up, preferred_element_type=jnp.float32)
    d_rows = (
        jnp.einsum("secf,edf->secd", d_gate, w_gate, preferred_element_type=jnp.float32)
        + jnp.einsum("secf,edf->secd", d_up, w_up, preferred_element_type=jnp.float32)
    ).astype(jnp.bfloat16)
    back = lax.all_to_all(d_rows, "expert", split_axis=0, concat_axis=0, tiled=True)
    per_slot = returned.reshape(experts * capacity, features)[target]
    per_slot = per_slot.reshape(tok_rows, per_token, features).astype(jnp.float32)
    output = jnp.sum(combine[:, :, None] * per_slot, axis=1).astype(jnp.bfloat16)
    d_combine = jnp.sum(per_slot * cot_float[:, None, :], axis=2)
    back_slot = back.reshape(experts * capacity, features)[target]
    back_slot = back_slot.reshape(tok_rows, per_token, features).astype(jnp.float32)
    d_tokens = jnp.sum(back_slot, axis=1).astype(jnp.bfloat16)
    sum_gate, sum_up, sum_down = (
        lax.psum_scatter(
            part_gate.astype(jnp.bfloat16), "dp", scatter_dimension=1, tiled=True
        ).astype(jnp.float32),
        lax.psum_scatter(
            part_up.astype(jnp.bfloat16), "dp", scatter_dimension=1, tiled=True
        ).astype(jnp.float32),
        lax.psum_scatter(
            part_down.astype(jnp.bfloat16), "dp", scatter_dimension=2, tiled=True
        ).astype(jnp.float32),
    )
    d_w_down = sum_down.astype(jnp.bfloat16)
    return (
        output,
        d_tokens,
        d_combine,
        sum_gate.astype(jnp.bfloat16),
        sum_up.astype(jnp.bfloat16),
        d_w_down,
    )


RING = (0, 1, 3, 5, 7, 6, 4, 2)


def ring_perms():
    n = len(RING)
    fwd = [(RING[i], RING[(i + 1) % n]) for i in range(n)]
    bwd = [(RING[(i + 1) % n], RING[i]) for i in range(n)]
    return fwd, bwd


def ring_sources():
    n = len(RING)
    place = {e: i for i, e in enumerate(RING)}
    steps = (0, -1, 1, -2, 2, -3, 3, 4)
    return [[RING[(place[e] + r) % n] for r in steps] for e in range(n)]


def forward(value):
    return lax.ppermute(value, "expert", ring_perms()[0])


def backward(value):
    return lax.ppermute(value, "expert", ring_perms()[1])


def tie(*values):
    return lax.optimization_barrier(values)


def add_rounded(a, b):
    return (a.astype(jnp.float32) + b.astype(jnp.float32)).astype(jnp.bfloat16)


def core_swap(away):
    n = lax.axis_size("dp")
    return lax.ppermute(away, "dp", [(j, j ^ 1) for j in range(n)])


def pick(halves, y):
    return lax.dynamic_index_in_dim(halves, y, 0, keepdims=False)


def y_parts(kept, got):
    y = lax.axis_index("dp") // 2
    half = kept.shape[1] // 2
    kept, got = pick(kept, 1 - y), pick(got, 1 - y)
    return add_rounded(kept[:half], got[:half]), add_rounded(kept[half:], got[half:])


def y_swap(other):
    n = lax.axis_size("dp")
    return lax.ppermute(other, "dp", [(j, j ^ 2) for j in range(n)])


ANY = pl.BlockSpec(memory_space=pl.ANY)
KERNEL_VMEM = 60 * 1024 * 1024
EXPERT_VMEM = 40 * 1024 * 1024
EXTRA = 16


class Mover:
    def __init__(self, sems):
        self.sems = sems
        self.used = 0

    def go(self, src, dst):
        copy = pltpu.make_async_copy(src, dst, self.sems.at[self.used])
        self.used += 1
        copy.start()
        return copy


def gradient_kernel(part, spots, tall_spots, core, *refs):
    n, m = len(spots), len(tall_spots)
    wide, narrow, refs = refs[:n], refs[n:n + m], refs[n + m:]
    away, kept, xs, st, ov, sems = refs
    quarters, _, size = xs.shape
    move = Mover(sems)
    load_s = [
        move.go(r, st.at[pl.ds(top, r.shape[0]), pl.ds(at, r.shape[1])])
        for r, (top, at) in zip(narrow, tall_spots)
    ]
    load_x = []
    for i in range(quarters):
        c = core[0] if i >= quarters // 2 else 1 - core[0]
        first = pl.multiple_of(((i % (quarters // 2)) * 2 + c) * size, size)
        load_x.append([
            move.go(r.at[pl.ds(0, part), pl.ds(first, size)], xs.at[i, pl.ds(at, part)])
            for r, at in zip(wide, spots)
        ])
    for c in load_s:
        c.wait()
    stores = []
    for i in range(quarters):
        for c in load_x[i]:
            c.wait()
        for f in range(0, st.shape[0], 256):
            ov[i, f:f + 256, :] = jnp.dot(
                st[f:f + 256, :], xs[i], preferred_element_type=jnp.float32
            ).astype(jnp.bfloat16)
        half = quarters // 2
        stores.append(move.go(ov.at[i], away.at[i] if i < half else kept.at[i - half]))
    for c in stores:
        c.wait()


FREE = pl.CostEstimate(flops=0, bytes_accessed=0, transcendentals=0)


def gradient(wide, part, narrows, name):
    n_dp = lax.axis_size("dp")
    spots, at = [part * i for i in range(len(wide))], part * len(wide)
    flat, tall_spots, tall = [], [], 0
    for pieces in narrows:
        col = 0
        for piece in pieces:
            flat.append(piece)
            tall_spots.append((tall, col))
            col += piece.shape[1]
        tall += pieces[0].shape[0]
    size = wide[0].shape[1] // n_dp
    half = jax.ShapeDtypeStruct((n_dp // 2, tall, size), jnp.bfloat16)
    core = (lax.axis_index("dp") % 2).reshape(1)
    return pl.pallas_call(
        functools.partial(gradient_kernel, part, tuple(spots), tuple(tall_spots)),
        out_shape=[half, half],
        in_specs=[pl.BlockSpec(memory_space=pltpu.SMEM)] + [ANY] * (len(wide) + len(flat)),
        out_specs=[ANY, ANY],
        scratch_shapes=[
            pltpu.VMEM((n_dp, at, size), jnp.bfloat16),
            pltpu.VMEM((tall, at), jnp.bfloat16),
            pltpu.VMEM((n_dp, tall, size), jnp.bfloat16),
            pltpu.SemaphoreType.DMA((len(flat) + n_dp * len(wide) + n_dp,)),
        ],
        compiler_params=pltpu.CompilerParams(vmem_limit_bytes=KERNEL_VMEM),
        cost_estimate=FREE,
        name=name,
    )(core, *wide, *flat)


def total_of(*values):
    total = values[0].astype(jnp.float32)
    for v in values[1:]:
        total = total + v.astype(jnp.float32)
    return total.astype(jnp.bfloat16)


def pair_kernel(part_f, got_f, part_b, got_b, f, b):
    f[...] = total_of(part_f[...], got_f[...])
    b[...] = total_of(part_b[...], got_b[...])


def end_kernel(own_o, of, ob, own_t, tf, tb, o, t):
    o[...] = total_of(own_o[...], of[...], ob[...])
    t[...] = total_of(own_t[...], tf[...], tb[...])


def by_columns(kernel, operands, out_shapes, name):
    features = out_shapes[0][-1]
    steps = 2

    def spec(shape):
        block = tuple(shape[:-1]) + (features // steps,)
        return pl.BlockSpec(block, lambda i, n=len(shape): (0,) * (n - 1) + (i,))

    return pl.pallas_call(
        kernel,
        out_shape=[jax.ShapeDtypeStruct(s, jnp.bfloat16) for s in out_shapes],
        grid=(steps,),
        in_specs=[spec(v.shape) for v in operands],
        out_specs=[spec(s) for s in out_shapes],
        compiler_params=pltpu.CompilerParams(vmem_limit_bytes=KERNEL_VMEM),
        cost_estimate=FREE,
        name=name,
    )(*operands)


def last_add_kernel(turned, y, kept, got, last_0, last_1, out):
    half = last_0.shape[0]
    for i, last in enumerate((last_0, last_1)):
        rows = pl.ds(i * half, half)
        total = kept[0, rows].astype(jnp.float32) + got[0, rows].astype(jnp.float32)
        total = total + last[...].astype(jnp.float32)
        if turned:
            out[0, :, rows] = total.T.astype(jnp.bfloat16)
        else:
            out[0, rows] = total.astype(jnp.bfloat16)


def last_add(kept, got, lasts, turned, name):
    _, ff, size = kept.shape
    y = (lax.axis_index("dp") // 2).reshape(1)
    shape = (1, size, ff) if turned else (1, ff, size)
    half = pl.BlockSpec((1, ff, size), lambda i, y: (y[0], 0, 0))
    piece = pl.BlockSpec((ff // 2, size), lambda i, y: (0, 0))
    return pl.pallas_call(
        functools.partial(last_add_kernel, turned),
        out_shape=jax.ShapeDtypeStruct(shape, jnp.bfloat16),
        grid_spec=pltpu.PrefetchScalarGridSpec(
            num_scalar_prefetch=1,
            grid=(1,),
            in_specs=[half, half, piece, piece],
            out_specs=pl.BlockSpec(shape, lambda i, y: (0, 0, 0)),
        ),
        compiler_params=pltpu.CompilerParams(vmem_limit_bytes=KERNEL_VMEM),
        cost_estimate=FREE,
        name=name,
    )(y, kept, got, *lasts)


def with_weights_kernel(cot, routes, combine, out):
    rows, features = cot.shape
    out[:rows] = cot[...]
    line = lax.broadcasted_iota(jnp.int32, (EXTRA, rows), 0)
    weights = jnp.zeros((EXTRA, rows), jnp.float32)
    for k in range(routes.shape[0]):
        weights += jnp.where(routes[k:k + 1] == line, combine[k:k + 1], 0.0)
    wide = weights * 65537.0
    high = wide - (wide - weights)
    rest = weights - high
    wide = rest * 65537.0
    middle = wide - (wide - rest)
    out[rows:] = jnp.zeros((EXTRA, features), jnp.bfloat16)
    for i, term in enumerate((high, middle, rest - middle)):
        out[rows:, i * rows:(i + 1) * rows] = term.astype(jnp.bfloat16)


def with_weights(cot, routes, combine):
    return pl.pallas_call(
        with_weights_kernel,
        out_shape=jax.ShapeDtypeStruct((cot.shape[0] + EXTRA, cot.shape[1]), cot.dtype),
        cost_estimate=FREE,
        name="with_weights",
    )(cot, routes.T, combine.T)


def expert_kernel(n, me, *refs):
    xs, gs, refs = refs[:n], refs[n:2 * n], refs[2 * n:]
    wg, wu, wd, wdt, wgt, wut = refs[:6]
    outs, backs, refs = refs[6:6 + n], refs[6 + n:6 + 2 * n], refs[6 + 2 * n:]
    s_o, dg_o, du_o, comb_o = refs[:4]
    x2, g2, gv, uv, sv, dgv, duv, wb, wv, st, dgt, dut, ov, rv, sems = refs[4:]
    part = xs[0].shape[0]
    rows, features = x2.shape
    ff = gv.shape[1]
    f32, bf16 = jnp.float32, jnp.bfloat16
    move = Mover(sems)
    cols = [pl.ds(f, 256) for f in range(0, ff, 256)]
    wide = [pl.ds(d, 512) for d in range(0, features, 512)]
    spots = [pl.ds(i * part, part) for i in range(n)]

    load_x = [move.go(r, x2.at[s]) for r, s in zip(xs, spots)]
    span = wb.shape[2]
    load_w = [move.go(r.at[pl.ds(part, EXTRA), pl.ds(0, span)], wb.at[i]) for i, r in enumerate(gs)]
    load_cot = [move.go(r.at[pl.ds(0, part)], g2.at[s]) for r, s in zip(gs, spots)]
    for c in load_w:
        c.wait()
    for i, s in enumerate(spots):
        terms = wb[i].astype(f32)
        mine = lax.broadcasted_iota(jnp.int32, terms.shape, 0) == me[0]
        terms = jnp.sum(jnp.where(mine, terms, 0.0), axis=0, keepdims=True)
        terms = terms[:, :part] + terms[:, part:2 * part] + terms[:, 2 * part:]
        wv[s, :] = jnp.broadcast_to(terms, (128, part)).T[:, :1]
    for c in load_x:
        c.wait()
    for c in cols:
        gv[:, c] = jnp.dot(x2[...], wg[:, c], preferred_element_type=f32)
    for c in cols:
        up = jnp.dot(x2[...], wu[:, c], preferred_element_type=f32)
        uv[:, c] = up
        gate = gv[:, c]
        scaled = (gate * jax.nn.sigmoid(gate) * up * wv[...]).astype(bf16)
        sv[:, c] = scaled
        st[c, :] = scaled.T
    stores = [move.go(st, s_o)]
    for c in wide:
        ov[:, c] = jnp.dot(sv[...], wd[:, c], preferred_element_type=f32).astype(bf16)
    stores += [move.go(ov.at[s], r) for r, s in zip(outs, spots)]
    for c in load_cot:
        c.wait()
    comb = jnp.zeros((rows, 1), f32)
    for c in cols:
        d_raw = jnp.dot(g2[...], wdt[:, c], preferred_element_type=f32)
        gate, up = gv[:, c], uv[:, c]
        sig = jax.nn.sigmoid(gate)
        act = gate * sig
        comb += jnp.sum(act * up * d_raw, axis=1, keepdims=True)
        d_hidden = d_raw * wv[...]
        d_gate = (d_hidden * up * sig * (1.0 + gate * (1.0 - sig))).astype(bf16)
        d_up = (d_hidden * act).astype(bf16)
        dgv[:, c] = d_gate
        duv[:, c] = d_up
        dgt[c, :] = d_gate.T
        dut[c, :] = d_up.T
    comb_o[...] = jnp.broadcast_to(comb, (rows, 128)).T[:1, :]
    stores += [move.go(dgt, dg_o), move.go(dut, du_o)]
    for c in wide:
        rv[:, c] = (
            jnp.dot(dgv[...], wgt[:, c], preferred_element_type=f32)
            + jnp.dot(duv[...], wut[:, c], preferred_element_type=f32)
        ).astype(bf16)
    stores += [move.go(rv.at[s], r) for r, s in zip(backs, spots)]
    for c in stores:
        c.wait()


def expert(xs, gs, matrices, name):
    n, (part, features) = len(xs), xs[0].shape
    ff = matrices[0].shape[1]
    rows = n * part
    bf16, f32 = jnp.bfloat16, jnp.float32
    vmem = pl.BlockSpec(memory_space=pltpu.VMEM)
    block = jax.ShapeDtypeStruct((part, features), bf16)
    turned = jax.ShapeDtypeStruct((ff, rows), bf16)
    me = lax.axis_index("expert").reshape(1)
    res = pl.pallas_call(
        functools.partial(expert_kernel, n),
        out_shape=[block] * (2 * n) + [turned] * 3 + [jax.ShapeDtypeStruct((1, rows), f32)],
        in_specs=[pl.BlockSpec(memory_space=pltpu.SMEM)] + [ANY] * (2 * n) + [vmem] * 6,
        out_specs=[ANY] * (2 * n + 3) + [vmem],
        scratch_shapes=[
            pltpu.VMEM((rows, features), bf16),
            pltpu.VMEM((rows, features), bf16),
            pltpu.VMEM((rows, ff), f32),
            pltpu.VMEM((rows, ff), f32),
            pltpu.VMEM((rows, ff), bf16),
            pltpu.VMEM((rows, ff), bf16),
            pltpu.VMEM((rows, ff), bf16),
            pltpu.VMEM((n, EXTRA, 3 * part), bf16),
            pltpu.VMEM((rows, 1), f32),
            pltpu.VMEM((ff, rows), bf16),
            pltpu.VMEM((ff, rows), bf16),
            pltpu.VMEM((ff, rows), bf16),
            pltpu.VMEM((rows, features), bf16),
            pltpu.VMEM((rows, features), bf16),
            pltpu.SemaphoreType.DMA((5 * n + 3,)),
        ],
        compiler_params=pltpu.CompilerParams(vmem_limit_bytes=EXPERT_VMEM),
        cost_estimate=FREE,
        name=name,
    )(me, *xs, *gs, *matrices)
    return res[:n], res[n:2 * n], res[2 * n:]


def gathered_plan(tokens, routes, combine, cotangent, w_gate, w_up, w_down):
    tok_rows, features = tokens.shape
    groups = lax.axis_size("expert")
    me = lax.axis_index("expert")
    chosen = routes[:, :, None] == jnp.arange(groups, dtype=jnp.int32)[None, None, :]
    matrices = [w_gate[0], w_up[0], w_down[0], w_down[0].T, w_gate[0].T, w_up[0].T]

    xs = [forward(tokens), backward(tokens)]
    both = with_weights(cotangent, routes, combine)
    gs = [forward(both), backward(both)]
    *moving, m3, m4, m5 = tie(*xs, *gs, *matrices[3:])
    matrices = matrices[:3] + [m3, m4, m5]
    all_x, all_g, outs, backs, smalls = [], [], [], [], []
    for step in range(1, 5):
        if step < 4:
            here_x, here_g = moving[:2], moving[2:]
        else:
            here_x, here_g = moving[:1], moving[1:]
        if step < 3:
            moving = [forward(here_x[0]), backward(here_x[1]), forward(here_g[0]), backward(here_g[1])]
        elif step == 3:
            moving = [forward(here_x[0]), backward(here_g[1])]
        else:
            moving = [forward(backs[6]), backward(outs[5])]
        if step == 1:
            here_x, here_g = [tokens, *here_x], [both, *here_g]
        out, back, small = expert(here_x, here_g, matrices, f"expert_{step}")
        *moving, first = tie(*moving, small[0])
        all_x += here_x
        all_g += here_g
        outs += out
        backs += back
        smalls.append([first, *small[1:]])

    scaled, d_gate, d_up, combs = (list(v) for v in zip(*smalls))
    two = [tokens.shape] * 2

    def summed(part_f, got_f, part_b, got_b, name):
        return by_columns(pair_kernel, [part_f, got_f, part_b, got_b], two, name)

    tf, ob = moving
    of, tb = forward(outs[7]), backward(backs[7])
    tf, ob = summed(backs[4], tf, outs[3], ob, "sum_a2")
    away_d, kept_d = gradient(all_g, tok_rows, [scaled], "grad_down")
    of, tb, tf, ob, away_d, d_gate[-1] = tie(of, tb, tf, ob, away_d, d_gate[-1])

    tf, ob, got_d = forward(tf), backward(ob), core_swap(away_d)
    of, tb = summed(outs[6], of, backs[5], tb, "sum_b3")
    first_d, other_d = y_parts(kept_d, got_d)
    first_d = y_swap(first_d)
    away_g, kept_g = gradient(all_x, tok_rows, [d_gate], "grad_gate")
    tf, ob, of, tb, away_g, d_up[-1], first_d, other_d = tie(
        tf, ob, of, tb, away_g, d_up[-1], first_d, other_d
    )

    of, tb, got_g, other_d = forward(of), backward(tb), core_swap(away_g), y_swap(other_d)
    tf, ob = summed(backs[2], tf, outs[1], ob, "sum_a1")
    first_g, other_g = y_parts(kept_g, got_g)
    away_u, kept_u = gradient(all_x, tok_rows, [d_up], "grad_up")
    of, tb, tf, ob, away_u, other_d, first_g, other_g, combs[-1] = tie(
        of, tb, tf, ob, away_u, other_d, first_g, other_g, combs[-1]
    )

    tf, ob, got_u, first_g = forward(tf), backward(ob), core_swap(away_u), y_swap(first_g)
    of, tb = summed(outs[4], of, backs[3], tb, "sum_b2")
    d_w_down = last_add(kept_d, got_d, [first_d, other_d], False, "sum_down")
    first_u, other_u = y_parts(kept_u, got_u)
    d_comb = jnp.concatenate(combs, axis=1).reshape(groups, tok_rows)
    table = ring_sources()
    inverse = jnp.asarray([[row.index(e) for e in range(groups)] for row in table], jnp.int32)[me]
    returned = lax.all_to_all(d_comb[inverse], "expert", split_axis=0, concat_axis=0, tiled=True)
    tf, ob, of, tb, first_g, first_u, other_u = tie(tf, ob, of, tb, first_g, first_u, other_u)

    of, tb, other_g = forward(of), backward(tb), y_swap(other_g)
    first_u = y_swap(first_u)
    of, tb, other_g, returned = tie(of, tb, other_g, returned)

    of, tb = summed(outs[2], of, backs[1], tb, "sum_b1")
    of, tb, other_u = forward(of), backward(tb), y_swap(other_u)
    d_w_gate = last_add(kept_g, got_g, [first_g, other_g], True, "sum_gate")
    d_combine = jnp.sum(jnp.where(chosen, returned.T[:, None, :], 0.0), axis=2)
    d_w_up = last_add(kept_u, got_u, [first_u, other_u], True, "sum_up")
    output, d_tokens = by_columns(
        end_kernel, [outs[0], of, ob, backs[0], tf, tb], two, "sum_end"
    )
    return output, d_tokens, d_combine, d_w_gate, d_w_up, d_w_down


def solution(mesh):
    rows = P(("dp", "expert"), None)
    small = mesh.shape["expert"] == len(RING) and mesh.shape["dp"] == 4
    return jax.shard_map(
        gathered_plan if small else routed_plan,
        mesh=mesh,
        in_specs=(rows, rows, rows, rows) + (P("expert", None, None),) * 3,
        out_specs=(
            rows,
            rows,
            rows,
            P("expert", "dp", None),
            P("expert", "dp", None),
            P("expert", None, "dp"),
        ),
        check_vma=False,
    )
```

```python
import functools
import jax
import jax.numpy as jnp
from jax import lax
from jax.experimental import pallas as pl
from jax.experimental.pallas import tpu as pltpu
from jax.sharding import PartitionSpec as P


def slot_map(routes, experts, capacity):
    flat_ids = routes.reshape(-1)
    onehot = (flat_ids[:, None] == jnp.arange(experts, dtype=jnp.int32)[None, :]).astype(jnp.int32)
    before = jnp.cumsum(onehot, axis=0) - onehot
    slots = jnp.sum(before * onehot, axis=1)
    target = flat_ids * capacity + slots
    source = (
        jnp.full((experts * capacity,), -1, jnp.int32)
        .at[target]
        .set(jnp.arange(flat_ids.shape[0], dtype=jnp.int32))
    )
    return (target, source)


def routed_plan(tokens, routes, combine, cotangent, w_gate, w_up, w_down):
    tok_rows, features = tokens.shape
    per_token = routes.shape[1]
    groups = lax.axis_size("expert")
    local_exp = w_gate.shape[0]
    experts = local_exp * groups
    capacity = 3 * tok_rows * per_token // (2 * experts)
    target, source = slot_map(routes, experts, capacity)
    filled = (source >= 0)[:, None]
    pair_index = jnp.maximum(source, 0)
    owner_row = pair_index // per_token
    outgoing = jnp.where(filled, tokens[owner_row], jnp.zeros((), jnp.bfloat16))
    outgoing = outgoing.reshape(groups, local_exp, capacity, features)
    cot_float = cotangent.astype(jnp.float32)
    scaled = (combine[:, :, None] * cot_float[:, None, :]).reshape(tok_rows * per_token, features)
    outgoing_grad = jnp.where(filled, scaled[pair_index], 0.0).astype(jnp.bfloat16)
    outgoing_grad = outgoing_grad.reshape(groups, local_exp, capacity, features)
    arrived = lax.all_to_all(outgoing, "expert", split_axis=0, concat_axis=0, tiled=True)
    gate_pre = jnp.einsum("secd,edf->secf", arrived, w_gate, preferred_element_type=jnp.float32)
    up_pre = jnp.einsum("secd,edf->secf", arrived, w_up, preferred_element_type=jnp.float32)
    activated = jax.nn.silu(gate_pre)
    hidden = (activated * up_pre).astype(jnp.bfloat16)
    produced = jnp.einsum(
        "secf,efd->secd", hidden, w_down, preferred_element_type=jnp.float32
    ).astype(jnp.bfloat16)
    returned = lax.all_to_all(produced, "expert", split_axis=0, concat_axis=0, tiled=True)
    d_in = lax.all_to_all(outgoing_grad, "expert", split_axis=0, concat_axis=0, tiled=True)
    d_hidden = jnp.einsum("secd,efd->secf", d_in, w_down, preferred_element_type=jnp.float32)
    part_down = jnp.einsum("secf,secd->efd", hidden, d_in, preferred_element_type=jnp.float32)
    sigmoid_g = jax.nn.sigmoid(gate_pre)
    d_gate = (d_hidden * up_pre * sigmoid_g * (1.0 + gate_pre * (1.0 - sigmoid_g))).astype(
        jnp.bfloat16
    )
    d_up = (d_hidden * activated).astype(jnp.bfloat16)
    part_gate = jnp.einsum("secd,secf->edf", arrived, d_gate, preferred_element_type=jnp.float32)
    part_up = jnp.einsum("secd,secf->edf", arrived, d_up, preferred_element_type=jnp.float32)
    d_rows = (
        jnp.einsum("secf,edf->secd", d_gate, w_gate, preferred_element_type=jnp.float32)
        + jnp.einsum("secf,edf->secd", d_up, w_up, preferred_element_type=jnp.float32)
    ).astype(jnp.bfloat16)
    back = lax.all_to_all(d_rows, "expert", split_axis=0, concat_axis=0, tiled=True)
    per_slot = returned.reshape(experts * capacity, features)[target]
    per_slot = per_slot.reshape(tok_rows, per_token, features).astype(jnp.float32)
    output = jnp.sum(combine[:, :, None] * per_slot, axis=1).astype(jnp.bfloat16)
    d_combine = jnp.sum(per_slot * cot_float[:, None, :], axis=2)
    back_slot = back.reshape(experts * capacity, features)[target]
    back_slot = back_slot.reshape(tok_rows, per_token, features).astype(jnp.float32)
    d_tokens = jnp.sum(back_slot, axis=1).astype(jnp.bfloat16)
    sum_gate, sum_up, sum_down = (
        lax.psum_scatter(
            part_gate.astype(jnp.bfloat16), "dp", scatter_dimension=1, tiled=True
        ).astype(jnp.float32),
        lax.psum_scatter(
            part_up.astype(jnp.bfloat16), "dp", scatter_dimension=1, tiled=True
        ).astype(jnp.float32),
        lax.psum_scatter(
            part_down.astype(jnp.bfloat16), "dp", scatter_dimension=2, tiled=True
        ).astype(jnp.float32),
    )
    d_w_down = sum_down.astype(jnp.bfloat16)
    return (
        output,
        d_tokens,
        d_combine,
        sum_gate.astype(jnp.bfloat16),
        sum_up.astype(jnp.bfloat16),
        d_w_down,
    )


RING = (0, 1, 3, 5, 7, 6, 4, 2)


def ring_perms():
    n = len(RING)
    fwd = [(RING[i], RING[(i + 1) % n]) for i in range(n)]
    bwd = [(RING[(i + 1) % n], RING[i]) for i in range(n)]
    return fwd, bwd


def ring_sources():
    n = len(RING)
    place = {e: i for i, e in enumerate(RING)}
    steps = (0, -1, 1, -2, 2, -3, 3, 4)
    return [[RING[(place[e] + r) % n] for r in steps] for e in range(n)]


def forward(value):
    return lax.ppermute(value, "expert", ring_perms()[0])


def backward(value):
    return lax.ppermute(value, "expert", ring_perms()[1])


def tie(*values):
    return lax.optimization_barrier(values)


def add_rounded(a, b):
    return (a.astype(jnp.float32) + b.astype(jnp.float32)).astype(jnp.bfloat16)


def core_swap(away):
    n = lax.axis_size("dp")
    return lax.ppermute(away, "dp", [(j, j ^ 1) for j in range(n)])


def pick(halves, y):
    return lax.dynamic_index_in_dim(halves, y, 0, keepdims=False)


def y_parts(kept, got):
    y = lax.axis_index("dp") // 2
    half = kept.shape[1] // 2
    kept, got = pick(kept, 1 - y), pick(got, 1 - y)
    return add_rounded(kept[:half], got[:half]), add_rounded(kept[half:], got[half:])


def y_swap(other):
    n = lax.axis_size("dp")
    return lax.ppermute(other, "dp", [(j, j ^ 2) for j in range(n)])


ANY = pl.BlockSpec(memory_space=pl.ANY)
KERNEL_VMEM = 60 * 1024 * 1024
EXTRA = 16


class Mover:
    def __init__(self, sems):
        self.sems = sems
        self.used = 0

    def go(self, src, dst):
        copy = pltpu.make_async_copy(src, dst, self.sems.at[self.used])
        self.used += 1
        copy.start()
        return copy


def gradient_kernel(part, spots, tall_spots, core, *refs):
    n, m = len(spots), len(tall_spots)
    wide, narrow, refs = refs[:n], refs[n:n + m], refs[n + m:]
    away, kept, xs, st, ov, sems = refs
    quarters, _, size = xs.shape
    move = Mover(sems)
    load_s = [
        move.go(r, st.at[pl.ds(top, r.shape[0]), pl.ds(at, r.shape[1])])
        for r, (top, at) in zip(narrow, tall_spots)
    ]

    def load_quarter(i):
        c = core[0] if i >= quarters // 2 else 1 - core[0]
        first = pl.multiple_of(((i % (quarters // 2)) * 2 + c) * size, size)
        return [
            move.go(r.at[pl.ds(0, part), pl.ds(first, size)], xs.at[i, pl.ds(at, part)])
            for r, at in zip(wide, spots)
        ]

    load_x = [load_quarter(0), load_quarter(1)]
    for c in load_s:
        c.wait()
    stores = []
    for i in range(quarters):
        for c in load_x[i]:
            c.wait()
        if i + 2 < quarters:
            load_x.append(load_quarter(i + 2))
        for f in range(0, st.shape[0], 256):
            ov[i, f:f + 256, :] = jnp.dot(
                st[f:f + 256, :], xs[i], preferred_element_type=jnp.float32
            ).astype(jnp.bfloat16)
        half = quarters // 2
        stores.append(move.go(ov.at[i], away.at[i] if i < half else kept.at[i - half]))
    for c in stores:
        c.wait()


FREE = pl.CostEstimate(flops=0, bytes_accessed=0, transcendentals=0)


def gradient(wide, part, narrows, name):
    n_dp = lax.axis_size("dp")
    spots, at = [part * i for i in range(len(wide))], part * len(wide)
    flat, tall_spots, tall = [], [], 0
    for pieces in narrows:
        col = 0
        for piece in pieces:
            flat.append(piece)
            tall_spots.append((tall, col))
            col += piece.shape[1]
        tall += pieces[0].shape[0]
    size = wide[0].shape[1] // n_dp
    half = jax.ShapeDtypeStruct((n_dp // 2, tall, size), jnp.bfloat16)
    core = (lax.axis_index("dp") % 2).reshape(1)
    return pl.pallas_call(
        functools.partial(gradient_kernel, part, tuple(spots), tuple(tall_spots)),
        out_shape=[half, half],
        in_specs=[pl.BlockSpec(memory_space=pltpu.SMEM)] + [ANY] * (len(wide) + len(flat)),
        out_specs=[ANY, ANY],
        scratch_shapes=[
            pltpu.VMEM((n_dp, at, size), jnp.bfloat16),
            pltpu.VMEM((tall, at), jnp.bfloat16),
            pltpu.VMEM((n_dp, tall, size), jnp.bfloat16),
            pltpu.SemaphoreType.DMA((len(flat) + n_dp * len(wide) + n_dp,)),
        ],
        compiler_params=pltpu.CompilerParams(vmem_limit_bytes=KERNEL_VMEM),
        cost_estimate=FREE,
        name=name,
    )(core, *wide, *flat)


def total_of(*values):
    total = values[0].astype(jnp.float32)
    for v in values[1:]:
        total = total + v.astype(jnp.float32)
    return total.astype(jnp.bfloat16)


def pair_kernel(part_f, got_f, part_b, got_b, f, b):
    f[...] = total_of(part_f[...], got_f[...])
    b[...] = total_of(part_b[...], got_b[...])


def end_kernel(own_o, of, ob, own_t, tf, tb, o, t):
    o[...] = total_of(own_o[...], of[...], ob[...])
    t[...] = total_of(own_t[...], tf[...], tb[...])


def by_columns(kernel, operands, out_shapes, name):
    features = out_shapes[0][-1]
    steps = 2

    def spec(shape):
        block = tuple(shape[:-1]) + (features // steps,)
        return pl.BlockSpec(block, lambda i, n=len(shape): (0,) * (n - 1) + (i,))

    return pl.pallas_call(
        kernel,
        out_shape=[jax.ShapeDtypeStruct(s, jnp.bfloat16) for s in out_shapes],
        grid=(steps,),
        in_specs=[spec(v.shape) for v in operands],
        out_specs=[spec(s) for s in out_shapes],
        compiler_params=pltpu.CompilerParams(vmem_limit_bytes=KERNEL_VMEM),
        cost_estimate=FREE,
        name=name,
    )(*operands)


def last_add_kernel(turned, y, kept, got, last_0, last_1, out):
    half = last_0.shape[0]
    for i, last in enumerate((last_0, last_1)):
        rows = pl.ds(i * half, half)
        total = kept[0, rows].astype(jnp.float32) + got[0, rows].astype(jnp.float32)
        total = total + last[...].astype(jnp.float32)
        if turned:
            out[0, :, rows] = total.T.astype(jnp.bfloat16)
        else:
            out[0, rows] = total.astype(jnp.bfloat16)


def last_add(kept, got, lasts, turned, name):
    _, ff, size = kept.shape
    y = (lax.axis_index("dp") // 2).reshape(1)
    shape = (1, size, ff) if turned else (1, ff, size)
    half = pl.BlockSpec((1, ff, size), lambda i, y: (y[0], 0, 0))
    piece = pl.BlockSpec((ff // 2, size), lambda i, y: (0, 0))
    return pl.pallas_call(
        functools.partial(last_add_kernel, turned),
        out_shape=jax.ShapeDtypeStruct(shape, jnp.bfloat16),
        grid_spec=pltpu.PrefetchScalarGridSpec(
            num_scalar_prefetch=1,
            grid=(1,),
            in_specs=[half, half, piece, piece],
            out_specs=pl.BlockSpec(shape, lambda i, y: (0, 0, 0)),
        ),
        compiler_params=pltpu.CompilerParams(vmem_limit_bytes=KERNEL_VMEM),
        cost_estimate=FREE,
        name=name,
    )(y, kept, got, *lasts)


def with_weights_kernel(cot, routes, combine, out):
    rows, features = cot.shape
    out[:rows] = cot[...]
    line = lax.broadcasted_iota(jnp.int32, (EXTRA, rows), 0)
    weights = jnp.zeros((EXTRA, rows), jnp.float32)
    for k in range(routes.shape[0]):
        weights += jnp.where(routes[k:k + 1] == line, combine[k:k + 1], 0.0)
    wide = weights * 65537.0
    high = wide - (wide - weights)
    rest = weights - high
    wide = rest * 65537.0
    middle = wide - (wide - rest)
    out[rows:] = jnp.zeros((EXTRA, features), jnp.bfloat16)
    for i, term in enumerate((high, middle, rest - middle)):
        out[rows:, i * rows:(i + 1) * rows] = term.astype(jnp.bfloat16)


def with_weights(cot, routes, combine):
    return pl.pallas_call(
        with_weights_kernel,
        out_shape=jax.ShapeDtypeStruct((cot.shape[0] + EXTRA, cot.shape[1]), cot.dtype),
        cost_estimate=FREE,
        name="with_weights",
    )(cot, routes.T, combine.T)


def expert_kernel(n, me, *refs):
    xs, gs, refs = refs[:n], refs[n:2 * n], refs[2 * n:]
    wg, wu, wd, wdt, wgt, wut = refs[:6]
    outs, backs, refs = refs[6:6 + n], refs[6 + n:6 + 2 * n], refs[6 + 2 * n:]
    s_o, dg_o, du_o, comb_o = refs[:4]
    x2, g2, wgv, wuv, wdv, wdtv, wgtv, wutv, gv, uv, sv, dgv, duv, wb, wv, st, dgt, dut, ov, rv, sems = refs[4:]
    part = xs[0].shape[0]
    rows, features = x2.shape
    ff = gv.shape[1]
    f32, bf16 = jnp.float32, jnp.bfloat16
    move = Mover(sems)
    cols = [pl.ds(f, 256) for f in range(0, ff, 256)]
    wide = [pl.ds(d, 512) for d in range(0, features, 512)]
    spots = [pl.ds(i * part, part) for i in range(n)]

    def load(src, dst, pieces):
        size = src.shape[0] // pieces
        return [
            move.go(src.at[pl.ds(i * size, size)], dst.at[pl.ds(i * size, size)])
            for i in range(pieces)
        ]

    load_x = [move.go(r, x2.at[s]) for r, s in zip(xs, spots)]
    span = wb.shape[2]
    load_w = [move.go(r.at[pl.ds(part, EXTRA), pl.ds(0, span)], wb.at[i]) for i, r in enumerate(gs)]
    load_g = load(wg, wgv, 4)
    load_u = load(wu, wuv, 4)
    load_cot = [move.go(r.at[pl.ds(0, part)], g2.at[s]) for r, s in zip(gs, spots)]
    load_d = load(wd, wdv, 4)
    load_dt = load(wdt, wdtv, 4)
    load_gt = load(wgt, wgtv, 4)
    load_ut = load(wut, wutv, 4)
    for c in load_w:
        c.wait()
    for i, s in enumerate(spots):
        terms = wb[i].astype(f32)
        mine = lax.broadcasted_iota(jnp.int32, terms.shape, 0) == me[0]
        terms = jnp.sum(jnp.where(mine, terms, 0.0), axis=0, keepdims=True)
        terms = terms[:, :part] + terms[:, part:2 * part] + terms[:, 2 * part:]
        wv[s, :] = jnp.broadcast_to(terms, (128, part)).T[:, :1]
    for c in load_x + load_g:
        c.wait()
    for c in cols:
        gv[:, c] = jnp.dot(x2[...], wgv[:, c], preferred_element_type=f32)
    for c in load_u:
        c.wait()
    for c in cols:
        up = jnp.dot(x2[...], wuv[:, c], preferred_element_type=f32)
        uv[:, c] = up
        gate = gv[:, c]
        scaled = (gate * jax.nn.sigmoid(gate) * up * wv[...]).astype(bf16)
        sv[:, c] = scaled
        st[c, :] = scaled.T
    stores = [move.go(st, s_o)]
    for c in load_d:
        c.wait()
    for c in wide:
        ov[:, c] = jnp.dot(sv[...], wdv[:, c], preferred_element_type=f32).astype(bf16)
    stores += [move.go(ov.at[s], r) for r, s in zip(outs, spots)]
    for c in load_cot + load_dt:
        c.wait()
    comb = jnp.zeros((rows, 1), f32)
    for c in cols:
        d_raw = jnp.dot(g2[...], wdtv[:, c], preferred_element_type=f32)
        gate, up = gv[:, c], uv[:, c]
        sig = jax.nn.sigmoid(gate)
        act = gate * sig
        comb += jnp.sum(act * up * d_raw, axis=1, keepdims=True)
        d_hidden = d_raw * wv[...]
        d_gate = (d_hidden * up * sig * (1.0 + gate * (1.0 - sig))).astype(bf16)
        d_up = (d_hidden * act).astype(bf16)
        dgv[:, c] = d_gate
        duv[:, c] = d_up
        dgt[c, :] = d_gate.T
        dut[c, :] = d_up.T
    comb_o[...] = jnp.broadcast_to(comb, (rows, 128)).T[:1, :]
    stores += [move.go(dgt, dg_o), move.go(dut, du_o)]
    for c in load_gt + load_ut:
        c.wait()
    for c in wide:
        rv[:, c] = (
            jnp.dot(dgv[...], wgtv[:, c], preferred_element_type=f32)
            + jnp.dot(duv[...], wutv[:, c], preferred_element_type=f32)
        ).astype(bf16)
    stores += [move.go(rv.at[s], r) for r, s in zip(backs, spots)]
    for c in stores:
        c.wait()


def expert(xs, gs, matrices, name):
    n, (part, features) = len(xs), xs[0].shape
    ff = matrices[0].shape[1]
    rows = n * part
    bf16, f32 = jnp.bfloat16, jnp.float32
    vmem = pl.BlockSpec(memory_space=pltpu.VMEM)
    block = jax.ShapeDtypeStruct((part, features), bf16)
    turned = jax.ShapeDtypeStruct((ff, rows), bf16)
    me = lax.axis_index("expert").reshape(1)
    res = pl.pallas_call(
        functools.partial(expert_kernel, n),
        out_shape=[block] * (2 * n) + [turned] * 3 + [jax.ShapeDtypeStruct((1, rows), f32)],
        in_specs=[pl.BlockSpec(memory_space=pltpu.SMEM)] + [ANY] * (2 * n + 6),
        out_specs=[ANY] * (2 * n + 3) + [vmem],
        scratch_shapes=[
            pltpu.VMEM((rows, features), bf16),
            pltpu.VMEM((rows, features), bf16),
            pltpu.VMEM((features, ff), bf16),
            pltpu.VMEM((features, ff), bf16),
            pltpu.VMEM((ff, features), bf16),
            pltpu.VMEM((features, ff), bf16),
            pltpu.VMEM((ff, features), bf16),
            pltpu.VMEM((ff, features), bf16),
            pltpu.VMEM((rows, ff), f32),
            pltpu.VMEM((rows, ff), f32),
            pltpu.VMEM((rows, ff), bf16),
            pltpu.VMEM((rows, ff), bf16),
            pltpu.VMEM((rows, ff), bf16),
            pltpu.VMEM((n, EXTRA, 3 * part), bf16),
            pltpu.VMEM((rows, 1), f32),
            pltpu.VMEM((ff, rows), bf16),
            pltpu.VMEM((ff, rows), bf16),
            pltpu.VMEM((ff, rows), bf16),
            pltpu.VMEM((rows, features), bf16),
            pltpu.VMEM((rows, features), bf16),
            pltpu.SemaphoreType.DMA((5 * n + 27,)),
        ],
        compiler_params=pltpu.CompilerParams(vmem_limit_bytes=KERNEL_VMEM),
        cost_estimate=FREE,
        name=name,
    )(me, *xs, *gs, *matrices)
    return res[:n], res[n:2 * n], res[2 * n:]


def gathered_plan(tokens, routes, combine, cotangent, w_gate, w_up, w_down):
    tok_rows, features = tokens.shape
    groups = lax.axis_size("expert")
    me = lax.axis_index("expert")
    chosen = routes[:, :, None] == jnp.arange(groups, dtype=jnp.int32)[None, None, :]
    matrices = [w_gate[0], w_up[0], w_down[0], w_down[0].T, w_gate[0].T, w_up[0].T]

    xs = [forward(tokens), backward(tokens)]
    both = with_weights(cotangent, routes, combine)
    gs = [forward(both), backward(both)]
    gf, gb, m3, m4, m5 = tie(*gs, *matrices[3:])
    matrices = matrices[:3] + [m3, m4, m5]
    xf, xb = xs
    all_x, all_g, outs, backs, smalls = [], [], [], [], []
    for step in range(1, 5):
        here_x, here_g = [xf, xb], [gf, gb]
        if step < 3:
            gf, gb = forward(gf), backward(gb)
            xf, xb = forward(xf), backward(xb)
        elif step == 3:
            gb, xf = backward(gb), forward(xf)
        else:
            here_x, here_g = [xf], [gb]
            tf, ob = forward(backs[6]), backward(outs[5])
        if step == 1:
            here_x, here_g = [tokens, *here_x], [both, *here_g]
        out, back, small = expert(here_x, here_g, matrices, f"expert_{step}")
        if step < 3:
            gf, gb, first = tie(gf, gb, small[0])
            xf, xb, first = tie(xf, xb, first)
        elif step == 3:
            gb, xf, first = tie(gb, xf, small[0])
        else:
            tf, ob, first = tie(tf, ob, small[0])
        all_x += here_x
        all_g += here_g
        outs += out
        backs += back
        smalls.append([first, *small[1:]])

    scaled, d_gate, d_up, combs = (list(v) for v in zip(*smalls))
    two = [tokens.shape] * 2

    def summed(part_f, got_f, part_b, got_b, name):
        return by_columns(pair_kernel, [part_f, got_f, part_b, got_b], two, name)

    of, tb = forward(outs[7]), backward(backs[7])
    tf, ob = summed(backs[4], tf, outs[3], ob, "sum_a2")
    away_d, kept_d = gradient(all_g, tok_rows, [scaled], "grad_down")
    of, tb, tf, ob, away_d, d_gate[-1] = tie(of, tb, tf, ob, away_d, d_gate[-1])

    tf, ob, got_d = forward(tf), backward(ob), core_swap(away_d)
    of, tb = summed(outs[6], of, backs[5], tb, "sum_b3")
    first_d, other_d = y_parts(kept_d, got_d)
    first_d = y_swap(first_d)
    away_g, kept_g = gradient(all_x, tok_rows, [d_gate], "grad_gate")
    tf, ob, of, tb, away_g, d_up[-1], first_d, other_d = tie(
        tf, ob, of, tb, away_g, d_up[-1], first_d, other_d
    )

    of, tb, got_g, other_d = forward(of), backward(tb), core_swap(away_g), y_swap(other_d)
    first_g, other_g = y_parts(kept_g, got_g)
    first_g, other_g, d_up[-1] = tie(first_g, other_g, d_up[-1])
    first_g = y_swap(first_g)
    tf, ob = summed(backs[2], tf, outs[1], ob, "sum_a1")
    away_u, kept_u = gradient(all_x, tok_rows, [d_up], "grad_up")
    of, tb, tf, ob, away_u, other_d, first_g, other_g, combs[-1] = tie(
        of, tb, tf, ob, away_u, other_d, first_g, other_g, combs[-1]
    )

    tf, ob, got_u, other_g = forward(tf), backward(ob), core_swap(away_u), y_swap(other_g)
    of, tb = summed(outs[4], of, backs[3], tb, "sum_b2")
    d_w_down = last_add(kept_d, got_d, [first_d, other_d], False, "sum_down")
    first_u, other_u = y_parts(kept_u, got_u)
    d_comb = jnp.concatenate(combs, axis=1).reshape(groups, tok_rows)
    table = ring_sources()
    inverse = jnp.asarray([[row.index(e) for e in range(groups)] for row in table], jnp.int32)[me]
    d_comb = d_comb[inverse]
    tf, ob, of, tb, other_g, first_u, other_u, d_comb, d_w_down = tie(
        tf, ob, of, tb, other_g, first_u, other_u, d_comb, d_w_down
    )

    of, tb, first_u = forward(of), backward(tb), y_swap(first_u)
    d_w_gate = last_add(kept_g, got_g, [first_g, other_g], True, "sum_gate")
    d_comb, d_w_gate = tie(d_comb, d_w_gate)
    returned = lax.all_to_all(d_comb, "expert", split_axis=0, concat_axis=0, tiled=True)
    of, tb, first_u, returned = tie(of, tb, first_u, returned)

    of, tb = summed(outs[2], of, backs[1], tb, "sum_b1")
    of, tb, other_u = forward(of), backward(tb), y_swap(other_u)
    d_combine = jnp.sum(jnp.where(chosen, returned.T[:, None, :], 0.0), axis=2)
    d_w_up = last_add(kept_u, got_u, [first_u, other_u], True, "sum_up")
    output, d_tokens = by_columns(
        end_kernel, [outs[0], of, ob, backs[0], tf, tb], two, "sum_end"
    )
    return output, d_tokens, d_combine, d_w_gate, d_w_up, d_w_down


def solution(mesh):
    rows = P(("dp", "expert"), None)
    small = mesh.shape["expert"] == len(RING) and mesh.shape["dp"] == 4
    return jax.shard_map(
        gathered_plan if small else routed_plan,
        mesh=mesh,
        in_specs=(rows, rows, rows, rows) + (P("expert", None, None),) * 3,
        out_specs=(
            rows,
            rows,
            rows,
            P("expert", "dp", None),
            P("expert", "dp", None),
            P("expert", None, "dp"),
        ),
        check_vma=False,
    )
```

```python
import functools
import jax
import jax.numpy as jnp
from jax import lax
from jax.experimental import pallas as pl
from jax.experimental.pallas import tpu as pltpu
from jax.sharding import PartitionSpec as P


def slot_map(routes, experts, capacity):
    flat_ids = routes.reshape(-1)
    onehot = (flat_ids[:, None] == jnp.arange(experts, dtype=jnp.int32)[None, :]).astype(jnp.int32)
    before = jnp.cumsum(onehot, axis=0) - onehot
    slots = jnp.sum(before * onehot, axis=1)
    target = flat_ids * capacity + slots
    source = (
        jnp.full((experts * capacity,), -1, jnp.int32)
        .at[target]
        .set(jnp.arange(flat_ids.shape[0], dtype=jnp.int32))
    )
    return (target, source)


def routed_plan(tokens, routes, combine, cotangent, w_gate, w_up, w_down):
    tok_rows, features = tokens.shape
    per_token = routes.shape[1]
    groups = lax.axis_size("expert")
    local_exp = w_gate.shape[0]
    experts = local_exp * groups
    capacity = 3 * tok_rows * per_token // (2 * experts)
    target, source = slot_map(routes, experts, capacity)
    filled = (source >= 0)[:, None]
    pair_index = jnp.maximum(source, 0)
    owner_row = pair_index // per_token
    outgoing = jnp.where(filled, tokens[owner_row], jnp.zeros((), jnp.bfloat16))
    outgoing = outgoing.reshape(groups, local_exp, capacity, features)
    cot_float = cotangent.astype(jnp.float32)
    scaled = (combine[:, :, None] * cot_float[:, None, :]).reshape(tok_rows * per_token, features)
    outgoing_grad = jnp.where(filled, scaled[pair_index], 0.0).astype(jnp.bfloat16)
    outgoing_grad = outgoing_grad.reshape(groups, local_exp, capacity, features)
    arrived = lax.all_to_all(outgoing, "expert", split_axis=0, concat_axis=0, tiled=True)
    gate_pre = jnp.einsum("secd,edf->secf", arrived, w_gate, preferred_element_type=jnp.float32)
    up_pre = jnp.einsum("secd,edf->secf", arrived, w_up, preferred_element_type=jnp.float32)
    activated = jax.nn.silu(gate_pre)
    hidden = (activated * up_pre).astype(jnp.bfloat16)
    produced = jnp.einsum(
        "secf,efd->secd", hidden, w_down, preferred_element_type=jnp.float32
    ).astype(jnp.bfloat16)
    returned = lax.all_to_all(produced, "expert", split_axis=0, concat_axis=0, tiled=True)
    d_in = lax.all_to_all(outgoing_grad, "expert", split_axis=0, concat_axis=0, tiled=True)
    d_hidden = jnp.einsum("secd,efd->secf", d_in, w_down, preferred_element_type=jnp.float32)
    part_down = jnp.einsum("secf,secd->efd", hidden, d_in, preferred_element_type=jnp.float32)
    sigmoid_g = jax.nn.sigmoid(gate_pre)
    d_gate = (d_hidden * up_pre * sigmoid_g * (1.0 + gate_pre * (1.0 - sigmoid_g))).astype(
        jnp.bfloat16
    )
    d_up = (d_hidden * activated).astype(jnp.bfloat16)
    part_gate = jnp.einsum("secd,secf->edf", arrived, d_gate, preferred_element_type=jnp.float32)
    part_up = jnp.einsum("secd,secf->edf", arrived, d_up, preferred_element_type=jnp.float32)
    d_rows = (
        jnp.einsum("secf,edf->secd", d_gate, w_gate, preferred_element_type=jnp.float32)
        + jnp.einsum("secf,edf->secd", d_up, w_up, preferred_element_type=jnp.float32)
    ).astype(jnp.bfloat16)
    back = lax.all_to_all(d_rows, "expert", split_axis=0, concat_axis=0, tiled=True)
    per_slot = returned.reshape(experts * capacity, features)[target]
    per_slot = per_slot.reshape(tok_rows, per_token, features).astype(jnp.float32)
    output = jnp.sum(combine[:, :, None] * per_slot, axis=1).astype(jnp.bfloat16)
    d_combine = jnp.sum(per_slot * cot_float[:, None, :], axis=2)
    back_slot = back.reshape(experts * capacity, features)[target]
    back_slot = back_slot.reshape(tok_rows, per_token, features).astype(jnp.float32)
    d_tokens = jnp.sum(back_slot, axis=1).astype(jnp.bfloat16)
    sum_gate, sum_up, sum_down = (
        lax.psum_scatter(
            part_gate.astype(jnp.bfloat16), "dp", scatter_dimension=1, tiled=True
        ).astype(jnp.float32),
        lax.psum_scatter(
            part_up.astype(jnp.bfloat16), "dp", scatter_dimension=1, tiled=True
        ).astype(jnp.float32),
        lax.psum_scatter(
            part_down.astype(jnp.bfloat16), "dp", scatter_dimension=2, tiled=True
        ).astype(jnp.float32),
    )
    d_w_down = sum_down.astype(jnp.bfloat16)
    return (
        output,
        d_tokens,
        d_combine,
        sum_gate.astype(jnp.bfloat16),
        sum_up.astype(jnp.bfloat16),
        d_w_down,
    )


RING = (0, 1, 3, 5, 7, 6, 4, 2)


def ring_perms():
    n = len(RING)
    fwd = [(RING[i], RING[(i + 1) % n]) for i in range(n)]
    bwd = [(RING[(i + 1) % n], RING[i]) for i in range(n)]
    return fwd, bwd


def ring_sources():
    n = len(RING)
    place = {e: i for i, e in enumerate(RING)}
    steps = (0, -1, 1, -2, 2, -3, 3, 4)
    return [[RING[(place[e] + r) % n] for r in steps] for e in range(n)]


def forward(value):
    return lax.ppermute(value, "expert", ring_perms()[0])


def backward(value):
    return lax.ppermute(value, "expert", ring_perms()[1])


def tie(*values):
    return lax.optimization_barrier(values)


def add_rounded(a, b):
    return (a.astype(jnp.float32) + b.astype(jnp.float32)).astype(jnp.bfloat16)


def core_swap(away):
    n = lax.axis_size("dp")
    return lax.ppermute(away, "dp", [(j, j ^ 1) for j in range(n)])


def y_swap(other):
    n = lax.axis_size("dp")
    return lax.ppermute(other, "dp", [(j, j ^ 2) for j in range(n)])


ANY = pl.BlockSpec(memory_space=pl.ANY)
KERNEL_VMEM = 60 * 1024 * 1024
EXTRA = 16


class Mover:
    def __init__(self, sems):
        self.sems = sems
        self.used = 0

    def go(self, src, dst):
        copy = pltpu.make_async_copy(src, dst, self.sems.at[self.used])
        self.used += 1
        copy.start()
        return copy


def gradient_kernel(part, spots, tall_spots, split, core, *refs):
    n, m = len(spots), len(tall_spots)
    wide, narrow, refs = refs[:n], refs[n:n + m], refs[n + m:]
    outs, (xs, st, ov, sems) = refs[:-4], refs[-4:]
    quarters, _, size = xs.shape
    half = quarters // 2
    move = Mover(sems)
    load_s = [
        move.go(r, st.at[pl.ds(top, r.shape[0]), pl.ds(at, r.shape[1])])
        for r, (top, at) in zip(narrow, tall_spots)
    ]

    def load_quarter(i):
        first = i * size
        if split:
            c = core[0] if i >= half else 1 - core[0]
            first = pl.multiple_of(((i % half) * 2 + c) * size, size)
        return [
            move.go(r.at[pl.ds(0, part), pl.ds(first, size)], xs.at[i, pl.ds(at, part)])
            for r, at in zip(wide, spots)
        ]

    load_x = [load_quarter(0), load_quarter(1)]
    for c in load_s:
        c.wait()
    stores = []
    for i in range(quarters):
        for c in load_x[i]:
            c.wait()
        if i + 2 < quarters:
            load_x.append(load_quarter(i + 2))
        ov[i] = jnp.dot(st[...], xs[i], preferred_element_type=jnp.float32).astype(jnp.bfloat16)
        target = outs[i // half].at[i % half] if split else outs[0].at[i]
        stores.append(move.go(ov.at[i], target))
    for c in stores:
        c.wait()


FREE = pl.CostEstimate(flops=0, bytes_accessed=0, transcendentals=0)


def gradient(wide, part, narrows, split, name):
    n_dp = lax.axis_size("dp")
    spots, at = [part * i for i in range(len(wide))], part * len(wide)
    flat, tall_spots, tall = [], [], 0
    for pieces in narrows:
        col = 0
        for piece in pieces:
            flat.append(piece)
            tall_spots.append((tall, col))
            col += piece.shape[1]
        tall += pieces[0].shape[0]
    size = wide[0].shape[1] // n_dp
    count = 2 if split else 1
    piece = jax.ShapeDtypeStruct((n_dp // count, tall, size), jnp.bfloat16)
    core = (lax.axis_index("dp") % 2).reshape(1)
    return pl.pallas_call(
        functools.partial(gradient_kernel, part, tuple(spots), tuple(tall_spots), split),
        out_shape=[piece] * count,
        in_specs=[pl.BlockSpec(memory_space=pltpu.SMEM)] + [ANY] * (len(wide) + len(flat)),
        out_specs=[ANY] * count,
        scratch_shapes=[
            pltpu.VMEM((n_dp, at, size), jnp.bfloat16),
            pltpu.VMEM((tall, at), jnp.bfloat16),
            pltpu.VMEM((n_dp, tall, size), jnp.bfloat16),
            pltpu.SemaphoreType.DMA((len(flat) + n_dp * len(wide) + n_dp,)),
        ],
        compiler_params=pltpu.CompilerParams(vmem_limit_bytes=KERNEL_VMEM),
        cost_estimate=FREE,
        name=name,
    )(core, *wide, *flat)


def total_of(*values):
    total = values[0].astype(jnp.float32)
    for v in values[1:]:
        total = total + v.astype(jnp.float32)
    return total.astype(jnp.bfloat16)


def pair_kernel(part_f, got_f, part_b, got_b, f, b):
    f[...] = total_of(part_f[...], got_f[...])
    b[...] = total_of(part_b[...], got_b[...])


def end_kernel(own_o, of, ob, own_t, tf, tb, o, t):
    o[...] = total_of(own_o[...], of[...], ob[...])
    t[...] = total_of(own_t[...], tf[...], tb[...])


def by_columns(kernel, operands, out_shapes, name):
    features = out_shapes[0][-1]
    steps = 2

    def spec(shape):
        block = tuple(shape[:-1]) + (features // steps,)
        return pl.BlockSpec(block, lambda i, n=len(shape): (0,) * (n - 1) + (i,))

    return pl.pallas_call(
        kernel,
        out_shape=[jax.ShapeDtypeStruct(s, jnp.bfloat16) for s in out_shapes],
        grid=(steps,),
        in_specs=[spec(v.shape) for v in operands],
        out_specs=[spec(s) for s in out_shapes],
        compiler_params=pltpu.CompilerParams(vmem_limit_bytes=KERNEL_VMEM),
        cost_estimate=FREE,
        name=name,
    )(*operands)


def y_parts_kernel(y, kept, got, first, second):
    half = first.shape[0]
    first[...] = total_of(kept[0, :half], got[0, :half])
    second[...] = total_of(kept[0, half:], got[0, half:])


def y_parts(kept, got, name):
    _, ff, size = kept.shape
    other = (1 - lax.axis_index("dp") // 2).reshape(1)
    quarter = pl.BlockSpec((1, ff, size), lambda i, y: (y[0], 0, 0))
    piece = jax.ShapeDtypeStruct((ff // 2, size), jnp.bfloat16)
    return pl.pallas_call(
        y_parts_kernel,
        out_shape=[piece, piece],
        grid_spec=pltpu.PrefetchScalarGridSpec(
            num_scalar_prefetch=1,
            grid=(1,),
            in_specs=[quarter, quarter],
            out_specs=[pl.BlockSpec(piece.shape, lambda i, y: (0, 0))] * 2,
        ),
        compiler_params=pltpu.CompilerParams(vmem_limit_bytes=KERNEL_VMEM),
        cost_estimate=FREE,
        name=name,
    )(other, kept, got)


def last_add_kernel(y, kept, got, last_0, last_1, out):
    half = last_0.shape[0]
    for i, last in enumerate((last_0, last_1)):
        rows = pl.ds(i * half, half)
        total = kept[0, rows].astype(jnp.float32) + got[0, rows].astype(jnp.float32)
        total = total + last[...].astype(jnp.float32)
        out[0, :, rows] = total.T.astype(jnp.bfloat16)


def last_add(kept, got, lasts, name):
    _, ff, size = kept.shape
    y = (lax.axis_index("dp") // 2).reshape(1)
    shape = (1, size, ff)
    half = pl.BlockSpec((1, ff, size), lambda i, y: (y[0], 0, 0))
    piece = pl.BlockSpec((ff // 2, size), lambda i, y: (0, 0))
    return pl.pallas_call(
        last_add_kernel,
        out_shape=jax.ShapeDtypeStruct(shape, jnp.bfloat16),
        grid_spec=pltpu.PrefetchScalarGridSpec(
            num_scalar_prefetch=1,
            grid=(1,),
            in_specs=[half, half, piece, piece],
            out_specs=pl.BlockSpec(shape, lambda i, y: (0, 0, 0)),
        ),
        compiler_params=pltpu.CompilerParams(vmem_limit_bytes=KERNEL_VMEM),
        cost_estimate=FREE,
        name=name,
    )(y, kept, got, *lasts)


def with_weights_kernel(cot, routes, combine, out):
    rows, features = cot.shape
    out[:rows] = cot[...]
    line = lax.broadcasted_iota(jnp.int32, (EXTRA, rows), 0)
    weights = jnp.zeros((EXTRA, rows), jnp.float32)
    for k in range(routes.shape[0]):
        weights += jnp.where(routes[k:k + 1] == line, combine[k:k + 1], 0.0)
    wide = weights * 65537.0
    high = wide - (wide - weights)
    rest = weights - high
    wide = rest * 65537.0
    middle = wide - (wide - rest)
    out[rows:] = jnp.zeros((EXTRA, features), jnp.bfloat16)
    for i, term in enumerate((high, middle, rest - middle)):
        out[rows:, i * rows:(i + 1) * rows] = term.astype(jnp.bfloat16)


def with_weights(cot, routes, combine):
    return pl.pallas_call(
        with_weights_kernel,
        out_shape=jax.ShapeDtypeStruct((cot.shape[0] + EXTRA, cot.shape[1]), cot.dtype),
        cost_estimate=FREE,
        name="with_weights",
    )(cot, routes.T, combine.T)


def expert_kernel(n, me, *refs):
    xs, gs, refs = refs[:n], refs[n:2 * n], refs[2 * n:]
    wg, wu, wd, wdt, wgt, wut = refs[:6]
    outs, backs, refs = refs[6:6 + n], refs[6 + n:6 + 2 * n], refs[6 + 2 * n:]
    s_o, dg_o, du_o, comb_o = refs[:4]
    x2, g2, wgv, wuv, wdv, wdtv, wgtv, wutv, gv, uv, sv, dgv, duv, wb, wv, st, dgt, dut, ov, rv, sems = refs[4:]
    part = xs[0].shape[0]
    rows, features = x2.shape
    ff = gv.shape[1]
    f32, bf16 = jnp.float32, jnp.bfloat16
    move = Mover(sems)
    cols = [pl.ds(f, 256) for f in range(0, ff, 256)]
    wide = [pl.ds(d, 512) for d in range(0, features, 512)]
    spots = [pl.ds(i * part, part) for i in range(n)]

    def load(src, dst, pieces):
        size = src.shape[0] // pieces
        return [
            move.go(src.at[pl.ds(i * size, size)], dst.at[pl.ds(i * size, size)])
            for i in range(pieces)
        ]

    load_x = [move.go(r, x2.at[s]) for r, s in zip(xs, spots)]
    span = wb.shape[2]
    load_w = [move.go(r.at[pl.ds(part, EXTRA), pl.ds(0, span)], wb.at[i]) for i, r in enumerate(gs)]
    load_g = load(wg, wgv, 4)
    load_u = load(wu, wuv, 4)
    load_cot = [move.go(r.at[pl.ds(0, part)], g2.at[s]) for r, s in zip(gs, spots)]
    load_d = load(wd, wdv, 4)
    load_dt = load(wdt, wdtv, 4)
    load_gt = load(wgt, wgtv, 4)
    load_ut = load(wut, wutv, 4)
    for c in load_w:
        c.wait()
    for i, s in enumerate(spots):
        terms = wb[i].astype(f32)
        mine = lax.broadcasted_iota(jnp.int32, terms.shape, 0) == me[0]
        terms = jnp.sum(jnp.where(mine, terms, 0.0), axis=0, keepdims=True)
        terms = terms[:, :part] + terms[:, part:2 * part] + terms[:, 2 * part:]
        wv[s, :] = jnp.broadcast_to(terms, (128, part)).T[:, :1]
    for c in load_x + load_g:
        c.wait()
    for c in cols:
        gv[:, c] = jnp.dot(x2[...], wgv[:, c], preferred_element_type=f32)
    for c in load_u:
        c.wait()
    for c in cols:
        up = jnp.dot(x2[...], wuv[:, c], preferred_element_type=f32)
        uv[:, c] = up
        gate = gv[:, c]
        scaled = (gate * jax.nn.sigmoid(gate) * up * wv[...]).astype(bf16)
        sv[:, c] = scaled
        st[c, :] = scaled.T
    stores = [move.go(st, s_o)]
    for c in load_d:
        c.wait()
    for c in wide:
        ov[:, c] = jnp.dot(sv[...], wdv[:, c], preferred_element_type=f32).astype(bf16)
    stores += [move.go(ov.at[s], r) for r, s in zip(outs, spots)]
    for c in load_cot + load_dt:
        c.wait()
    comb = jnp.zeros((rows, 1), f32)
    for c in cols:
        d_raw = jnp.dot(g2[...], wdtv[:, c], preferred_element_type=f32)
        gate, up = gv[:, c], uv[:, c]
        sig = jax.nn.sigmoid(gate)
        act = gate * sig
        comb += jnp.sum(act * up * d_raw, axis=1, keepdims=True)
        d_hidden = d_raw * wv[...]
        d_gate = (d_hidden * up * sig * (1.0 + gate * (1.0 - sig))).astype(bf16)
        d_up = (d_hidden * act).astype(bf16)
        dgv[:, c] = d_gate
        duv[:, c] = d_up
        dgt[c, :] = d_gate.T
        dut[c, :] = d_up.T
    comb_o[...] = jnp.broadcast_to(comb, (rows, 128)).T[:1, :]
    stores += [move.go(dgt, dg_o), move.go(dut, du_o)]
    for c in load_gt + load_ut:
        c.wait()
    for c in wide:
        rv[:, c] = (
            jnp.dot(dgv[...], wgtv[:, c], preferred_element_type=f32)
            + jnp.dot(duv[...], wutv[:, c], preferred_element_type=f32)
        ).astype(bf16)
    stores += [move.go(rv.at[s], r) for r, s in zip(backs, spots)]
    for c in stores:
        c.wait()


def expert(xs, gs, matrices, name):
    n, (part, features) = len(xs), xs[0].shape
    ff = matrices[0].shape[1]
    rows = n * part
    bf16, f32 = jnp.bfloat16, jnp.float32
    vmem = pl.BlockSpec(memory_space=pltpu.VMEM)
    block = jax.ShapeDtypeStruct((part, features), bf16)
    turned = jax.ShapeDtypeStruct((ff, rows), bf16)
    me = lax.axis_index("expert").reshape(1)
    res = pl.pallas_call(
        functools.partial(expert_kernel, n),
        out_shape=[block] * (2 * n) + [turned] * 3 + [jax.ShapeDtypeStruct((1, rows), f32)],
        in_specs=[pl.BlockSpec(memory_space=pltpu.SMEM)] + [ANY] * (2 * n + 6),
        out_specs=[ANY] * (2 * n + 3) + [vmem],
        scratch_shapes=[
            pltpu.VMEM((rows, features), bf16),
            pltpu.VMEM((rows, features), bf16),
            pltpu.VMEM((features, ff), bf16),
            pltpu.VMEM((features, ff), bf16),
            pltpu.VMEM((ff, features), bf16),
            pltpu.VMEM((features, ff), bf16),
            pltpu.VMEM((ff, features), bf16),
            pltpu.VMEM((ff, features), bf16),
            pltpu.VMEM((rows, ff), f32),
            pltpu.VMEM((rows, ff), f32),
            pltpu.VMEM((rows, ff), bf16),
            pltpu.VMEM((rows, ff), bf16),
            pltpu.VMEM((rows, ff), bf16),
            pltpu.VMEM((n, EXTRA, 3 * part), bf16),
            pltpu.VMEM((rows, 1), f32),
            pltpu.VMEM((ff, rows), bf16),
            pltpu.VMEM((ff, rows), bf16),
            pltpu.VMEM((ff, rows), bf16),
            pltpu.VMEM((rows, features), bf16),
            pltpu.VMEM((rows, features), bf16),
            pltpu.SemaphoreType.DMA((5 * n + 27,)),
        ],
        compiler_params=pltpu.CompilerParams(vmem_limit_bytes=KERNEL_VMEM),
        cost_estimate=FREE,
        name=name,
    )(me, *xs, *gs, *matrices)
    return res[:n], res[n:2 * n], res[2 * n:]


def gathered_plan(tokens, routes, combine, cotangent, w_gate, w_up, w_down):
    tok_rows, features = tokens.shape
    groups = lax.axis_size("expert")
    me = lax.axis_index("expert")
    chosen = routes[:, :, None] == jnp.arange(groups, dtype=jnp.int32)[None, None, :]
    matrices = [w_gate[0], w_up[0], w_down[0], w_down[0].T, w_gate[0].T, w_up[0].T]

    xs = [forward(tokens), backward(tokens)]
    both = with_weights(cotangent, routes, combine)
    gs = [forward(both), backward(both)]
    gf, gb, m3, m4, m5 = tie(*gs, *matrices[3:])
    matrices = matrices[:3] + [m3, m4, m5]
    xf, xb = xs
    all_x, all_g, outs, backs, smalls = [], [], [], [], []
    for step in range(1, 5):
        here_x, here_g = [xf, xb], [gf, gb]
        if step < 3:
            gf, gb = forward(gf), backward(gb)
            xf, xb = forward(xf), backward(xb)
        elif step == 3:
            gb, xf = backward(gb), forward(xf)
        else:
            here_x, here_g = [xf], [gb]
            tf, ob = forward(backs[6]), backward(outs[5])
        if step == 1:
            here_x, here_g = [tokens, *here_x], [both, *here_g]
        out, back, small = expert(here_x, here_g, matrices, f"expert_{step}")
        if step < 3:
            gf, gb, first = tie(gf, gb, small[0])
            xf, xb, first = tie(xf, xb, first)
        elif step == 3:
            gb, xf, first = tie(gb, xf, small[0])
        else:
            tf, ob, first = tie(tf, ob, small[0])
        all_x += here_x
        all_g += here_g
        outs += out
        backs += back
        smalls.append([first, *small[1:]])

    scaled, d_gate, d_up, combs = (list(v) for v in zip(*smalls))
    two = [tokens.shape] * 2

    def summed(part_f, got_f, part_b, got_b, name):
        return by_columns(pair_kernel, [part_f, got_f, part_b, got_b], two, name)

    of, tb = forward(outs[7]), backward(backs[7])
    tf, ob = summed(backs[4], tf, outs[3], ob, "sum_a2")
    part_d, = gradient(all_g, tok_rows, [scaled], False, "grad_down")
    of, tb, tf, ob, part_d, d_gate[-1] = tie(of, tb, tf, ob, part_d, d_gate[-1])

    d_w_down = lax.psum_scatter(part_d, "dp", scatter_dimension=0, tiled=False)
    tf, ob = forward(tf), backward(ob)
    of, tb = summed(outs[6], of, backs[5], tb, "sum_b3")
    away_g, kept_g = gradient(all_x, tok_rows, [d_gate], True, "grad_gate")
    tf, ob, of, tb, away_g, d_up[-1] = tie(tf, ob, of, tb, away_g, d_up[-1])

    of, tb, got_g = forward(of), backward(tb), core_swap(away_g)
    first_g, other_g = y_parts(kept_g, got_g, "half_gate")
    first_g, other_g, d_up[-1] = tie(first_g, other_g, d_up[-1])
    first_g = y_swap(first_g)
    tf, ob = summed(backs[2], tf, outs[1], ob, "sum_a1")
    away_u, kept_u = gradient(all_x, tok_rows, [d_up], True, "grad_up")
    of, tb, tf, ob, away_u, first_g, other_g, combs[-1] = tie(
        of, tb, tf, ob, away_u, first_g, other_g, combs[-1]
    )

    tf, ob, got_u, other_g = forward(tf), backward(ob), core_swap(away_u), y_swap(other_g)
    of, tb = summed(outs[4], of, backs[3], tb, "sum_b2")
    first_u, other_u = y_parts(kept_u, got_u, "half_up")
    d_comb = jnp.concatenate(combs, axis=1).reshape(groups, tok_rows)
    table = ring_sources()
    inverse = jnp.asarray([[row.index(e) for e in range(groups)] for row in table], jnp.int32)[me]
    d_comb = d_comb[inverse]
    tf, ob, of, tb, other_g, first_u, other_u, d_comb = tie(
        tf, ob, of, tb, other_g, first_u, other_u, d_comb
    )

    of, tb, first_u = forward(of), backward(tb), y_swap(first_u)
    d_w_gate = last_add(kept_g, got_g, [first_g, other_g], "sum_gate")
    of, tb, first_u, d_comb, d_w_gate, d_w_down = tie(of, tb, first_u, d_comb, d_w_gate, d_w_down)

    of, tb = summed(outs[2], of, backs[1], tb, "sum_b1")
    of, tb, other_u = forward(of), backward(tb), y_swap(other_u)
    returned = lax.all_to_all(d_comb, "expert", split_axis=0, concat_axis=0, tiled=True)
    d_combine = jnp.sum(jnp.where(chosen, returned.T[:, None, :], 0.0), axis=2)
    d_w_up = last_add(kept_u, got_u, [first_u, other_u], "sum_up")
    output, d_tokens = by_columns(
        end_kernel, [outs[0], of, ob, backs[0], tf, tb], two, "sum_end"
    )
    return output, d_tokens, d_combine, d_w_gate, d_w_up, d_w_down[None]


def solution(mesh):
    rows = P(("dp", "expert"), None)
    small = mesh.shape["expert"] == len(RING) and mesh.shape["dp"] == 4
    return jax.shard_map(
        gathered_plan if small else routed_plan,
        mesh=mesh,
        in_specs=(rows, rows, rows, rows) + (P("expert", None, None),) * 3,
        out_specs=(
            rows,
            rows,
            rows,
            P("expert", "dp", None),
            P("expert", "dp", None),
            P("expert", None, "dp"),
        ),
        check_vma=False,
    )
```

```python
import functools
import jax
import jax.numpy as jnp
from jax import lax
from jax.experimental import pallas as pl
from jax.experimental.pallas import tpu as pltpu
from jax.sharding import PartitionSpec as P


def slot_map(routes, experts, capacity):
    flat_ids = routes.reshape(-1)
    onehot = (flat_ids[:, None] == jnp.arange(experts, dtype=jnp.int32)[None, :]).astype(jnp.int32)
    before = jnp.cumsum(onehot, axis=0) - onehot
    slots = jnp.sum(before * onehot, axis=1)
    target = flat_ids * capacity + slots
    source = (
        jnp.full((experts * capacity,), -1, jnp.int32)
        .at[target]
        .set(jnp.arange(flat_ids.shape[0], dtype=jnp.int32))
    )
    return (target, source)


def routed_plan(tokens, routes, combine, cotangent, w_gate, w_up, w_down):
    tok_rows, features = tokens.shape
    per_token = routes.shape[1]
    groups = lax.axis_size("expert")
    local_exp = w_gate.shape[0]
    experts = local_exp * groups
    capacity = 3 * tok_rows * per_token // (2 * experts)
    target, source = slot_map(routes, experts, capacity)
    filled = (source >= 0)[:, None]
    pair_index = jnp.maximum(source, 0)
    owner_row = pair_index // per_token
    outgoing = jnp.where(filled, tokens[owner_row], jnp.zeros((), jnp.bfloat16))
    outgoing = outgoing.reshape(groups, local_exp, capacity, features)
    cot_float = cotangent.astype(jnp.float32)
    scaled = (combine[:, :, None] * cot_float[:, None, :]).reshape(tok_rows * per_token, features)
    outgoing_grad = jnp.where(filled, scaled[pair_index], 0.0).astype(jnp.bfloat16)
    outgoing_grad = outgoing_grad.reshape(groups, local_exp, capacity, features)
    arrived = lax.all_to_all(outgoing, "expert", split_axis=0, concat_axis=0, tiled=True)
    gate_pre = jnp.einsum("secd,edf->secf", arrived, w_gate, preferred_element_type=jnp.float32)
    up_pre = jnp.einsum("secd,edf->secf", arrived, w_up, preferred_element_type=jnp.float32)
    activated = jax.nn.silu(gate_pre)
    hidden = (activated * up_pre).astype(jnp.bfloat16)
    produced = jnp.einsum(
        "secf,efd->secd", hidden, w_down, preferred_element_type=jnp.float32
    ).astype(jnp.bfloat16)
    returned = lax.all_to_all(produced, "expert", split_axis=0, concat_axis=0, tiled=True)
    d_in = lax.all_to_all(outgoing_grad, "expert", split_axis=0, concat_axis=0, tiled=True)
    d_hidden = jnp.einsum("secd,efd->secf", d_in, w_down, preferred_element_type=jnp.float32)
    part_down = jnp.einsum("secf,secd->efd", hidden, d_in, preferred_element_type=jnp.float32)
    sigmoid_g = jax.nn.sigmoid(gate_pre)
    d_gate = (d_hidden * up_pre * sigmoid_g * (1.0 + gate_pre * (1.0 - sigmoid_g))).astype(
        jnp.bfloat16
    )
    d_up = (d_hidden * activated).astype(jnp.bfloat16)
    part_gate = jnp.einsum("secd,secf->edf", arrived, d_gate, preferred_element_type=jnp.float32)
    part_up = jnp.einsum("secd,secf->edf", arrived, d_up, preferred_element_type=jnp.float32)
    d_rows = (
        jnp.einsum("secf,edf->secd", d_gate, w_gate, preferred_element_type=jnp.float32)
        + jnp.einsum("secf,edf->secd", d_up, w_up, preferred_element_type=jnp.float32)
    ).astype(jnp.bfloat16)
    back = lax.all_to_all(d_rows, "expert", split_axis=0, concat_axis=0, tiled=True)
    per_slot = returned.reshape(experts * capacity, features)[target]
    per_slot = per_slot.reshape(tok_rows, per_token, features).astype(jnp.float32)
    output = jnp.sum(combine[:, :, None] * per_slot, axis=1).astype(jnp.bfloat16)
    d_combine = jnp.sum(per_slot * cot_float[:, None, :], axis=2)
    back_slot = back.reshape(experts * capacity, features)[target]
    back_slot = back_slot.reshape(tok_rows, per_token, features).astype(jnp.float32)
    d_tokens = jnp.sum(back_slot, axis=1).astype(jnp.bfloat16)
    sum_gate, sum_up, sum_down = (
        lax.psum_scatter(
            part_gate.astype(jnp.bfloat16), "dp", scatter_dimension=1, tiled=True
        ).astype(jnp.float32),
        lax.psum_scatter(
            part_up.astype(jnp.bfloat16), "dp", scatter_dimension=1, tiled=True
        ).astype(jnp.float32),
        lax.psum_scatter(
            part_down.astype(jnp.bfloat16), "dp", scatter_dimension=2, tiled=True
        ).astype(jnp.float32),
    )
    d_w_down = sum_down.astype(jnp.bfloat16)
    return (
        output,
        d_tokens,
        d_combine,
        sum_gate.astype(jnp.bfloat16),
        sum_up.astype(jnp.bfloat16),
        d_w_down,
    )


RING = (0, 1, 3, 5, 7, 6, 4, 2)


def ring_perms():
    n = len(RING)
    fwd = [(RING[i], RING[(i + 1) % n]) for i in range(n)]
    bwd = [(RING[(i + 1) % n], RING[i]) for i in range(n)]
    return fwd, bwd


def ring_sources():
    n = len(RING)
    place = {e: i for i, e in enumerate(RING)}
    steps = (0, -1, 1, -2, 2, -3, 3, 4)
    return [[RING[(place[e] + r) % n] for r in steps] for e in range(n)]


def forward(value):
    return lax.ppermute(value, "expert", ring_perms()[0])


def backward(value):
    return lax.ppermute(value, "expert", ring_perms()[1])


def tie(*values):
    return lax.optimization_barrier(values)


def add_rounded(a, b):
    return (a.astype(jnp.float32) + b.astype(jnp.float32)).astype(jnp.bfloat16)


def core_swap(away):
    n = lax.axis_size("dp")
    return lax.ppermute(away, "dp", [(j, j ^ 1) for j in range(n)])


def y_swap(other):
    n = lax.axis_size("dp")
    return lax.ppermute(other, "dp", [(j, j ^ 2) for j in range(n)])


ANY = pl.BlockSpec(memory_space=pl.ANY)
KERNEL_VMEM = 60 * 1024 * 1024
EXTRA = 16


class Mover:
    def __init__(self, sems):
        self.sems = sems
        self.used = 0

    def go(self, src, dst):
        copy = pltpu.make_async_copy(src, dst, self.sems.at[self.used])
        self.used += 1
        copy.start()
        return copy


def gradient_kernel(part, spots, tall_spots, core, *refs):
    n, m = len(spots), len(tall_spots)
    wide, narrow, refs = refs[:n], refs[n:n + m], refs[n + m:]
    away, kept, xs, st, ov, sems = refs
    quarters, _, size = xs.shape
    move = Mover(sems)
    load_s = [
        move.go(r, st.at[pl.ds(top, r.shape[0]), pl.ds(at, r.shape[1])])
        for r, (top, at) in zip(narrow, tall_spots)
    ]

    def load_quarter(i):
        c = core[0] if i >= quarters // 2 else 1 - core[0]
        first = pl.multiple_of(((i % (quarters // 2)) * 2 + c) * size, size)
        return [
            move.go(r.at[pl.ds(0, part), pl.ds(first, size)], xs.at[i, pl.ds(at, part)])
            for r, at in zip(wide, spots)
        ]

    load_x = [load_quarter(0), load_quarter(1)]
    for c in load_s:
        c.wait()
    stores = []
    for i in range(quarters):
        for c in load_x[i]:
            c.wait()
        if i + 2 < quarters:
            load_x.append(load_quarter(i + 2))
        for f in range(0, st.shape[0], 256):
            ov[i, f:f + 256, :] = jnp.dot(
                st[f:f + 256, :], xs[i], preferred_element_type=jnp.float32
            ).astype(jnp.bfloat16)
        half = quarters // 2
        stores.append(move.go(ov.at[i], away.at[i] if i < half else kept.at[i - half]))
    for c in stores:
        c.wait()


FREE = pl.CostEstimate(flops=0, bytes_accessed=0, transcendentals=0)


def gradient(wide, part, narrows, name):
    n_dp = lax.axis_size("dp")
    spots, at = [part * i for i in range(len(wide))], part * len(wide)
    flat, tall_spots, tall = [], [], 0
    for pieces in narrows:
        col = 0
        for piece in pieces:
            flat.append(piece)
            tall_spots.append((tall, col))
            col += piece.shape[1]
        tall += pieces[0].shape[0]
    size = wide[0].shape[1] // n_dp
    half = jax.ShapeDtypeStruct((n_dp // 2, tall, size), jnp.bfloat16)
    core = (lax.axis_index("dp") % 2).reshape(1)
    return pl.pallas_call(
        functools.partial(gradient_kernel, part, tuple(spots), tuple(tall_spots)),
        out_shape=[half, half],
        in_specs=[pl.BlockSpec(memory_space=pltpu.SMEM)] + [ANY] * (len(wide) + len(flat)),
        out_specs=[ANY, ANY],
        scratch_shapes=[
            pltpu.VMEM((n_dp, at, size), jnp.bfloat16),
            pltpu.VMEM((tall, at), jnp.bfloat16),
            pltpu.VMEM((n_dp, tall, size), jnp.bfloat16),
            pltpu.SemaphoreType.DMA((len(flat) + n_dp * len(wide) + n_dp,)),
        ],
        compiler_params=pltpu.CompilerParams(vmem_limit_bytes=KERNEL_VMEM),
        cost_estimate=FREE,
        name=name,
    )(core, *wide, *flat)


def total_of(*values):
    total = values[0].astype(jnp.float32)
    for v in values[1:]:
        total = total + v.astype(jnp.float32)
    return total.astype(jnp.bfloat16)


def pair_kernel(part_f, got_f, part_b, got_b, f, b):
    f[...] = total_of(part_f[...], got_f[...])
    b[...] = total_of(part_b[...], got_b[...])


def end_kernel(own_o, of, ob, own_t, tf, tb, o, t):
    o[...] = total_of(own_o[...], of[...], ob[...])
    t[...] = total_of(own_t[...], tf[...], tb[...])


def by_columns(kernel, operands, out_shapes, name):
    features = out_shapes[0][-1]
    steps = 2

    def spec(shape):
        block = tuple(shape[:-1]) + (features // steps,)
        return pl.BlockSpec(block, lambda i, n=len(shape): (0,) * (n - 1) + (i,))

    return pl.pallas_call(
        kernel,
        out_shape=[jax.ShapeDtypeStruct(s, jnp.bfloat16) for s in out_shapes],
        grid=(steps,),
        in_specs=[spec(v.shape) for v in operands],
        out_specs=[spec(s) for s in out_shapes],
        compiler_params=pltpu.CompilerParams(vmem_limit_bytes=KERNEL_VMEM),
        cost_estimate=FREE,
        name=name,
    )(*operands)


def y_parts_kernel(y, kept, got, first, second):
    half = first.shape[0]
    first[...] = total_of(kept[0, :half], got[0, :half])
    second[...] = total_of(kept[0, half:], got[0, half:])


def y_parts(kept, got, name):
    _, ff, size = kept.shape
    other = (1 - lax.axis_index("dp") // 2).reshape(1)
    quarter = pl.BlockSpec((1, ff, size), lambda i, y: (y[0], 0, 0))
    piece = jax.ShapeDtypeStruct((ff // 2, size), jnp.bfloat16)
    return pl.pallas_call(
        y_parts_kernel,
        out_shape=[piece, piece],
        grid_spec=pltpu.PrefetchScalarGridSpec(
            num_scalar_prefetch=1,
            grid=(1,),
            in_specs=[quarter, quarter],
            out_specs=[pl.BlockSpec(piece.shape, lambda i, y: (0, 0))] * 2,
        ),
        compiler_params=pltpu.CompilerParams(vmem_limit_bytes=KERNEL_VMEM),
        cost_estimate=FREE,
        name=name,
    )(other, kept, got)


def last_add_kernel(turned, y, kept, got, last_0, last_1, out):
    half = last_0.shape[0]
    for i, last in enumerate((last_0, last_1)):
        rows = pl.ds(i * half, half)
        total = kept[0, rows].astype(jnp.float32) + got[0, rows].astype(jnp.float32)
        total = total + last[...].astype(jnp.float32)
        if turned:
            out[0, :, rows] = total.T.astype(jnp.bfloat16)
        else:
            out[0, rows] = total.astype(jnp.bfloat16)


def last_add(kept, got, lasts, turned, name):
    _, ff, size = kept.shape
    y = (lax.axis_index("dp") // 2).reshape(1)
    shape = (1, size, ff) if turned else (1, ff, size)
    half = pl.BlockSpec((1, ff, size), lambda i, y: (y[0], 0, 0))
    piece = pl.BlockSpec((ff // 2, size), lambda i, y: (0, 0))
    return pl.pallas_call(
        functools.partial(last_add_kernel, turned),
        out_shape=jax.ShapeDtypeStruct(shape, jnp.bfloat16),
        grid_spec=pltpu.PrefetchScalarGridSpec(
            num_scalar_prefetch=1,
            grid=(1,),
            in_specs=[half, half, piece, piece],
            out_specs=pl.BlockSpec(shape, lambda i, y: (0, 0, 0)),
        ),
        compiler_params=pltpu.CompilerParams(vmem_limit_bytes=KERNEL_VMEM),
        cost_estimate=FREE,
        name=name,
    )(y, kept, got, *lasts)


def with_weights_kernel(cot, routes, combine, out):
    rows, features = cot.shape
    out[:rows] = cot[...]
    line = lax.broadcasted_iota(jnp.int32, (EXTRA, rows), 0)
    weights = jnp.zeros((EXTRA, rows), jnp.float32)
    for k in range(routes.shape[0]):
        weights += jnp.where(routes[k:k + 1] == line, combine[k:k + 1], 0.0)
    wide = weights * 65537.0
    high = wide - (wide - weights)
    rest = weights - high
    wide = rest * 65537.0
    middle = wide - (wide - rest)
    out[rows:] = jnp.zeros((EXTRA, features), jnp.bfloat16)
    for i, term in enumerate((high, middle, rest - middle)):
        out[rows:, i * rows:(i + 1) * rows] = term.astype(jnp.bfloat16)


def with_weights(cot, routes, combine):
    return pl.pallas_call(
        with_weights_kernel,
        out_shape=jax.ShapeDtypeStruct((cot.shape[0] + EXTRA, cot.shape[1]), cot.dtype),
        cost_estimate=FREE,
        name="with_weights",
    )(cot, routes.T, combine.T)


def expert_kernel(n, me, *refs):
    xs, gs, refs = refs[:n], refs[n:2 * n], refs[2 * n:]
    wg, wu, wd, wdt, wgt, wut = refs[:6]
    outs, backs, refs = refs[6:6 + n], refs[6 + n:6 + 2 * n], refs[6 + 2 * n:]
    s_o, dg_o, du_o, comb_o = refs[:4]
    x2, g2, wgv, wuv, wdv, wdtv, wgtv, wutv, gv, uv, sv, dgv, duv, wb, wv, st, dgt, dut, ov, rv, sems = refs[4:]
    part = xs[0].shape[0]
    rows, features = x2.shape
    ff = gv.shape[1]
    f32, bf16 = jnp.float32, jnp.bfloat16
    move = Mover(sems)
    cols = [pl.ds(f, 256) for f in range(0, ff, 256)]
    wide = [pl.ds(d, 512) for d in range(0, features, 512)]
    spots = [pl.ds(i * part, part) for i in range(n)]

    def load(src, dst, pieces):
        size = src.shape[0] // pieces
        return [
            move.go(src.at[pl.ds(i * size, size)], dst.at[pl.ds(i * size, size)])
            for i in range(pieces)
        ]

    load_x = [move.go(r, x2.at[s]) for r, s in zip(xs, spots)]
    span = wb.shape[2]
    load_w = [move.go(r.at[pl.ds(part, EXTRA), pl.ds(0, span)], wb.at[i]) for i, r in enumerate(gs)]
    load_g = load(wg, wgv, 4)
    load_u = load(wu, wuv, 4)
    load_cot = [move.go(r.at[pl.ds(0, part)], g2.at[s]) for r, s in zip(gs, spots)]
    load_d = load(wd, wdv, 4)
    load_dt = load(wdt, wdtv, 4)
    load_gt = load(wgt, wgtv, 4)
    load_ut = load(wut, wutv, 4)
    for c in load_w:
        c.wait()
    for i, s in enumerate(spots):
        terms = wb[i].astype(f32)
        mine = lax.broadcasted_iota(jnp.int32, terms.shape, 0) == me[0]
        terms = jnp.sum(jnp.where(mine, terms, 0.0), axis=0, keepdims=True)
        terms = terms[:, :part] + terms[:, part:2 * part] + terms[:, 2 * part:]
        wv[s, :] = jnp.broadcast_to(terms, (128, part)).T[:, :1]
    for c in load_x + load_g:
        c.wait()
    for c in cols:
        gv[:, c] = jnp.dot(x2[...], wgv[:, c], preferred_element_type=f32)
    for c in load_u:
        c.wait()
    for c in cols:
        up = jnp.dot(x2[...], wuv[:, c], preferred_element_type=f32)
        uv[:, c] = up
        gate = gv[:, c]
        scaled = (gate * jax.nn.sigmoid(gate) * up * wv[...]).astype(bf16)
        sv[:, c] = scaled
        st[c, :] = scaled.T
    stores = [move.go(st, s_o)]
    for c in load_d:
        c.wait()
    for c in wide:
        ov[:, c] = jnp.dot(sv[...], wdv[:, c], preferred_element_type=f32).astype(bf16)
    stores += [move.go(ov.at[s], r) for r, s in zip(outs, spots)]
    for c in load_cot + load_dt:
        c.wait()
    comb = jnp.zeros((rows, 1), f32)
    for c in cols:
        d_raw = jnp.dot(g2[...], wdtv[:, c], preferred_element_type=f32)
        gate, up = gv[:, c], uv[:, c]
        sig = jax.nn.sigmoid(gate)
        act = gate * sig
        comb += jnp.sum(act * up * d_raw, axis=1, keepdims=True)
        d_hidden = d_raw * wv[...]
        d_gate = (d_hidden * up * sig * (1.0 + gate * (1.0 - sig))).astype(bf16)
        d_up = (d_hidden * act).astype(bf16)
        dgv[:, c] = d_gate
        duv[:, c] = d_up
        dgt[c, :] = d_gate.T
        dut[c, :] = d_up.T
    comb_o[...] = jnp.broadcast_to(comb, (rows, 128)).T[:1, :]
    stores += [move.go(dgt, dg_o), move.go(dut, du_o)]
    for c in load_gt + load_ut:
        c.wait()
    for c in wide:
        rv[:, c] = (
            jnp.dot(dgv[...], wgtv[:, c], preferred_element_type=f32)
            + jnp.dot(duv[...], wutv[:, c], preferred_element_type=f32)
        ).astype(bf16)
    stores += [move.go(rv.at[s], r) for r, s in zip(backs, spots)]
    for c in stores:
        c.wait()


def expert(xs, gs, matrices, name):
    n, (part, features) = len(xs), xs[0].shape
    ff = matrices[0].shape[1]
    rows = n * part
    bf16, f32 = jnp.bfloat16, jnp.float32
    vmem = pl.BlockSpec(memory_space=pltpu.VMEM)
    block = jax.ShapeDtypeStruct((part, features), bf16)
    turned = jax.ShapeDtypeStruct((ff, rows), bf16)
    me = lax.axis_index("expert").reshape(1)
    res = pl.pallas_call(
        functools.partial(expert_kernel, n),
        out_shape=[block] * (2 * n) + [turned] * 3 + [jax.ShapeDtypeStruct((1, rows), f32)],
        in_specs=[pl.BlockSpec(memory_space=pltpu.SMEM)] + [ANY] * (2 * n + 6),
        out_specs=[ANY] * (2 * n + 3) + [vmem],
        scratch_shapes=[
            pltpu.VMEM((rows, features), bf16),
            pltpu.VMEM((rows, features), bf16),
            pltpu.VMEM((features, ff), bf16),
            pltpu.VMEM((features, ff), bf16),
            pltpu.VMEM((ff, features), bf16),
            pltpu.VMEM((features, ff), bf16),
            pltpu.VMEM((ff, features), bf16),
            pltpu.VMEM((ff, features), bf16),
            pltpu.VMEM((rows, ff), f32),
            pltpu.VMEM((rows, ff), f32),
            pltpu.VMEM((rows, ff), bf16),
            pltpu.VMEM((rows, ff), bf16),
            pltpu.VMEM((rows, ff), bf16),
            pltpu.VMEM((n, EXTRA, 3 * part), bf16),
            pltpu.VMEM((rows, 1), f32),
            pltpu.VMEM((ff, rows), bf16),
            pltpu.VMEM((ff, rows), bf16),
            pltpu.VMEM((ff, rows), bf16),
            pltpu.VMEM((rows, features), bf16),
            pltpu.VMEM((rows, features), bf16),
            pltpu.SemaphoreType.DMA((5 * n + 27,)),
        ],
        compiler_params=pltpu.CompilerParams(vmem_limit_bytes=KERNEL_VMEM),
        cost_estimate=FREE,
        name=name,
    )(me, *xs, *gs, *matrices)
    return res[:n], res[n:2 * n], res[2 * n:]


def gathered_plan(tokens, routes, combine, cotangent, w_gate, w_up, w_down):
    tok_rows, features = tokens.shape
    groups = lax.axis_size("expert")
    me = lax.axis_index("expert")
    chosen = routes[:, :, None] == jnp.arange(groups, dtype=jnp.int32)[None, None, :]
    matrices = [w_gate[0], w_up[0], w_down[0], w_down[0].T, w_gate[0].T, w_up[0].T]

    xs = [forward(tokens), backward(tokens)]
    both = with_weights(cotangent, routes, combine)
    gs = [forward(both), backward(both)]
    gf, gb, m3, m4, m5 = tie(*gs, *matrices[3:])
    matrices = matrices[:3] + [m3, m4, m5]
    xf, xb = xs
    all_x, all_g, outs, backs, smalls = [], [], [], [], []
    for step in range(1, 5):
        here_x, here_g = [xf, xb], [gf, gb]
        if step < 3:
            gf, gb = forward(gf), backward(gb)
            xf, xb = forward(xf), backward(xb)
        elif step == 3:
            gb, xf = backward(gb), forward(xf)
        else:
            here_x, here_g = [xf], [gb]
            tf, ob = forward(backs[6]), backward(outs[5])
        if step == 1:
            here_x, here_g = [tokens, *here_x], [both, *here_g]
        out, back, small = expert(here_x, here_g, matrices, f"expert_{step}")
        if step < 3:
            gf, gb, first = tie(gf, gb, small[0])
            xf, xb, first = tie(xf, xb, first)
        elif step == 3:
            gb, xf, first = tie(gb, xf, small[0])
        else:
            tf, ob, first = tie(tf, ob, small[0])
        all_x += here_x
        all_g += here_g
        outs += out
        backs += back
        smalls.append([first, *small[1:]])

    scaled, d_gate, d_up, combs = (list(v) for v in zip(*smalls))
    two = [tokens.shape] * 2

    def summed(part_f, got_f, part_b, got_b, name):
        return by_columns(pair_kernel, [part_f, got_f, part_b, got_b], two, name)

    of, tb = forward(outs[7]), backward(backs[7])
    tf, ob = summed(backs[4], tf, outs[3], ob, "sum_a2")
    tf, ob, scaled[-1] = tie(tf, ob, scaled[-1])
    tf, ob = forward(tf), backward(ob)
    away_d, kept_d = gradient(all_g, tok_rows, [scaled], "grad_down")
    away_g, kept_g = gradient(all_x, tok_rows, [d_gate], "grad_gate")
    of, tb = summed(outs[6], of, backs[5], tb, "sum_b3")
    of, tb, tf, ob, away_d, away_g, d_up[-1] = tie(of, tb, tf, ob, away_d, away_g, d_up[-1])

    of, tb, got_d, got_g = forward(of), backward(tb), core_swap(away_d), core_swap(away_g)
    tf, ob = summed(backs[2], tf, outs[1], ob, "sum_a1")
    got_d, got_g = tie(got_d, got_g)
    first_d, other_d = y_parts(kept_d, got_d, "half_down")
    tf, ob, first_d, other_d, d_up[-1] = tie(tf, ob, first_d, other_d, d_up[-1])
    tf, ob, first_d, other_d = forward(tf), backward(ob), y_swap(first_d), y_swap(other_d)
    away_u, kept_u = gradient(all_x, tok_rows, [d_up], "grad_up")
    first_g, other_g = y_parts(kept_g, got_g, "half_gate")
    of, tb = summed(outs[4], of, backs[3], tb, "sum_b2")
    of, tb, tf, ob, first_d, other_d, first_g, other_g, away_u, combs[-1] = tie(
        of, tb, tf, ob, first_d, other_d, first_g, other_g, away_u, combs[-1]
    )

    of, tb, got_u = forward(of), backward(tb), core_swap(away_u)
    first_g, other_g = y_swap(first_g), y_swap(other_g)
    first_u, other_u = y_parts(kept_u, got_u, "half_up")
    d_w_down = last_add(kept_d, got_d, [first_d, other_d], False, "sum_down")
    d_comb = jnp.concatenate(combs, axis=1).reshape(groups, tok_rows)
    table = ring_sources()
    inverse = jnp.asarray([[row.index(e) for e in range(groups)] for row in table], jnp.int32)[me]
    d_comb = d_comb[inverse]
    of, tb, first_g, other_g, first_u, other_u, d_comb, d_w_down = tie(
        of, tb, first_g, other_g, first_u, other_u, d_comb, d_w_down
    )

    of, tb = summed(outs[2], of, backs[1], tb, "sum_b1")
    of, tb, first_u, other_u = forward(of), backward(tb), y_swap(first_u), y_swap(other_u)
    d_w_gate = last_add(kept_g, got_g, [first_g, other_g], True, "sum_gate")
    returned = lax.all_to_all(d_comb, "expert", split_axis=0, concat_axis=0, tiled=True)
    d_combine = jnp.sum(jnp.where(chosen, returned.T[:, None, :], 0.0), axis=2)
    output, d_tokens = by_columns(
        end_kernel, [outs[0], of, ob, backs[0], tf, tb], two, "sum_end"
    )
    d_w_up = last_add(kept_u, got_u, [first_u, other_u], True, "sum_up")
    return output, d_tokens, d_combine, d_w_gate, d_w_up, d_w_down


def solution(mesh):
    rows = P(("dp", "expert"), None)
    small = mesh.shape["expert"] == len(RING) and mesh.shape["dp"] == 4
    return jax.shard_map(
        gathered_plan if small else routed_plan,
        mesh=mesh,
        in_specs=(rows, rows, rows, rows) + (P("expert", None, None),) * 3,
        out_specs=(
            rows,
            rows,
            rows,
            P("expert", "dp", None),
            P("expert", "dp", None),
            P("expert", None, "dp"),
        ),
        check_vma=False,
    )
```

```python
import functools
import jax
import jax.numpy as jnp
from jax import lax
from jax.experimental import pallas as pl
from jax.experimental.pallas import tpu as pltpu
from jax.sharding import PartitionSpec as P


def slot_map(routes, experts, capacity):
    flat_ids = routes.reshape(-1)
    onehot = (flat_ids[:, None] == jnp.arange(experts, dtype=jnp.int32)[None, :]).astype(jnp.int32)
    before = jnp.cumsum(onehot, axis=0) - onehot
    slots = jnp.sum(before * onehot, axis=1)
    target = flat_ids * capacity + slots
    source = (
        jnp.full((experts * capacity,), -1, jnp.int32)
        .at[target]
        .set(jnp.arange(flat_ids.shape[0], dtype=jnp.int32))
    )
    return (target, source)


def routed_plan(tokens, routes, combine, cotangent, w_gate, w_up, w_down):
    tok_rows, features = tokens.shape
    per_token = routes.shape[1]
    groups = lax.axis_size("expert")
    local_exp = w_gate.shape[0]
    experts = local_exp * groups
    capacity = 3 * tok_rows * per_token // (2 * experts)
    target, source = slot_map(routes, experts, capacity)
    filled = (source >= 0)[:, None]
    pair_index = jnp.maximum(source, 0)
    owner_row = pair_index // per_token
    outgoing = jnp.where(filled, tokens[owner_row], jnp.zeros((), jnp.bfloat16))
    outgoing = outgoing.reshape(groups, local_exp, capacity, features)
    cot_float = cotangent.astype(jnp.float32)
    scaled = (combine[:, :, None] * cot_float[:, None, :]).reshape(tok_rows * per_token, features)
    outgoing_grad = jnp.where(filled, scaled[pair_index], 0.0).astype(jnp.bfloat16)
    outgoing_grad = outgoing_grad.reshape(groups, local_exp, capacity, features)
    arrived = lax.all_to_all(outgoing, "expert", split_axis=0, concat_axis=0, tiled=True)
    gate_pre = jnp.einsum("secd,edf->secf", arrived, w_gate, preferred_element_type=jnp.float32)
    up_pre = jnp.einsum("secd,edf->secf", arrived, w_up, preferred_element_type=jnp.float32)
    activated = jax.nn.silu(gate_pre)
    hidden = (activated * up_pre).astype(jnp.bfloat16)
    produced = jnp.einsum(
        "secf,efd->secd", hidden, w_down, preferred_element_type=jnp.float32
    ).astype(jnp.bfloat16)
    returned = lax.all_to_all(produced, "expert", split_axis=0, concat_axis=0, tiled=True)
    d_in = lax.all_to_all(outgoing_grad, "expert", split_axis=0, concat_axis=0, tiled=True)
    d_hidden = jnp.einsum("secd,efd->secf", d_in, w_down, preferred_element_type=jnp.float32)
    part_down = jnp.einsum("secf,secd->efd", hidden, d_in, preferred_element_type=jnp.float32)
    sigmoid_g = jax.nn.sigmoid(gate_pre)
    d_gate = (d_hidden * up_pre * sigmoid_g * (1.0 + gate_pre * (1.0 - sigmoid_g))).astype(
        jnp.bfloat16
    )
    d_up = (d_hidden * activated).astype(jnp.bfloat16)
    part_gate = jnp.einsum("secd,secf->edf", arrived, d_gate, preferred_element_type=jnp.float32)
    part_up = jnp.einsum("secd,secf->edf", arrived, d_up, preferred_element_type=jnp.float32)
    d_rows = (
        jnp.einsum("secf,edf->secd", d_gate, w_gate, preferred_element_type=jnp.float32)
        + jnp.einsum("secf,edf->secd", d_up, w_up, preferred_element_type=jnp.float32)
    ).astype(jnp.bfloat16)
    back = lax.all_to_all(d_rows, "expert", split_axis=0, concat_axis=0, tiled=True)
    per_slot = returned.reshape(experts * capacity, features)[target]
    per_slot = per_slot.reshape(tok_rows, per_token, features).astype(jnp.float32)
    output = jnp.sum(combine[:, :, None] * per_slot, axis=1).astype(jnp.bfloat16)
    d_combine = jnp.sum(per_slot * cot_float[:, None, :], axis=2)
    back_slot = back.reshape(experts * capacity, features)[target]
    back_slot = back_slot.reshape(tok_rows, per_token, features).astype(jnp.float32)
    d_tokens = jnp.sum(back_slot, axis=1).astype(jnp.bfloat16)
    sum_gate, sum_up, sum_down = (
        lax.psum_scatter(
            part_gate.astype(jnp.bfloat16), "dp", scatter_dimension=1, tiled=True
        ).astype(jnp.float32),
        lax.psum_scatter(
            part_up.astype(jnp.bfloat16), "dp", scatter_dimension=1, tiled=True
        ).astype(jnp.float32),
        lax.psum_scatter(
            part_down.astype(jnp.bfloat16), "dp", scatter_dimension=2, tiled=True
        ).astype(jnp.float32),
    )
    d_w_down = sum_down.astype(jnp.bfloat16)
    return (
        output,
        d_tokens,
        d_combine,
        sum_gate.astype(jnp.bfloat16),
        sum_up.astype(jnp.bfloat16),
        d_w_down,
    )


RING = (0, 1, 3, 5, 7, 6, 4, 2)


def ring_perms():
    n = len(RING)
    fwd = [(RING[i], RING[(i + 1) % n]) for i in range(n)]
    bwd = [(RING[(i + 1) % n], RING[i]) for i in range(n)]
    return fwd, bwd


def ring_sources():
    n = len(RING)
    place = {e: i for i, e in enumerate(RING)}
    steps = (0, -1, 1, -2, 2, -3, 3, 4)
    return [[RING[(place[e] + r) % n] for r in steps] for e in range(n)]


def forward(value):
    return lax.ppermute(value, "expert", ring_perms()[0])


def backward(value):
    return lax.ppermute(value, "expert", ring_perms()[1])


def tie(*values):
    return lax.optimization_barrier(values)


def add_rounded(a, b):
    return (a.astype(jnp.float32) + b.astype(jnp.float32)).astype(jnp.bfloat16)


def core_swap(away):
    n = lax.axis_size("dp")
    return lax.ppermute(away, "dp", [(j, j ^ 1) for j in range(n)])


def pick(halves, y):
    return lax.dynamic_index_in_dim(halves, y, 0, keepdims=False)


def y_parts(kept, got):
    y = lax.axis_index("dp") // 2
    half = kept.shape[1] // 2
    kept, got = pick(kept, 1 - y), pick(got, 1 - y)
    return add_rounded(kept[:half], got[:half]), add_rounded(kept[half:], got[half:])


def y_swap(other):
    n = lax.axis_size("dp")
    return lax.ppermute(other, "dp", [(j, j ^ 2) for j in range(n)])


ANY = pl.BlockSpec(memory_space=pl.ANY)
KERNEL_VMEM = 60 * 1024 * 1024
EXTRA = 16


class Mover:
    def __init__(self, sems):
        self.sems = sems
        self.used = 0

    def go(self, src, dst):
        copy = pltpu.make_async_copy(src, dst, self.sems.at[self.used])
        self.used += 1
        copy.start()
        return copy


def gradient_kernel(part, spots, tall_spots, core, *refs):
    n, m = len(spots), len(tall_spots)
    wide, narrow, refs = refs[:n], refs[n:n + m], refs[n + m:]
    away, kept, xs, st, ov, sems = refs
    quarters, _, size = xs.shape
    move = Mover(sems)
    load_s = [
        move.go(r, st.at[pl.ds(top, r.shape[0]), pl.ds(at, r.shape[1])])
        for r, (top, at) in zip(narrow, tall_spots)
    ]

    def load_quarter(i):
        c = core[0] if i >= quarters // 2 else 1 - core[0]
        first = pl.multiple_of(((i % (quarters // 2)) * 2 + c) * size, size)
        return [
            move.go(r.at[pl.ds(0, part), pl.ds(first, size)], xs.at[i, pl.ds(at, part)])
            for r, at in zip(wide, spots)
        ]

    load_x = [load_quarter(0), load_quarter(1)]
    for c in load_s:
        c.wait()
    stores = []
    for i in range(quarters):
        for c in load_x[i]:
            c.wait()
        if i + 2 < quarters:
            load_x.append(load_quarter(i + 2))
        for f in range(0, st.shape[0], 256):
            ov[i, f:f + 256, :] = jnp.dot(
                st[f:f + 256, :], xs[i], preferred_element_type=jnp.float32
            ).astype(jnp.bfloat16)
        half = quarters // 2
        stores.append(move.go(ov.at[i], away.at[i] if i < half else kept.at[i - half]))
    for c in stores:
        c.wait()


FREE = pl.CostEstimate(flops=0, bytes_accessed=0, transcendentals=0)


def gradient(wide, part, narrows, name):
    n_dp = lax.axis_size("dp")
    spots, at = [part * i for i in range(len(wide))], part * len(wide)
    flat, tall_spots, tall = [], [], 0
    for pieces in narrows:
        col = 0
        for piece in pieces:
            flat.append(piece)
            tall_spots.append((tall, col))
            col += piece.shape[1]
        tall += pieces[0].shape[0]
    size = wide[0].shape[1] // n_dp
    half = jax.ShapeDtypeStruct((n_dp // 2, tall, size), jnp.bfloat16)
    core = (lax.axis_index("dp") % 2).reshape(1)
    return pl.pallas_call(
        functools.partial(gradient_kernel, part, tuple(spots), tuple(tall_spots)),
        out_shape=[half, half],
        in_specs=[pl.BlockSpec(memory_space=pltpu.SMEM)] + [ANY] * (len(wide) + len(flat)),
        out_specs=[ANY, ANY],
        scratch_shapes=[
            pltpu.VMEM((n_dp, at, size), jnp.bfloat16),
            pltpu.VMEM((tall, at), jnp.bfloat16),
            pltpu.VMEM((n_dp, tall, size), jnp.bfloat16),
            pltpu.SemaphoreType.DMA((len(flat) + n_dp * len(wide) + n_dp,)),
        ],
        compiler_params=pltpu.CompilerParams(vmem_limit_bytes=KERNEL_VMEM),
        cost_estimate=FREE,
        name=name,
    )(core, *wide, *flat)


def total_of(*values):
    total = values[0].astype(jnp.float32)
    for v in values[1:]:
        total = total + v.astype(jnp.float32)
    return total.astype(jnp.bfloat16)


def pair_kernel(part_f, got_f, part_b, got_b, f, b):
    f[...] = total_of(part_f[...], got_f[...])
    b[...] = total_of(part_b[...], got_b[...])


def end_kernel(own_o, of, ob, own_t, tf, tb, o, t):
    o[...] = total_of(own_o[...], of[...], ob[...])
    t[...] = total_of(own_t[...], tf[...], tb[...])


def by_columns(kernel, operands, out_shapes, name):
    features = out_shapes[0][-1]
    steps = 2

    def spec(shape):
        block = tuple(shape[:-1]) + (features // steps,)
        return pl.BlockSpec(block, lambda i, n=len(shape): (0,) * (n - 1) + (i,))

    return pl.pallas_call(
        kernel,
        out_shape=[jax.ShapeDtypeStruct(s, jnp.bfloat16) for s in out_shapes],
        grid=(steps,),
        in_specs=[spec(v.shape) for v in operands],
        out_specs=[spec(s) for s in out_shapes],
        compiler_params=pltpu.CompilerParams(vmem_limit_bytes=KERNEL_VMEM),
        cost_estimate=FREE,
        name=name,
    )(*operands)


def last_add_kernel(turned, y, kept, got, last_0, last_1, out):
    half = last_0.shape[0]
    for i, last in enumerate((last_0, last_1)):
        rows = pl.ds(i * half, half)
        total = kept[0, rows].astype(jnp.float32) + got[0, rows].astype(jnp.float32)
        total = total + last[...].astype(jnp.float32)
        if turned:
            out[0, :, rows] = total.T.astype(jnp.bfloat16)
        else:
            out[0, rows] = total.astype(jnp.bfloat16)


def last_add(kept, got, lasts, turned, name):
    _, ff, size = kept.shape
    y = (lax.axis_index("dp") // 2).reshape(1)
    shape = (1, size, ff) if turned else (1, ff, size)
    half = pl.BlockSpec((1, ff, size), lambda i, y: (y[0], 0, 0))
    piece = pl.BlockSpec((ff // 2, size), lambda i, y: (0, 0))
    return pl.pallas_call(
        functools.partial(last_add_kernel, turned),
        out_shape=jax.ShapeDtypeStruct(shape, jnp.bfloat16),
        grid_spec=pltpu.PrefetchScalarGridSpec(
            num_scalar_prefetch=1,
            grid=(1,),
            in_specs=[half, half, piece, piece],
            out_specs=pl.BlockSpec(shape, lambda i, y: (0, 0, 0)),
        ),
        compiler_params=pltpu.CompilerParams(vmem_limit_bytes=KERNEL_VMEM),
        cost_estimate=FREE,
        name=name,
    )(y, kept, got, *lasts)


def with_weights_kernel(cot, routes, combine, out):
    rows, features = cot.shape
    out[:rows] = cot[...]
    line = lax.broadcasted_iota(jnp.int32, (EXTRA, rows), 0)
    weights = jnp.zeros((EXTRA, rows), jnp.float32)
    for k in range(routes.shape[0]):
        weights += jnp.where(routes[k:k + 1] == line, combine[k:k + 1], 0.0)
    wide = weights * 65537.0
    high = wide - (wide - weights)
    rest = weights - high
    wide = rest * 65537.0
    middle = wide - (wide - rest)
    out[rows:] = jnp.zeros((EXTRA, features), jnp.bfloat16)
    for i, term in enumerate((high, middle, rest - middle)):
        out[rows:, i * rows:(i + 1) * rows] = term.astype(jnp.bfloat16)


def with_weights(cot, routes, combine):
    return pl.pallas_call(
        with_weights_kernel,
        out_shape=jax.ShapeDtypeStruct((cot.shape[0] + EXTRA, cot.shape[1]), cot.dtype),
        cost_estimate=FREE,
        name="with_weights",
    )(cot, routes.T, combine.T)


def expert_kernel(n, me, *refs):
    xs, gs, refs = refs[:n], refs[n:2 * n], refs[2 * n:]
    wg, wu, wd, wdt, wgt, wut = refs[:6]
    outs, backs, refs = refs[6:6 + n], refs[6 + n:6 + 2 * n], refs[6 + 2 * n:]
    s_o, dg_o, du_o, comb_o = refs[:4]
    x2, g2, wgv, wuv, wdv, wdtv, wgtv, wutv, gv, uv, sv, dgv, duv, wb, wv, st, dgt, dut, ov, rv, sems = refs[4:]
    part = xs[0].shape[0]
    rows, features = x2.shape
    ff = gv.shape[1]
    f32, bf16 = jnp.float32, jnp.bfloat16
    move = Mover(sems)
    cols = [pl.ds(f, 256) for f in range(0, ff, 256)]
    wide = [pl.ds(d, 512) for d in range(0, features, 512)]
    spots = [pl.ds(i * part, part) for i in range(n)]

    def load(src, dst, pieces):
        size = src.shape[0] // pieces
        return [
            move.go(src.at[pl.ds(i * size, size)], dst.at[pl.ds(i * size, size)])
            for i in range(pieces)
        ]

    load_x = [move.go(r, x2.at[s]) for r, s in zip(xs, spots)]
    span = wb.shape[2]
    load_w = [move.go(r.at[pl.ds(part, EXTRA), pl.ds(0, span)], wb.at[i]) for i, r in enumerate(gs)]
    load_g = load(wg, wgv, 4)
    load_u = load(wu, wuv, 4)
    load_cot = [move.go(r.at[pl.ds(0, part)], g2.at[s]) for r, s in zip(gs, spots)]
    load_d = load(wd, wdv, 4)
    load_dt = load(wdt, wdtv, 4)
    load_gt = load(wgt, wgtv, 4)
    load_ut = load(wut, wutv, 4)
    for c in load_w:
        c.wait()
    for i, s in enumerate(spots):
        terms = wb[i].astype(f32)
        mine = lax.broadcasted_iota(jnp.int32, terms.shape, 0) == me[0]
        terms = jnp.sum(jnp.where(mine, terms, 0.0), axis=0, keepdims=True)
        terms = terms[:, :part] + terms[:, part:2 * part] + terms[:, 2 * part:]
        wv[s, :] = jnp.broadcast_to(terms, (128, part)).T[:, :1]
    for c in load_x + load_g:
        c.wait()
    for c in cols:
        gv[:, c] = jnp.dot(x2[...], wgv[:, c], preferred_element_type=f32)
    for c in load_u:
        c.wait()
    for c in cols:
        up = jnp.dot(x2[...], wuv[:, c], preferred_element_type=f32)
        uv[:, c] = up
        gate = gv[:, c]
        scaled = (gate * jax.nn.sigmoid(gate) * up * wv[...]).astype(bf16)
        sv[:, c] = scaled
        st[c, :] = scaled.T
    stores = [move.go(st, s_o)]
    for c in load_d:
        c.wait()
    for c in wide:
        ov[:, c] = jnp.dot(sv[...], wdv[:, c], preferred_element_type=f32).astype(bf16)
    stores += [move.go(ov.at[s], r) for r, s in zip(outs, spots)]
    for c in load_cot + load_dt:
        c.wait()
    comb = jnp.zeros((rows, 1), f32)
    for c in cols:
        d_raw = jnp.dot(g2[...], wdtv[:, c], preferred_element_type=f32)
        gate, up = gv[:, c], uv[:, c]
        sig = jax.nn.sigmoid(gate)
        act = gate * sig
        comb += jnp.sum(act * up * d_raw, axis=1, keepdims=True)
        d_hidden = d_raw * wv[...]
        d_gate = (d_hidden * up * sig * (1.0 + gate * (1.0 - sig))).astype(bf16)
        d_up = (d_hidden * act).astype(bf16)
        dgv[:, c] = d_gate
        duv[:, c] = d_up
        dgt[c, :] = d_gate.T
        dut[c, :] = d_up.T
    comb_o[...] = jnp.broadcast_to(comb, (rows, 128)).T[:1, :]
    stores += [move.go(dgt, dg_o), move.go(dut, du_o)]
    for c in load_gt + load_ut:
        c.wait()
    for c in wide:
        rv[:, c] = (
            jnp.dot(dgv[...], wgtv[:, c], preferred_element_type=f32)
            + jnp.dot(duv[...], wutv[:, c], preferred_element_type=f32)
        ).astype(bf16)
    stores += [move.go(rv.at[s], r) for r, s in zip(backs, spots)]
    for c in stores:
        c.wait()


def expert(xs, gs, matrices, name):
    n, (part, features) = len(xs), xs[0].shape
    ff = matrices[0].shape[1]
    rows = n * part
    bf16, f32 = jnp.bfloat16, jnp.float32
    vmem = pl.BlockSpec(memory_space=pltpu.VMEM)
    block = jax.ShapeDtypeStruct((part, features), bf16)
    turned = jax.ShapeDtypeStruct((ff, rows), bf16)
    me = lax.axis_index("expert").reshape(1)
    res = pl.pallas_call(
        functools.partial(expert_kernel, n),
        out_shape=[block] * (2 * n) + [turned] * 3 + [jax.ShapeDtypeStruct((1, rows), f32)],
        in_specs=[pl.BlockSpec(memory_space=pltpu.SMEM)] + [ANY] * (2 * n + 6),
        out_specs=[ANY] * (2 * n + 3) + [vmem],
        scratch_shapes=[
            pltpu.VMEM((rows, features), bf16),
            pltpu.VMEM((rows, features), bf16),
            pltpu.VMEM((features, ff), bf16),
            pltpu.VMEM((features, ff), bf16),
            pltpu.VMEM((ff, features), bf16),
            pltpu.VMEM((features, ff), bf16),
            pltpu.VMEM((ff, features), bf16),
            pltpu.VMEM((ff, features), bf16),
            pltpu.VMEM((rows, ff), f32),
            pltpu.VMEM((rows, ff), f32),
            pltpu.VMEM((rows, ff), bf16),
            pltpu.VMEM((rows, ff), bf16),
            pltpu.VMEM((rows, ff), bf16),
            pltpu.VMEM((n, EXTRA, 3 * part), bf16),
            pltpu.VMEM((rows, 1), f32),
            pltpu.VMEM((ff, rows), bf16),
            pltpu.VMEM((ff, rows), bf16),
            pltpu.VMEM((ff, rows), bf16),
            pltpu.VMEM((rows, features), bf16),
            pltpu.VMEM((rows, features), bf16),
            pltpu.SemaphoreType.DMA((5 * n + 27,)),
        ],
        compiler_params=pltpu.CompilerParams(vmem_limit_bytes=KERNEL_VMEM),
        cost_estimate=FREE,
        name=name,
    )(me, *xs, *gs, *matrices)
    return res[:n], res[n:2 * n], res[2 * n:]


def gathered_plan(tokens, routes, combine, cotangent, w_gate, w_up, w_down):
    tok_rows, features = tokens.shape
    groups = lax.axis_size("expert")
    me = lax.axis_index("expert")
    chosen = routes[:, :, None] == jnp.arange(groups, dtype=jnp.int32)[None, None, :]
    matrices = [w_gate[0], w_up[0], w_down[0], w_down[0].T, w_gate[0].T, w_up[0].T]

    xs = [forward(tokens), backward(tokens)]
    both = with_weights(cotangent, routes, combine)
    gs = [forward(both), backward(both)]
    gf, gb, m3, m4, m5 = tie(*gs, *matrices[3:])
    matrices = matrices[:3] + [m3, m4, m5]
    xf, xb = xs
    all_x, all_g, outs, backs, smalls = [], [], [], [], []
    for step in range(1, 5):
        here_x, here_g = [xf, xb], [gf, gb]
        if step < 3:
            gf, gb = forward(gf), backward(gb)
            xf, xb = forward(xf), backward(xb)
        elif step == 3:
            gb, xf = backward(gb), forward(xf)
        else:
            here_x, here_g = [xf], [gb]
            tf, ob = forward(backs[6]), backward(outs[5])
        if step == 1:
            here_x, here_g = [tokens, *here_x], [both, *here_g]
        out, back, small = expert(here_x, here_g, matrices, f"expert_{step}")
        if step < 3:
            gf, gb, first = tie(gf, gb, small[0])
            xf, xb, first = tie(xf, xb, first)
        elif step == 3:
            gb, xf, first = tie(gb, xf, small[0])
        else:
            tf, ob, first = tie(tf, ob, small[0])
        all_x += here_x
        all_g += here_g
        outs += out
        backs += back
        smalls.append([first, *small[1:]])

    scaled, d_gate, d_up, combs = (list(v) for v in zip(*smalls))
    two = [tokens.shape] * 2

    def summed(part_f, got_f, part_b, got_b, name):
        return by_columns(pair_kernel, [part_f, got_f, part_b, got_b], two, name)

    of, tb = forward(outs[7]), backward(backs[7])
    tf, ob = summed(backs[4], tf, outs[3], ob, "sum_a2")
    away_d, kept_d = gradient(all_g, tok_rows, [scaled], "grad_down")
    of, tb, tf, ob, away_d, d_gate[-1] = tie(of, tb, tf, ob, away_d, d_gate[-1])

    tf, ob, got_d = forward(tf), backward(ob), core_swap(away_d)
    of, tb = summed(outs[6], of, backs[5], tb, "sum_b3")
    first_d, other_d = y_parts(kept_d, got_d)
    first_d = y_swap(first_d)
    away_g, kept_g = gradient(all_x, tok_rows, [d_gate], "grad_gate")
    tf, ob, of, tb, away_g, d_up[-1], first_d, other_d = tie(
        tf, ob, of, tb, away_g, d_up[-1], first_d, other_d
    )

    of, tb, got_g, other_d = forward(of), backward(tb), core_swap(away_g), y_swap(other_d)
    tf, ob = summed(backs[2], tf, outs[1], ob, "sum_a1")
    first_g, other_g = y_parts(kept_g, got_g)
    away_u, kept_u = gradient(all_x, tok_rows, [d_up], "grad_up")
    of, tb, tf, ob, away_u, other_d, first_g, other_g, combs[-1] = tie(
        of, tb, tf, ob, away_u, other_d, first_g, other_g, combs[-1]
    )

    tf, ob, got_u, first_g = forward(tf), backward(ob), core_swap(away_u), y_swap(first_g)
    of, tb = summed(outs[4], of, backs[3], tb, "sum_b2")
    d_w_down = last_add(kept_d, got_d, [first_d, other_d], False, "sum_down")
    first_u, other_u = y_parts(kept_u, got_u)
    d_comb = jnp.concatenate(combs, axis=1).reshape(groups, tok_rows)
    table = ring_sources()
    inverse = jnp.asarray([[row.index(e) for e in range(groups)] for row in table], jnp.int32)[me]
    d_comb = d_comb[inverse]
    tf, ob, of, tb, first_g, first_u, other_u, d_comb, d_w_down = tie(
        tf, ob, of, tb, first_g, first_u, other_u, d_comb, d_w_down
    )

    of, tb, other_g, first_u = forward(of), backward(tb), y_swap(other_g), y_swap(first_u)
    of, tb, other_g, first_u, d_comb = tie(of, tb, other_g, first_u, d_comb)

    of, tb = summed(outs[2], of, backs[1], tb, "sum_b1")
    of, tb, other_u = forward(of), backward(tb), y_swap(other_u)
    d_w_gate = last_add(kept_g, got_g, [first_g, other_g], True, "sum_gate")
    returned = lax.all_to_all(d_comb, "expert", split_axis=0, concat_axis=0, tiled=True)
    other_u, d_w_gate, returned, of, tb = tie(other_u, d_w_gate, returned, of, tb)
    d_combine = jnp.sum(jnp.where(chosen, returned.T[:, None, :], 0.0), axis=2)
    d_w_up = last_add(kept_u, got_u, [first_u, other_u], True, "sum_up")
    output, d_tokens = by_columns(
        end_kernel, [outs[0], of, ob, backs[0], tf, tb], two, "sum_end"
    )
    return output, d_tokens, d_combine, d_w_gate, d_w_up, d_w_down


def solution(mesh):
    rows = P(("dp", "expert"), None)
    small = mesh.shape["expert"] == len(RING) and mesh.shape["dp"] == 4
    return jax.shard_map(
        gathered_plan if small else routed_plan,
        mesh=mesh,
        in_specs=(rows, rows, rows, rows) + (P("expert", None, None),) * 3,
        out_specs=(
            rows,
            rows,
            rows,
            P("expert", "dp", None),
            P("expert", "dp", None),
            P("expert", None, "dp"),
        ),
        check_vma=False,
    )
```

```python
import functools
import jax
import jax.numpy as jnp
from jax import lax
from jax.experimental import pallas as pl
from jax.experimental.pallas import tpu as pltpu
from jax.sharding import PartitionSpec as P


def slot_map(routes, experts, capacity):
    flat_ids = routes.reshape(-1)
    onehot = (flat_ids[:, None] == jnp.arange(experts, dtype=jnp.int32)[None, :]).astype(jnp.int32)
    before = jnp.cumsum(onehot, axis=0) - onehot
    slots = jnp.sum(before * onehot, axis=1)
    target = flat_ids * capacity + slots
    source = (
        jnp.full((experts * capacity,), -1, jnp.int32)
        .at[target]
        .set(jnp.arange(flat_ids.shape[0], dtype=jnp.int32))
    )
    return (target, source)


def routed_plan(tokens, routes, combine, cotangent, w_gate, w_up, w_down):
    tok_rows, features = tokens.shape
    per_token = routes.shape[1]
    groups = lax.axis_size("expert")
    local_exp = w_gate.shape[0]
    experts = local_exp * groups
    capacity = 3 * tok_rows * per_token // (2 * experts)
    target, source = slot_map(routes, experts, capacity)
    filled = (source >= 0)[:, None]
    pair_index = jnp.maximum(source, 0)
    owner_row = pair_index // per_token
    outgoing = jnp.where(filled, tokens[owner_row], jnp.zeros((), jnp.bfloat16))
    outgoing = outgoing.reshape(groups, local_exp, capacity, features)
    cot_float = cotangent.astype(jnp.float32)
    scaled = (combine[:, :, None] * cot_float[:, None, :]).reshape(tok_rows * per_token, features)
    outgoing_grad = jnp.where(filled, scaled[pair_index], 0.0).astype(jnp.bfloat16)
    outgoing_grad = outgoing_grad.reshape(groups, local_exp, capacity, features)
    arrived = lax.all_to_all(outgoing, "expert", split_axis=0, concat_axis=0, tiled=True)
    gate_pre = jnp.einsum("secd,edf->secf", arrived, w_gate, preferred_element_type=jnp.float32)
    up_pre = jnp.einsum("secd,edf->secf", arrived, w_up, preferred_element_type=jnp.float32)
    activated = jax.nn.silu(gate_pre)
    hidden = (activated * up_pre).astype(jnp.bfloat16)
    produced = jnp.einsum(
        "secf,efd->secd", hidden, w_down, preferred_element_type=jnp.float32
    ).astype(jnp.bfloat16)
    returned = lax.all_to_all(produced, "expert", split_axis=0, concat_axis=0, tiled=True)
    d_in = lax.all_to_all(outgoing_grad, "expert", split_axis=0, concat_axis=0, tiled=True)
    d_hidden = jnp.einsum("secd,efd->secf", d_in, w_down, preferred_element_type=jnp.float32)
    part_down = jnp.einsum("secf,secd->efd", hidden, d_in, preferred_element_type=jnp.float32)
    sigmoid_g = jax.nn.sigmoid(gate_pre)
    d_gate = (d_hidden * up_pre * sigmoid_g * (1.0 + gate_pre * (1.0 - sigmoid_g))).astype(
        jnp.bfloat16
    )
    d_up = (d_hidden * activated).astype(jnp.bfloat16)
    part_gate = jnp.einsum("secd,secf->edf", arrived, d_gate, preferred_element_type=jnp.float32)
    part_up = jnp.einsum("secd,secf->edf", arrived, d_up, preferred_element_type=jnp.float32)
    d_rows = (
        jnp.einsum("secf,edf->secd", d_gate, w_gate, preferred_element_type=jnp.float32)
        + jnp.einsum("secf,edf->secd", d_up, w_up, preferred_element_type=jnp.float32)
    ).astype(jnp.bfloat16)
    back = lax.all_to_all(d_rows, "expert", split_axis=0, concat_axis=0, tiled=True)
    per_slot = returned.reshape(experts * capacity, features)[target]
    per_slot = per_slot.reshape(tok_rows, per_token, features).astype(jnp.float32)
    output = jnp.sum(combine[:, :, None] * per_slot, axis=1).astype(jnp.bfloat16)
    d_combine = jnp.sum(per_slot * cot_float[:, None, :], axis=2)
    back_slot = back.reshape(experts * capacity, features)[target]
    back_slot = back_slot.reshape(tok_rows, per_token, features).astype(jnp.float32)
    d_tokens = jnp.sum(back_slot, axis=1).astype(jnp.bfloat16)
    sum_gate, sum_up, sum_down = (
        lax.psum_scatter(
            part_gate.astype(jnp.bfloat16), "dp", scatter_dimension=1, tiled=True
        ).astype(jnp.float32),
        lax.psum_scatter(
            part_up.astype(jnp.bfloat16), "dp", scatter_dimension=1, tiled=True
        ).astype(jnp.float32),
        lax.psum_scatter(
            part_down.astype(jnp.bfloat16), "dp", scatter_dimension=2, tiled=True
        ).astype(jnp.float32),
    )
    d_w_down = sum_down.astype(jnp.bfloat16)
    return (
        output,
        d_tokens,
        d_combine,
        sum_gate.astype(jnp.bfloat16),
        sum_up.astype(jnp.bfloat16),
        d_w_down,
    )


RING = (0, 1, 3, 5, 7, 6, 4, 2)


def ring_perms():
    n = len(RING)
    fwd = [(RING[i], RING[(i + 1) % n]) for i in range(n)]
    bwd = [(RING[(i + 1) % n], RING[i]) for i in range(n)]
    return fwd, bwd


def ring_sources():
    n = len(RING)
    place = {e: i for i, e in enumerate(RING)}
    steps = (0, -1, 1, -2, 2, -3, 3, 4)
    return [[RING[(place[e] + r) % n] for r in steps] for e in range(n)]


def forward(value):
    return lax.ppermute(value, "expert", ring_perms()[0])


def backward(value):
    return lax.ppermute(value, "expert", ring_perms()[1])


def tie(*values):
    return lax.optimization_barrier(values)


def add_rounded(a, b):
    return (a.astype(jnp.float32) + b.astype(jnp.float32)).astype(jnp.bfloat16)


def core_swap(away):
    n = lax.axis_size("dp")
    return lax.ppermute(away, "dp", [(j, j ^ 1) for j in range(n)])


def pick(halves, y):
    return lax.dynamic_index_in_dim(halves, y, 0, keepdims=False)


def y_part(kept, got):
    y = lax.axis_index("dp") // 2
    return add_rounded(pick(kept, 1 - y), pick(got, 1 - y))


def y_swap(other):
    n = lax.axis_size("dp")
    return lax.ppermute(other, "dp", [(j, j ^ 2) for j in range(n)])


ANY = pl.BlockSpec(memory_space=pl.ANY)
KERNEL_VMEM = 60 * 1024 * 1024
EXTRA = 16


class Mover:
    def __init__(self, sems):
        self.sems = sems
        self.used = 0

    def go(self, src, dst):
        copy = pltpu.make_async_copy(src, dst, self.sems.at[self.used])
        self.used += 1
        copy.start()
        return copy


def gradient_kernel(part, spots, tall_spots, core, *refs):
    n, m = len(spots), len(tall_spots)
    wide, narrow, refs = refs[:n], refs[n:n + m], refs[n + m:]
    away, kept, xs, st, ov, sems = refs
    quarters, _, size = xs.shape
    move = Mover(sems)
    load_s = [
        move.go(r, st.at[pl.ds(top, r.shape[0]), pl.ds(at, r.shape[1])])
        for r, (top, at) in zip(narrow, tall_spots)
    ]

    def load_quarter(i):
        c = core[0] if i >= quarters // 2 else 1 - core[0]
        first = pl.multiple_of(((i % (quarters // 2)) * 2 + c) * size, size)
        return [
            move.go(r.at[pl.ds(0, part), pl.ds(first, size)], xs.at[i, pl.ds(at, part)])
            for r, at in zip(wide, spots)
        ]

    load_x = [load_quarter(0), load_quarter(1)]
    for c in load_s:
        c.wait()
    stores = []
    for i in range(quarters):
        for c in load_x[i]:
            c.wait()
        if i + 2 < quarters:
            load_x.append(load_quarter(i + 2))
        for f in range(0, st.shape[0], 256):
            ov[i, f:f + 256, :] = jnp.dot(
                st[f:f + 256, :], xs[i], preferred_element_type=jnp.float32
            ).astype(jnp.bfloat16)
        half = quarters // 2
        stores.append(move.go(ov.at[i], away.at[i] if i < half else kept.at[i - half]))
    for c in stores:
        c.wait()


FREE = pl.CostEstimate(flops=0, bytes_accessed=0, transcendentals=0)


def gradient(wide, part, narrows, name):
    n_dp = lax.axis_size("dp")
    spots, at = [part * i for i in range(len(wide))], part * len(wide)
    flat, tall_spots, tall = [], [], 0
    for pieces in narrows:
        col = 0
        for piece in pieces:
            flat.append(piece)
            tall_spots.append((tall, col))
            col += piece.shape[1]
        tall += pieces[0].shape[0]
    size = wide[0].shape[1] // n_dp
    half = jax.ShapeDtypeStruct((n_dp // 2, tall, size), jnp.bfloat16)
    core = (lax.axis_index("dp") % 2).reshape(1)
    return pl.pallas_call(
        functools.partial(gradient_kernel, part, tuple(spots), tuple(tall_spots)),
        out_shape=[half, half],
        in_specs=[pl.BlockSpec(memory_space=pltpu.SMEM)] + [ANY] * (len(wide) + len(flat)),
        out_specs=[ANY, ANY],
        scratch_shapes=[
            pltpu.VMEM((n_dp, at, size), jnp.bfloat16),
            pltpu.VMEM((tall, at), jnp.bfloat16),
            pltpu.VMEM((n_dp, tall, size), jnp.bfloat16),
            pltpu.SemaphoreType.DMA((len(flat) + n_dp * len(wide) + n_dp,)),
        ],
        compiler_params=pltpu.CompilerParams(vmem_limit_bytes=KERNEL_VMEM),
        cost_estimate=FREE,
        name=name,
    )(core, *wide, *flat)


def total_of(*values):
    total = values[0].astype(jnp.float32)
    for v in values[1:]:
        total = total + v.astype(jnp.float32)
    return total.astype(jnp.bfloat16)


def pair_kernel(part_f, got_f, part_b, got_b, f, b):
    f[...] = total_of(part_f[...], got_f[...])
    b[...] = total_of(part_b[...], got_b[...])


def end_kernel(own_o, of, ob, own_t, tf, tb, o, t):
    o[...] = total_of(own_o[...], of[...], ob[...])
    t[...] = total_of(own_t[...], tf[...], tb[...])


def by_columns(kernel, operands, out_shapes, name):
    features = out_shapes[0][-1]
    steps = 2

    def spec(shape):
        block = tuple(shape[:-1]) + (features // steps,)
        return pl.BlockSpec(block, lambda i, n=len(shape): (0,) * (n - 1) + (i,))

    return pl.pallas_call(
        kernel,
        out_shape=[jax.ShapeDtypeStruct(s, jnp.bfloat16) for s in out_shapes],
        grid=(steps,),
        in_specs=[spec(v.shape) for v in operands],
        out_specs=[spec(s) for s in out_shapes],
        compiler_params=pltpu.CompilerParams(vmem_limit_bytes=KERNEL_VMEM),
        cost_estimate=FREE,
        name=name,
    )(*operands)


def last_add_kernel(turned, y, kept, got, last, out):
    total = kept[0].astype(jnp.float32) + got[0].astype(jnp.float32) + last[...].astype(jnp.float32)
    out[...] = (total.T if turned else total).astype(jnp.bfloat16)[None]


def last_add(kept, got, last, turned, name):
    _, ff, size = kept.shape
    y = (lax.axis_index("dp") // 2).reshape(1)
    shape = (1, size, ff) if turned else (1, ff, size)
    half = pl.BlockSpec((1, ff, size), lambda i, y: (y[0], 0, 0))
    return pl.pallas_call(
        functools.partial(last_add_kernel, turned),
        out_shape=jax.ShapeDtypeStruct(shape, jnp.bfloat16),
        grid_spec=pltpu.PrefetchScalarGridSpec(
            num_scalar_prefetch=1,
            grid=(1,),
            in_specs=[half, half, pl.BlockSpec((ff, size), lambda i, y: (0, 0))],
            out_specs=pl.BlockSpec(shape, lambda i, y: (0, 0, 0)),
        ),
        compiler_params=pltpu.CompilerParams(vmem_limit_bytes=KERNEL_VMEM),
        cost_estimate=FREE,
        name=name,
    )(y, kept, got, last)


def with_weights_kernel(cot, routes, combine, out):
    rows, features = cot.shape
    out[:rows] = cot[...]
    line = lax.broadcasted_iota(jnp.int32, (EXTRA, rows), 0)
    weights = jnp.zeros((EXTRA, rows), jnp.float32)
    for k in range(routes.shape[0]):
        weights += jnp.where(routes[k:k + 1] == line, combine[k:k + 1], 0.0)
    wide = weights * 65537.0
    high = wide - (wide - weights)
    rest = weights - high
    wide = rest * 65537.0
    middle = wide - (wide - rest)
    out[rows:] = jnp.zeros((EXTRA, features), jnp.bfloat16)
    for i, term in enumerate((high, middle, rest - middle)):
        out[rows:, i * rows:(i + 1) * rows] = term.astype(jnp.bfloat16)


def with_weights(cot, routes, combine):
    return pl.pallas_call(
        with_weights_kernel,
        out_shape=jax.ShapeDtypeStruct((cot.shape[0] + EXTRA, cot.shape[1]), cot.dtype),
        cost_estimate=FREE,
        name="with_weights",
    )(cot, routes.T, combine.T)


def expert_kernel(n, me, *refs):
    xs, gs, refs = refs[:n], refs[n:2 * n], refs[2 * n:]
    wg, wu, wd, wdt, wgt, wut = refs[:6]
    outs, backs, refs = refs[6:6 + n], refs[6 + n:6 + 2 * n], refs[6 + 2 * n:]
    s_o, dg_o, du_o, comb_o = refs[:4]
    x2, g2, wgv, wuv, wdv, wdtv, wgtv, wutv, gv, uv, sv, dgv, duv, wb, wv, st, dgt, dut, ov, rv, sems = refs[4:]
    part = xs[0].shape[0]
    rows, features = x2.shape
    ff = gv.shape[1]
    f32, bf16 = jnp.float32, jnp.bfloat16
    move = Mover(sems)
    cols = [pl.ds(f, 256) for f in range(0, ff, 256)]
    wide = [pl.ds(d, 512) for d in range(0, features, 512)]
    spots = [pl.ds(i * part, part) for i in range(n)]

    def load(src, dst, pieces):
        size = src.shape[0] // pieces
        return [
            move.go(src.at[pl.ds(i * size, size)], dst.at[pl.ds(i * size, size)])
            for i in range(pieces)
        ]

    load_x = [move.go(r, x2.at[s]) for r, s in zip(xs, spots)]
    span = wb.shape[2]
    load_w = [move.go(r.at[pl.ds(part, EXTRA), pl.ds(0, span)], wb.at[i]) for i, r in enumerate(gs)]
    load_g = load(wg, wgv, 4)
    load_u = load(wu, wuv, 4)
    load_cot = [move.go(r.at[pl.ds(0, part)], g2.at[s]) for r, s in zip(gs, spots)]
    load_d = load(wd, wdv, 4)
    load_dt = load(wdt, wdtv, 4)
    load_gt = load(wgt, wgtv, 4)
    load_ut = load(wut, wutv, 4)
    for c in load_w:
        c.wait()
    for i, s in enumerate(spots):
        terms = wb[i].astype(f32)
        mine = lax.broadcasted_iota(jnp.int32, terms.shape, 0) == me[0]
        terms = jnp.sum(jnp.where(mine, terms, 0.0), axis=0, keepdims=True)
        terms = terms[:, :part] + terms[:, part:2 * part] + terms[:, 2 * part:]
        wv[s, :] = jnp.broadcast_to(terms, (128, part)).T[:, :1]
    for c in load_x + load_g:
        c.wait()
    for c in cols:
        gv[:, c] = jnp.dot(x2[...], wgv[:, c], preferred_element_type=f32)
    for c in load_u:
        c.wait()
    for c in cols:
        up = jnp.dot(x2[...], wuv[:, c], preferred_element_type=f32)
        uv[:, c] = up
        gate = gv[:, c]
        scaled = (gate * jax.nn.sigmoid(gate) * up * wv[...]).astype(bf16)
        sv[:, c] = scaled
        st[c, :] = scaled.T
    stores = [move.go(st, s_o)]
    for c in load_d:
        c.wait()
    for c in wide:
        ov[:, c] = jnp.dot(sv[...], wdv[:, c], preferred_element_type=f32).astype(bf16)
    stores += [move.go(ov.at[s], r) for r, s in zip(outs, spots)]
    for c in load_cot + load_dt:
        c.wait()
    comb = jnp.zeros((rows, 1), f32)
    for c in cols:
        d_raw = jnp.dot(g2[...], wdtv[:, c], preferred_element_type=f32)
        gate, up = gv[:, c], uv[:, c]
        sig = jax.nn.sigmoid(gate)
        act = gate * sig
        comb += jnp.sum(act * up * d_raw, axis=1, keepdims=True)
        d_hidden = d_raw * wv[...]
        d_gate = (d_hidden * up * sig * (1.0 + gate * (1.0 - sig))).astype(bf16)
        d_up = (d_hidden * act).astype(bf16)
        dgv[:, c] = d_gate
        duv[:, c] = d_up
        dgt[c, :] = d_gate.T
        dut[c, :] = d_up.T
    comb_o[...] = jnp.broadcast_to(comb, (rows, 128)).T[:1, :]
    stores += [move.go(dgt, dg_o), move.go(dut, du_o)]
    for c in load_gt + load_ut:
        c.wait()
    for c in wide:
        rv[:, c] = (
            jnp.dot(dgv[...], wgtv[:, c], preferred_element_type=f32)
            + jnp.dot(duv[...], wutv[:, c], preferred_element_type=f32)
        ).astype(bf16)
    stores += [move.go(rv.at[s], r) for r, s in zip(backs, spots)]
    for c in stores:
        c.wait()


def expert(xs, gs, matrices, name):
    n, (part, features) = len(xs), xs[0].shape
    ff = matrices[0].shape[1]
    rows = n * part
    bf16, f32 = jnp.bfloat16, jnp.float32
    vmem = pl.BlockSpec(memory_space=pltpu.VMEM)
    block = jax.ShapeDtypeStruct((part, features), bf16)
    turned = jax.ShapeDtypeStruct((ff, rows), bf16)
    me = lax.axis_index("expert").reshape(1)
    res = pl.pallas_call(
        functools.partial(expert_kernel, n),
        out_shape=[block] * (2 * n) + [turned] * 3 + [jax.ShapeDtypeStruct((1, rows), f32)],
        in_specs=[pl.BlockSpec(memory_space=pltpu.SMEM)] + [ANY] * (2 * n + 6),
        out_specs=[ANY] * (2 * n + 3) + [vmem],
        scratch_shapes=[
            pltpu.VMEM((rows, features), bf16),
            pltpu.VMEM((rows, features), bf16),
            pltpu.VMEM((features, ff), bf16),
            pltpu.VMEM((features, ff), bf16),
            pltpu.VMEM((ff, features), bf16),
            pltpu.VMEM((features, ff), bf16),
            pltpu.VMEM((ff, features), bf16),
            pltpu.VMEM((ff, features), bf16),
            pltpu.VMEM((rows, ff), f32),
            pltpu.VMEM((rows, ff), f32),
            pltpu.VMEM((rows, ff), bf16),
            pltpu.VMEM((rows, ff), bf16),
            pltpu.VMEM((rows, ff), bf16),
            pltpu.VMEM((n, EXTRA, 3 * part), bf16),
            pltpu.VMEM((rows, 1), f32),
            pltpu.VMEM((ff, rows), bf16),
            pltpu.VMEM((ff, rows), bf16),
            pltpu.VMEM((ff, rows), bf16),
            pltpu.VMEM((rows, features), bf16),
            pltpu.VMEM((rows, features), bf16),
            pltpu.SemaphoreType.DMA((5 * n + 27,)),
        ],
        compiler_params=pltpu.CompilerParams(vmem_limit_bytes=KERNEL_VMEM),
        cost_estimate=FREE,
        name=name,
    )(me, *xs, *gs, *matrices)
    return res[:n], res[n:2 * n], res[2 * n:]


def gathered_plan(tokens, routes, combine, cotangent, w_gate, w_up, w_down):
    tok_rows, features = tokens.shape
    groups = lax.axis_size("expert")
    me = lax.axis_index("expert")
    chosen = routes[:, :, None] == jnp.arange(groups, dtype=jnp.int32)[None, None, :]
    matrices = [w_gate[0], w_up[0], w_down[0], w_down[0].T, w_gate[0].T, w_up[0].T]

    xs = [forward(tokens), backward(tokens)]
    both = with_weights(cotangent, routes, combine)
    gs = [forward(both), backward(both)]
    gf, gb, m3, m4, m5 = tie(*gs, *matrices[3:])
    matrices = matrices[:3] + [m3, m4, m5]
    xf, xb = xs
    all_x, all_g, outs, backs, smalls = [], [], [], [], []
    for step in range(1, 5):
        here_x, here_g = [xf, xb], [gf, gb]
        if step < 3:
            gf, gb = forward(gf), backward(gb)
            xf, xb = forward(xf), backward(xb)
        elif step == 3:
            gb, xf = backward(gb), forward(xf)
        else:
            here_x, here_g = [xf], [gb]
            tf, ob = forward(backs[6]), backward(outs[5])
        if step == 1:
            here_x, here_g = [tokens, *here_x], [both, *here_g]
        out, back, small = expert(here_x, here_g, matrices, f"expert_{step}")
        if step < 3:
            gf, gb, first = tie(gf, gb, small[0])
            xf, xb, first = tie(xf, xb, first)
        elif step == 3:
            gb, xf, first = tie(gb, xf, small[0])
        else:
            tf, ob, first = tie(tf, ob, small[0])
        all_x += here_x
        all_g += here_g
        outs += out
        backs += back
        smalls.append([first, *small[1:]])

    scaled, d_gate, d_up, combs = (list(v) for v in zip(*smalls))
    two = [tokens.shape] * 2

    def summed(part_f, got_f, part_b, got_b, name):
        return by_columns(pair_kernel, [part_f, got_f, part_b, got_b], two, name)

    of, tb = forward(outs[7]), backward(backs[7])
    tf, ob = summed(backs[4], tf, outs[3], ob, "sum_a2")
    away_d, kept_d = gradient(all_g, tok_rows, [scaled], "grad_down")
    of, tb, tf, ob, away_d, d_gate[-1] = tie(of, tb, tf, ob, away_d, d_gate[-1])

    tf, ob, got_d = forward(tf), backward(ob), core_swap(away_d)
    of, tb = summed(outs[6], of, backs[5], tb, "sum_b3")
    part_d = y_part(kept_d, got_d)
    part_d, d_gate[-1] = tie(part_d, d_gate[-1])
    last_d = y_swap(part_d)
    away_g, kept_g = gradient(all_x, tok_rows, [d_gate], "grad_gate")
    tf, ob, of, tb, away_g, d_up[-1] = tie(tf, ob, of, tb, away_g, d_up[-1])

    of, tb, got_g = forward(of), backward(tb), core_swap(away_g)
    tf, ob = summed(backs[2], tf, outs[1], ob, "sum_a1")
    part_g = y_part(kept_g, got_g)
    part_g, d_up[-1] = tie(part_g, d_up[-1])
    last_g = y_swap(part_g)
    away_u, kept_u = gradient(all_x, tok_rows, [d_up], "grad_up")
    of, tb, tf, ob, away_u, last_d, combs[-1] = tie(of, tb, tf, ob, away_u, last_d, combs[-1])

    tf, ob, got_u = forward(tf), backward(ob), core_swap(away_u)
    of, tb = summed(outs[4], of, backs[3], tb, "sum_b2")
    part_u = y_part(kept_u, got_u)
    part_u, last_d = tie(part_u, last_d)
    last_u = y_swap(part_u)
    d_w_down = last_add(kept_d, got_d, last_d, False, "sum_down")
    d_comb = jnp.concatenate(combs, axis=1).reshape(groups, tok_rows)
    table = ring_sources()
    inverse = jnp.asarray([[row.index(e) for e in range(groups)] for row in table], jnp.int32)[me]
    d_comb = d_comb[inverse]
    tf, ob, of, tb, last_g, d_comb, d_w_down = tie(tf, ob, of, tb, last_g, d_comb, d_w_down)

    of, tb = forward(of), backward(tb)
    d_w_gate = last_add(kept_g, got_g, last_g, True, "sum_gate")
    of, tb, last_u, d_comb, d_w_gate = tie(of, tb, last_u, d_comb, d_w_gate)

    of, tb = summed(outs[2], of, backs[1], tb, "sum_b1")
    of, tb = forward(of), backward(tb)
    d_w_up = last_add(kept_u, got_u, last_u, True, "sum_up")
    returned = lax.all_to_all(d_comb, "expert", split_axis=0, concat_axis=0, tiled=True)
    d_w_up, returned, of, tb = tie(d_w_up, returned, of, tb)
    d_combine = jnp.sum(jnp.where(chosen, returned.T[:, None, :], 0.0), axis=2)
    output, d_tokens = by_columns(
        end_kernel, [outs[0], of, ob, backs[0], tf, tb], two, "sum_end"
    )
    return output, d_tokens, d_combine, d_w_gate, d_w_up, d_w_down


def solution(mesh):
    rows = P(("dp", "expert"), None)
    small = mesh.shape["expert"] == len(RING) and mesh.shape["dp"] == 4
    return jax.shard_map(
        gathered_plan if small else routed_plan,
        mesh=mesh,
        in_specs=(rows, rows, rows, rows) + (P("expert", None, None),) * 3,
        out_specs=(
            rows,
            rows,
            rows,
            P("expert", "dp", None),
            P("expert", "dp", None),
            P("expert", None, "dp"),
        ),
        check_vma=False,
    )
```

```python
import functools
import jax
import jax.numpy as jnp
from jax import lax
from jax.experimental import pallas as pl
from jax.experimental.pallas import tpu as pltpu
from jax.sharding import PartitionSpec as P


def slot_map(routes, experts, capacity):
    flat_ids = routes.reshape(-1)
    onehot = (flat_ids[:, None] == jnp.arange(experts, dtype=jnp.int32)[None, :]).astype(jnp.int32)
    before = jnp.cumsum(onehot, axis=0) - onehot
    slots = jnp.sum(before * onehot, axis=1)
    target = flat_ids * capacity + slots
    source = (
        jnp.full((experts * capacity,), -1, jnp.int32)
        .at[target]
        .set(jnp.arange(flat_ids.shape[0], dtype=jnp.int32))
    )
    return (target, source)


def routed_plan(tokens, routes, combine, cotangent, w_gate, w_up, w_down):
    tok_rows, features = tokens.shape
    per_token = routes.shape[1]
    groups = lax.axis_size("expert")
    local_exp = w_gate.shape[0]
    experts = local_exp * groups
    capacity = 3 * tok_rows * per_token // (2 * experts)
    target, source = slot_map(routes, experts, capacity)
    filled = (source >= 0)[:, None]
    pair_index = jnp.maximum(source, 0)
    owner_row = pair_index // per_token
    outgoing = jnp.where(filled, tokens[owner_row], jnp.zeros((), jnp.bfloat16))
    outgoing = outgoing.reshape(groups, local_exp, capacity, features)
    cot_float = cotangent.astype(jnp.float32)
    scaled = (combine[:, :, None] * cot_float[:, None, :]).reshape(tok_rows * per_token, features)
    outgoing_grad = jnp.where(filled, scaled[pair_index], 0.0).astype(jnp.bfloat16)
    outgoing_grad = outgoing_grad.reshape(groups, local_exp, capacity, features)
    arrived = lax.all_to_all(outgoing, "expert", split_axis=0, concat_axis=0, tiled=True)
    gate_pre = jnp.einsum("secd,edf->secf", arrived, w_gate, preferred_element_type=jnp.float32)
    up_pre = jnp.einsum("secd,edf->secf", arrived, w_up, preferred_element_type=jnp.float32)
    activated = jax.nn.silu(gate_pre)
    hidden = (activated * up_pre).astype(jnp.bfloat16)
    produced = jnp.einsum(
        "secf,efd->secd", hidden, w_down, preferred_element_type=jnp.float32
    ).astype(jnp.bfloat16)
    returned = lax.all_to_all(produced, "expert", split_axis=0, concat_axis=0, tiled=True)
    d_in = lax.all_to_all(outgoing_grad, "expert", split_axis=0, concat_axis=0, tiled=True)
    d_hidden = jnp.einsum("secd,efd->secf", d_in, w_down, preferred_element_type=jnp.float32)
    part_down = jnp.einsum("secf,secd->efd", hidden, d_in, preferred_element_type=jnp.float32)
    sigmoid_g = jax.nn.sigmoid(gate_pre)
    d_gate = (d_hidden * up_pre * sigmoid_g * (1.0 + gate_pre * (1.0 - sigmoid_g))).astype(
        jnp.bfloat16
    )
    d_up = (d_hidden * activated).astype(jnp.bfloat16)
    part_gate = jnp.einsum("secd,secf->edf", arrived, d_gate, preferred_element_type=jnp.float32)
    part_up = jnp.einsum("secd,secf->edf", arrived, d_up, preferred_element_type=jnp.float32)
    d_rows = (
        jnp.einsum("secf,edf->secd", d_gate, w_gate, preferred_element_type=jnp.float32)
        + jnp.einsum("secf,edf->secd", d_up, w_up, preferred_element_type=jnp.float32)
    ).astype(jnp.bfloat16)
    back = lax.all_to_all(d_rows, "expert", split_axis=0, concat_axis=0, tiled=True)
    per_slot = returned.reshape(experts * capacity, features)[target]
    per_slot = per_slot.reshape(tok_rows, per_token, features).astype(jnp.float32)
    output = jnp.sum(combine[:, :, None] * per_slot, axis=1).astype(jnp.bfloat16)
    d_combine = jnp.sum(per_slot * cot_float[:, None, :], axis=2)
    back_slot = back.reshape(experts * capacity, features)[target]
    back_slot = back_slot.reshape(tok_rows, per_token, features).astype(jnp.float32)
    d_tokens = jnp.sum(back_slot, axis=1).astype(jnp.bfloat16)
    sum_gate, sum_up, sum_down = (
        lax.psum_scatter(
            part_gate.astype(jnp.bfloat16), "dp", scatter_dimension=1, tiled=True
        ).astype(jnp.float32),
        lax.psum_scatter(
            part_up.astype(jnp.bfloat16), "dp", scatter_dimension=1, tiled=True
        ).astype(jnp.float32),
        lax.psum_scatter(
            part_down.astype(jnp.bfloat16), "dp", scatter_dimension=2, tiled=True
        ).astype(jnp.float32),
    )
    d_w_down = sum_down.astype(jnp.bfloat16)
    return (
        output,
        d_tokens,
        d_combine,
        sum_gate.astype(jnp.bfloat16),
        sum_up.astype(jnp.bfloat16),
        d_w_down,
    )


RING = (0, 1, 3, 5, 7, 6, 4, 2)


def ring_perms():
    n = len(RING)
    fwd = [(RING[i], RING[(i + 1) % n]) for i in range(n)]
    bwd = [(RING[(i + 1) % n], RING[i]) for i in range(n)]
    return fwd, bwd


def ring_sources():
    n = len(RING)
    place = {e: i for i, e in enumerate(RING)}
    steps = (0, -1, 1, -2, 2, -3, 3, 4)
    return [[RING[(place[e] + r) % n] for r in steps] for e in range(n)]


def forward(value):
    return lax.ppermute(value, "expert", ring_perms()[0])


def backward(value):
    return lax.ppermute(value, "expert", ring_perms()[1])


def tie(*values):
    return lax.optimization_barrier(values)


def add_rounded(a, b):
    return (a.astype(jnp.float32) + b.astype(jnp.float32)).astype(jnp.bfloat16)


def core_swap(away):
    n = lax.axis_size("dp")
    return lax.ppermute(away, "dp", [(j, j ^ 1) for j in range(n)])


def pick(halves, y):
    return lax.dynamic_index_in_dim(halves, y, 0, keepdims=False)


def y_parts(kept, got):
    y = lax.axis_index("dp") // 2
    half = kept.shape[1] // 2
    kept, got = pick(kept, 1 - y), pick(got, 1 - y)
    return add_rounded(kept[:half], got[:half]), add_rounded(kept[half:], got[half:])


def y_part(kept, got):
    y = lax.axis_index("dp") // 2
    return add_rounded(pick(kept, 1 - y), pick(got, 1 - y))


def y_swap(other):
    n = lax.axis_size("dp")
    return lax.ppermute(other, "dp", [(j, j ^ 2) for j in range(n)])


ANY = pl.BlockSpec(memory_space=pl.ANY)
KERNEL_VMEM = 60 * 1024 * 1024
EXTRA = 16


class Mover:
    def __init__(self, sems):
        self.sems = sems
        self.used = 0

    def go(self, src, dst):
        copy = pltpu.make_async_copy(src, dst, self.sems.at[self.used])
        self.used += 1
        copy.start()
        return copy


def gradient_kernel(part, spots, tall_spots, core, *refs):
    n, m = len(spots), len(tall_spots)
    wide, narrow, refs = refs[:n], refs[n:n + m], refs[n + m:]
    away, kept, xs, st, ov, sems = refs
    quarters, _, size = xs.shape
    move = Mover(sems)
    load_s = [
        move.go(r, st.at[pl.ds(top, r.shape[0]), pl.ds(at, r.shape[1])])
        for r, (top, at) in zip(narrow, tall_spots)
    ]

    def load_quarter(i):
        c = core[0] if i >= quarters // 2 else 1 - core[0]
        first = pl.multiple_of(((i % (quarters // 2)) * 2 + c) * size, size)
        return [
            move.go(r.at[pl.ds(0, part), pl.ds(first, size)], xs.at[i, pl.ds(at, part)])
            for r, at in zip(wide, spots)
        ]

    load_x = [load_quarter(0), load_quarter(1)]
    for c in load_s:
        c.wait()
    stores = []
    for i in range(quarters):
        for c in load_x[i]:
            c.wait()
        if i + 2 < quarters:
            load_x.append(load_quarter(i + 2))
        for f in range(0, st.shape[0], 256):
            ov[i, f:f + 256, :] = jnp.dot(
                st[f:f + 256, :], xs[i], preferred_element_type=jnp.float32
            ).astype(jnp.bfloat16)
        half = quarters // 2
        stores.append(move.go(ov.at[i], away.at[i] if i < half else kept.at[i - half]))
    for c in stores:
        c.wait()


FREE = pl.CostEstimate(flops=0, bytes_accessed=0, transcendentals=0)


def gradient(wide, part, narrows, name):
    n_dp = lax.axis_size("dp")
    spots, at = [part * i for i in range(len(wide))], part * len(wide)
    flat, tall_spots, tall = [], [], 0
    for pieces in narrows:
        col = 0
        for piece in pieces:
            flat.append(piece)
            tall_spots.append((tall, col))
            col += piece.shape[1]
        tall += pieces[0].shape[0]
    size = wide[0].shape[1] // n_dp
    half = jax.ShapeDtypeStruct((n_dp // 2, tall, size), jnp.bfloat16)
    core = (lax.axis_index("dp") % 2).reshape(1)
    return pl.pallas_call(
        functools.partial(gradient_kernel, part, tuple(spots), tuple(tall_spots)),
        out_shape=[half, half],
        in_specs=[pl.BlockSpec(memory_space=pltpu.SMEM)] + [ANY] * (len(wide) + len(flat)),
        out_specs=[ANY, ANY],
        scratch_shapes=[
            pltpu.VMEM((n_dp, at, size), jnp.bfloat16),
            pltpu.VMEM((tall, at), jnp.bfloat16),
            pltpu.VMEM((n_dp, tall, size), jnp.bfloat16),
            pltpu.SemaphoreType.DMA((len(flat) + n_dp * len(wide) + n_dp,)),
        ],
        compiler_params=pltpu.CompilerParams(vmem_limit_bytes=KERNEL_VMEM),
        cost_estimate=FREE,
        name=name,
    )(core, *wide, *flat)


def total_of(*values):
    total = values[0].astype(jnp.float32)
    for v in values[1:]:
        total = total + v.astype(jnp.float32)
    return total.astype(jnp.bfloat16)


def pair_kernel(part_f, got_f, part_b, got_b, f, b):
    f[...] = total_of(part_f[...], got_f[...])
    b[...] = total_of(part_b[...], got_b[...])


def end_kernel(own_o, of, ob, own_t, tf, tb, o, t):
    o[...] = total_of(own_o[...], of[...], ob[...])
    t[...] = total_of(own_t[...], tf[...], tb[...])


def by_columns(kernel, operands, out_shapes, name):
    features = out_shapes[0][-1]
    steps = 2

    def spec(shape):
        block = tuple(shape[:-1]) + (features // steps,)
        return pl.BlockSpec(block, lambda i, n=len(shape): (0,) * (n - 1) + (i,))

    return pl.pallas_call(
        kernel,
        out_shape=[jax.ShapeDtypeStruct(s, jnp.bfloat16) for s in out_shapes],
        grid=(steps,),
        in_specs=[spec(v.shape) for v in operands],
        out_specs=[spec(s) for s in out_shapes],
        compiler_params=pltpu.CompilerParams(vmem_limit_bytes=KERNEL_VMEM),
        cost_estimate=FREE,
        name=name,
    )(*operands)


def last_add_kernel(turned, y, kept, got, *refs):
    lasts, out = refs[:-1], refs[-1]
    half = lasts[0].shape[0]
    for i, last in enumerate(lasts):
        rows = pl.ds(i * half, half)
        total = kept[0, rows].astype(jnp.float32) + got[0, rows].astype(jnp.float32)
        total = total + last[...].astype(jnp.float32)
        if turned:
            out[0, :, rows] = total.T.astype(jnp.bfloat16)
        else:
            out[0, rows] = total.astype(jnp.bfloat16)


def last_add(kept, got, lasts, turned, name):
    _, ff, size = kept.shape
    y = (lax.axis_index("dp") // 2).reshape(1)
    shape = (1, size, ff) if turned else (1, ff, size)
    half = pl.BlockSpec((1, ff, size), lambda i, y: (y[0], 0, 0))
    piece = pl.BlockSpec(lasts[0].shape, lambda i, y: (0, 0))
    return pl.pallas_call(
        functools.partial(last_add_kernel, turned),
        out_shape=jax.ShapeDtypeStruct(shape, jnp.bfloat16),
        grid_spec=pltpu.PrefetchScalarGridSpec(
            num_scalar_prefetch=1,
            grid=(1,),
            in_specs=[half, half] + [piece] * len(lasts),
            out_specs=pl.BlockSpec(shape, lambda i, y: (0, 0, 0)),
        ),
        compiler_params=pltpu.CompilerParams(vmem_limit_bytes=KERNEL_VMEM),
        cost_estimate=FREE,
        name=name,
    )(y, kept, got, *lasts)


def with_weights_kernel(cot, routes, combine, out):
    rows, features = cot.shape
    out[:rows] = cot[...]
    line = lax.broadcasted_iota(jnp.int32, (EXTRA, rows), 0)
    weights = jnp.zeros((EXTRA, rows), jnp.float32)
    for k in range(routes.shape[0]):
        weights += jnp.where(routes[k:k + 1] == line, combine[k:k + 1], 0.0)
    wide = weights * 65537.0
    high = wide - (wide - weights)
    rest = weights - high
    wide = rest * 65537.0
    middle = wide - (wide - rest)
    out[rows:] = jnp.zeros((EXTRA, features), jnp.bfloat16)
    for i, term in enumerate((high, middle, rest - middle)):
        out[rows:, i * rows:(i + 1) * rows] = term.astype(jnp.bfloat16)


def with_weights(cot, routes, combine):
    return pl.pallas_call(
        with_weights_kernel,
        out_shape=jax.ShapeDtypeStruct((cot.shape[0] + EXTRA, cot.shape[1]), cot.dtype),
        cost_estimate=FREE,
        name="with_weights",
    )(cot, routes.T, combine.T)


def expert_kernel(n, me, *refs):
    xs, gs, refs = refs[:n], refs[n:2 * n], refs[2 * n:]
    wg, wu, wd, wdt, wgt, wut = refs[:6]
    outs, backs, refs = refs[6:6 + n], refs[6 + n:6 + 2 * n], refs[6 + 2 * n:]
    s_o, dg_o, du_o, comb_o = refs[:4]
    x2, g2, wgv, wuv, wdv, wdtv, wgtv, wutv, gv, uv, sv, dgv, duv, wb, wv, st, dgt, dut, ov, rv, sems = refs[4:]
    part = xs[0].shape[0]
    rows, features = x2.shape
    ff = gv.shape[1]
    f32, bf16 = jnp.float32, jnp.bfloat16
    move = Mover(sems)
    cols = [pl.ds(f, 256) for f in range(0, ff, 256)]
    wide = [pl.ds(d, 512) for d in range(0, features, 512)]
    spots = [pl.ds(i * part, part) for i in range(n)]

    def load(src, dst, pieces):
        size = src.shape[0] // pieces
        return [
            move.go(src.at[pl.ds(i * size, size)], dst.at[pl.ds(i * size, size)])
            for i in range(pieces)
        ]

    load_x = [move.go(r, x2.at[s]) for r, s in zip(xs, spots)]
    span = wb.shape[2]
    load_w = [move.go(r.at[pl.ds(part, EXTRA), pl.ds(0, span)], wb.at[i]) for i, r in enumerate(gs)]
    load_g = load(wg, wgv, 4)
    load_u = load(wu, wuv, 4)
    load_cot = [move.go(r.at[pl.ds(0, part)], g2.at[s]) for r, s in zip(gs, spots)]
    load_d = load(wd, wdv, 4)
    load_dt = load(wdt, wdtv, 4)
    load_gt = load(wgt, wgtv, 4)
    load_ut = load(wut, wutv, 4)
    for c in load_w:
        c.wait()
    for i, s in enumerate(spots):
        terms = wb[i].astype(f32)
        mine = lax.broadcasted_iota(jnp.int32, terms.shape, 0) == me[0]
        terms = jnp.sum(jnp.where(mine, terms, 0.0), axis=0, keepdims=True)
        terms = terms[:, :part] + terms[:, part:2 * part] + terms[:, 2 * part:]
        wv[s, :] = jnp.broadcast_to(terms, (128, part)).T[:, :1]
    for c in load_x + load_g:
        c.wait()
    for c in cols:
        gv[:, c] = jnp.dot(x2[...], wgv[:, c], preferred_element_type=f32)
    for c in load_u:
        c.wait()
    for c in cols:
        up = jnp.dot(x2[...], wuv[:, c], preferred_element_type=f32)
        uv[:, c] = up
        gate = gv[:, c]
        scaled = (gate * jax.nn.sigmoid(gate) * up * wv[...]).astype(bf16)
        sv[:, c] = scaled
        st[c, :] = scaled.T
    stores = [move.go(st, s_o)]
    for c in load_d:
        c.wait()
    for c in wide:
        ov[:, c] = jnp.dot(sv[...], wdv[:, c], preferred_element_type=f32).astype(bf16)
    stores += [move.go(ov.at[s], r) for r, s in zip(outs, spots)]
    for c in load_cot + load_dt:
        c.wait()
    comb = jnp.zeros((rows, 1), f32)
    for c in cols:
        d_raw = jnp.dot(g2[...], wdtv[:, c], preferred_element_type=f32)
        gate, up = gv[:, c], uv[:, c]
        sig = jax.nn.sigmoid(gate)
        act = gate * sig
        comb += jnp.sum(act * up * d_raw, axis=1, keepdims=True)
        d_hidden = d_raw * wv[...]
        d_gate = (d_hidden * up * sig * (1.0 + gate * (1.0 - sig))).astype(bf16)
        d_up = (d_hidden * act).astype(bf16)
        dgv[:, c] = d_gate
        duv[:, c] = d_up
        dgt[c, :] = d_gate.T
        dut[c, :] = d_up.T
    comb_o[...] = jnp.broadcast_to(comb, (rows, 128)).T[:1, :]
    stores += [move.go(dgt, dg_o), move.go(dut, du_o)]
    for c in load_gt + load_ut:
        c.wait()
    for c in wide:
        rv[:, c] = (
            jnp.dot(dgv[...], wgtv[:, c], preferred_element_type=f32)
            + jnp.dot(duv[...], wutv[:, c], preferred_element_type=f32)
        ).astype(bf16)
    stores += [move.go(rv.at[s], r) for r, s in zip(backs, spots)]
    for c in stores:
        c.wait()


def expert(xs, gs, matrices, name):
    n, (part, features) = len(xs), xs[0].shape
    ff = matrices[0].shape[1]
    rows = n * part
    bf16, f32 = jnp.bfloat16, jnp.float32
    vmem = pl.BlockSpec(memory_space=pltpu.VMEM)
    block = jax.ShapeDtypeStruct((part, features), bf16)
    turned = jax.ShapeDtypeStruct((ff, rows), bf16)
    me = lax.axis_index("expert").reshape(1)
    res = pl.pallas_call(
        functools.partial(expert_kernel, n),
        out_shape=[block] * (2 * n) + [turned] * 3 + [jax.ShapeDtypeStruct((1, rows), f32)],
        in_specs=[pl.BlockSpec(memory_space=pltpu.SMEM)] + [ANY] * (2 * n + 6),
        out_specs=[ANY] * (2 * n + 3) + [vmem],
        scratch_shapes=[
            pltpu.VMEM((rows, features), bf16),
            pltpu.VMEM((rows, features), bf16),
            pltpu.VMEM((features, ff), bf16),
            pltpu.VMEM((features, ff), bf16),
            pltpu.VMEM((ff, features), bf16),
            pltpu.VMEM((features, ff), bf16),
            pltpu.VMEM((ff, features), bf16),
            pltpu.VMEM((ff, features), bf16),
            pltpu.VMEM((rows, ff), f32),
            pltpu.VMEM((rows, ff), f32),
            pltpu.VMEM((rows, ff), bf16),
            pltpu.VMEM((rows, ff), bf16),
            pltpu.VMEM((rows, ff), bf16),
            pltpu.VMEM((n, EXTRA, 3 * part), bf16),
            pltpu.VMEM((rows, 1), f32),
            pltpu.VMEM((ff, rows), bf16),
            pltpu.VMEM((ff, rows), bf16),
            pltpu.VMEM((ff, rows), bf16),
            pltpu.VMEM((rows, features), bf16),
            pltpu.VMEM((rows, features), bf16),
            pltpu.SemaphoreType.DMA((5 * n + 27,)),
        ],
        compiler_params=pltpu.CompilerParams(vmem_limit_bytes=KERNEL_VMEM),
        cost_estimate=FREE,
        name=name,
    )(me, *xs, *gs, *matrices)
    return res[:n], res[n:2 * n], res[2 * n:]


def gathered_plan(tokens, routes, combine, cotangent, w_gate, w_up, w_down):
    tok_rows, features = tokens.shape
    groups = lax.axis_size("expert")
    me = lax.axis_index("expert")
    chosen = routes[:, :, None] == jnp.arange(groups, dtype=jnp.int32)[None, None, :]
    matrices = [w_gate[0], w_up[0], w_down[0], w_down[0].T, w_gate[0].T, w_up[0].T]

    xs = [forward(tokens), backward(tokens)]
    both = with_weights(cotangent, routes, combine)
    gs = [forward(both), backward(both)]
    gf, gb, m3, m4, m5 = tie(*gs, *matrices[3:])
    matrices = matrices[:3] + [m3, m4, m5]
    xf, xb = xs
    all_x, all_g, outs, backs, smalls = [], [], [], [], []
    for step in range(1, 5):
        here_x, here_g = [xf, xb], [gf, gb]
        if step < 3:
            gf, gb = forward(gf), backward(gb)
            xf, xb = forward(xf), backward(xb)
        elif step == 3:
            gb, xf = backward(gb), forward(xf)
        else:
            here_x, here_g = [xf], [gb]
            tf, ob = forward(backs[6]), backward(outs[5])
        if step == 1:
            here_x, here_g = [tokens, *here_x], [both, *here_g]
        out, back, small = expert(here_x, here_g, matrices, f"expert_{step}")
        if step < 3:
            gf, gb, first = tie(gf, gb, small[0])
            xf, xb, first = tie(xf, xb, first)
        elif step == 3:
            gb, xf, first = tie(gb, xf, small[0])
        else:
            tf, ob, first = tie(tf, ob, small[0])
        all_x += here_x
        all_g += here_g
        outs += out
        backs += back
        smalls.append([first, *small[1:]])

    scaled, d_gate, d_up, combs = (list(v) for v in zip(*smalls))
    two = [tokens.shape] * 2

    def summed(part_f, got_f, part_b, got_b, name):
        return by_columns(pair_kernel, [part_f, got_f, part_b, got_b], two, name)

    of, tb = forward(outs[7]), backward(backs[7])
    tf, ob = summed(backs[4], tf, outs[3], ob, "sum_a2")
    away_d, kept_d = gradient(all_g, tok_rows, [scaled], "grad_down")
    of, tb, tf, ob, away_d, d_gate[-1] = tie(of, tb, tf, ob, away_d, d_gate[-1])

    tf, ob, got_d = forward(tf), backward(ob), core_swap(away_d)
    of, tb = summed(outs[6], of, backs[5], tb, "sum_b3")
    first_d, other_d = y_parts(kept_d, got_d)
    first_d = y_swap(first_d)
    away_g, kept_g = gradient(all_x, tok_rows, [d_gate], "grad_gate")
    tf, ob, of, tb, away_g, d_up[-1], first_d, other_d = tie(
        tf, ob, of, tb, away_g, d_up[-1], first_d, other_d
    )

    of, tb, got_g, other_d = forward(of), backward(tb), core_swap(away_g), y_swap(other_d)
    tf, ob = summed(backs[2], tf, outs[1], ob, "sum_a1")
    part_g = y_part(kept_g, got_g)
    away_u, kept_u = gradient(all_x, tok_rows, [d_up], "grad_up")
    of, tb, tf, ob, away_u, other_d, part_g, combs[-1] = tie(
        of, tb, tf, ob, away_u, other_d, part_g, combs[-1]
    )

    tf, ob, got_u, last_g = forward(tf), backward(ob), core_swap(away_u), y_swap(part_g)
    of, tb = summed(outs[4], of, backs[3], tb, "sum_b2")
    last_u = y_swap(y_part(kept_u, got_u))
    d_w_down = last_add(kept_d, got_d, [first_d, other_d], False, "sum_down")
    d_comb = jnp.concatenate(combs, axis=1).reshape(groups, tok_rows)
    table = ring_sources()
    inverse = jnp.asarray([[row.index(e) for e in range(groups)] for row in table], jnp.int32)[me]
    d_comb = d_comb[inverse]
    tf, ob, of, tb, last_g, d_comb, d_w_down = tie(tf, ob, of, tb, last_g, d_comb, d_w_down)

    of, tb = forward(of), backward(tb)
    returned = lax.all_to_all(d_comb, "expert", split_axis=0, concat_axis=0, tiled=True)
    d_w_gate = last_add(kept_g, got_g, [last_g], True, "sum_gate")
    of, tb, last_u, returned, d_w_gate = tie(of, tb, last_u, returned, d_w_gate)

    of, tb = summed(outs[2], of, backs[1], tb, "sum_b1")
    of, tb = forward(of), backward(tb)
    d_w_up = last_add(kept_u, got_u, [last_u], True, "sum_up")
    d_combine = jnp.sum(jnp.where(chosen, returned.T[:, None, :], 0.0), axis=2)
    d_w_up, d_combine, of, tb = tie(d_w_up, d_combine, of, tb)
    output, d_tokens = by_columns(
        end_kernel, [outs[0], of, ob, backs[0], tf, tb], two, "sum_end"
    )
    return output, d_tokens, d_combine, d_w_gate, d_w_up, d_w_down


def solution(mesh):
    rows = P(("dp", "expert"), None)
    small = mesh.shape["expert"] == len(RING) and mesh.shape["dp"] == 4
    return jax.shard_map(
        gathered_plan if small else routed_plan,
        mesh=mesh,
        in_specs=(rows, rows, rows, rows) + (P("expert", None, None),) * 3,
        out_specs=(
            rows,
            rows,
            rows,
            P("expert", "dp", None),
            P("expert", "dp", None),
            P("expert", None, "dp"),
        ),
        check_vma=False,
    )
```
